32 devices in a mesh: dp: 8 (over y, x, core), seq: 4 (over z).
Axes of the slice: x: 2, y: 2, z: 4, core: 2. Of those that a mesh axis runs over, the one named last changes fastest.
Arguments:
- hidden_in: bfloat16 [8192, 1024], P(('dp', 'seq')), may hold values from -6 to 6
- doc_lengths: int32 [9], replicated, may hold values from 128 to 1792, as said below
- pad_lengths: int32 [9], replicated, may hold values from 0 to 64
- w_query: float32 [1024, 2048], P('dp'), may hold values from -0.1875 to 0.1875
- key_matrix: float32 [1024, 1024], P('dp'), may hold values from -0.1875 to 0.1875
- value_matrix: float32 [1024, 1024], P('dp'), may hold values from -0.1875 to 0.1875
- w_output: float32 [2048, 1024], P(None, 'dp'), may hold values from -1 to 1
- w_gate: float32 [1024, 3072], P('dp'), may hold values from -0.1875 to 0.1875
- w_up: float32 [1024, 3072], P('dp'), may hold values from -0.1875 to 0.1875
- w_down: float32 [3072, 1024], P(None, 'dp'), may hold values from -0.109375 to 0.109375
- attn_gain: float32 [1024], P('dp'), may hold values from 0.1 to 1.9
- mlp_gain: float32 [1024], P('dp'), may hold values from 0.1 to 1.9
- query_gain: float32 [128], P('dp'), may hold values from 0.1 to 1.9
- key_gain: float32 [128], P('dp'), may hold values from 0.1 to 1.9
- out_grad: bfloat16 [8192, 1024], P(('dp', 'seq')), may hold values from -6 to 6
Outputs:
- output_act: bfloat16 [8192, 1024], P(('dp', 'seq'))
- in_grad: bfloat16 [8192, 1024], P(('dp', 'seq'))
- grad_query: float32 [1024, 2048], P('dp')
- grad_key: float32 [1024, 1024], P('dp')
- grad_value: float32 [1024, 1024], P('dp')
- grad_output: float32 [2048, 1024], P(None, 'dp')
- grad_gate: float32 [1024, 3072], P('dp')
- grad_up: float32 [1024, 3072], P('dp')
- grad_down: float32 [3072, 1024], P(None, 'dp')
- grad_attn_gain: float32 [1024], P('dp')
- grad_mlp_gain: float32 [1024], P('dp')
- grad_query_gain: float32 [128], P('dp')
- grad_key_gain: float32 [128], P('dp')
The draws below stay inside these ranges and needn't reach their ends.
Inputs may be any that keep to these rules, and one draw needn't show every extreme that they name: `doc_lengths`: the lengths of the documents packed in order into the stream; they sum to 8192; the shortest and the longest bound are reached in every draw.
All inputs are finite; a program needn't handle non-finite values.
Results may differ from the reference program's by a relative error of at most 0.02.
Values may be sent and summed in bfloat16 or wider, within the bound.
No kernel may reach another device: no remote copies, remote signals or barrier semaphores. Data moves between devices by JAX's collectives and lax.ppermute only.
A program may use at most 256 MiB of HBM per device.

```python
import jax
import jax.numpy as jnp
from jax import lax

MODEL_WIDTH = 1024
QUERY_HEADS = 16
KEY_VALUE_HEADS = 8
HEAD_WIDTH = 128
FEEDFWD_UNITS = 3072
WINDOW_TOKENS = 1024
QBLOCK = 512
PAD_MOST = 64
STRETCH = 1024
TOKEN_TOTAL = 8192
DOCS = 9
N_DP = 8


def draw_doc_lengths(key, part):
    key = jax.random.fold_in(key, 11)
    offset_key, pick_key = jax.random.split(key)
    low_cut = STRETCH // 8
    high_cut = 7 * STRETCH // 8
    offsets = jax.random.randint(offset_key, (N_DP,), low_cut, high_cut + 1).astype(jnp.int32)
    longest = jax.random.randint(pick_key, (), 1, N_DP).astype(jnp.int32)
    slots = jnp.arange(N_DP, dtype=jnp.int32)
    offsets = jnp.where(slots == 0, low_cut, offsets)
    offsets = jnp.where(slots == longest - 1, low_cut, offsets)
    offsets = jnp.where(slots == longest, high_cut, offsets).astype(jnp.int32)
    cuts = slots * STRETCH + offsets
    bounds = jnp.concatenate([jnp.zeros((1,), jnp.int32), cuts, jnp.full((1,), TOKEN_TOTAL, jnp.int32)])
    return (bounds[1:] - bounds[:-1]).astype(jnp.int32)


def with_ends(array, rng, least, top_value):
    shape = array.shape
    spot = [jax.random.randint(jax.random.fold_in(rng, axis), (), 0, shape[axis]) for axis in range(len(shape))]
    array = array.at[tuple(spot)].set(least)
    longest = shape.index(max(shape))
    spot[longest] = (spot[longest] + 1) % shape[longest]
    return array.at[tuple(spot)].set(top_value)


def block_scale(rng, dims, pieces, least, largest):
    def one(dim, blocks):
        draws = jax.random.uniform(jax.random.fold_in(jax.random.fold_in(rng, 6), dim), (blocks,), jnp.float32, least / len(pieces), largest / len(pieces))
        return jnp.repeat(jnp.exp(draws), dims[dim] // blocks).reshape((-1,) + (1,) * (len(dims) - dim - 1))

    loudness = one(*pieces[0])
    for cut in pieces[1:]:
        loudness = loudness * one(*cut)
    return loudness


def normal_values(rng, shape, scale, limit, cuts=(), kind=jnp.bfloat16):
    drawn = scale * jax.random.normal(rng, shape, jnp.float32)
    if cuts:
        drawn = drawn * block_scale(rng, shape, cuts, -0.22, 0.18)
    return jnp.clip(drawn, -limit, limit).astype(kind)


def setup_inputs(seed: int = 0) -> dict:
    splits = jax.random.split(jax.random.key(seed), 16)
    hidden_in = normal_values(splits[0], (TOKEN_TOTAL, MODEL_WIDTH), 1.0, 6.0, ((0, 32),))
    doc_lengths = draw_doc_lengths(jax.random.fold_in(splits[15], 71), 0)
    pad_lengths = with_ends(jax.random.randint(splits[2], (DOCS,), 0, PAD_MOST + 1), jax.random.fold_in(splits[2], 1), 0, PAD_MOST).astype(jnp.int32)
    w_query = normal_values(splits[3], (MODEL_WIDTH, QUERY_HEADS * HEAD_WIDTH), MODEL_WIDTH ** -0.5, 0.1875, ((0, 8),), jnp.float32)
    key_matrix = normal_values(splits[4], (MODEL_WIDTH, KEY_VALUE_HEADS * HEAD_WIDTH), MODEL_WIDTH ** -0.5, 0.1875, ((0, 8),), jnp.float32)
    value_matrix = normal_values(splits[5], (MODEL_WIDTH, KEY_VALUE_HEADS * HEAD_WIDTH), MODEL_WIDTH ** -0.5, 0.1875, ((0, 8),), jnp.float32)
    w_output = normal_values(splits[6], (QUERY_HEADS * HEAD_WIDTH, MODEL_WIDTH), 32 ** -0.5, 1.0, ((1, 8),), jnp.float32)
    w_gate = normal_values(splits[7], (MODEL_WIDTH, FEEDFWD_UNITS), MODEL_WIDTH ** -0.5, 0.1875, ((0, 8),), jnp.float32)
    w_up = normal_values(splits[8], (MODEL_WIDTH, FEEDFWD_UNITS), MODEL_WIDTH ** -0.5, 0.1875, ((0, 8),), jnp.float32)
    w_down = normal_values(splits[9], (FEEDFWD_UNITS, MODEL_WIDTH), FEEDFWD_UNITS ** -0.5, 0.109375, ((1, 8),), jnp.float32)
    attn_gain = jnp.clip(1.0 + 0.18 * jax.random.normal(splits[10], (MODEL_WIDTH,), jnp.float32), 0.1, 1.9)
    mlp_gain = jnp.clip(1.0 + 0.18 * jax.random.normal(splits[11], (MODEL_WIDTH,), jnp.float32), 0.1, 1.9)
    query_gain = jnp.clip(1.0 + 0.18 * jax.random.normal(splits[12], (HEAD_WIDTH,), jnp.float32), 0.1, 1.9)
    key_gain = jnp.clip(1.0 + 0.18 * jax.random.normal(splits[13], (HEAD_WIDTH,), jnp.float32), 0.1, 1.9)
    out_grad = normal_values(splits[14], (TOKEN_TOTAL, MODEL_WIDTH), 1.0, 6.0, ((0, 32),))
    return {"hidden_in": hidden_in, "doc_lengths": doc_lengths, "pad_lengths": pad_lengths, "w_query": w_query, "key_matrix": key_matrix, "value_matrix": value_matrix, "w_output": w_output, "w_gate": w_gate, "w_up": w_up, "w_down": w_down, "attn_gain": attn_gain, "mlp_gain": mlp_gain, "query_gain": query_gain, "key_gain": key_gain, "out_grad": out_grad}


norm_eps = 1e-06
rope_base = 1000000.0
masked_score = -1e+30

@jax.custom_vjp
def reduced_precision(v):
    return lax.optimization_barrier(v.astype(jnp.bfloat16)).astype(jnp.float32)

@jax.custom_vjp
def reduced_backward(v):
    return v

def low_keep(v):
    return (reduced_precision(v), None)

def low_pass(kept, grad):
    return (grad,)

def back_keep(v):
    return (v, None)

def back_low(kept, grad):
    return (reduced_precision(grad),)
reduced_precision.defvjp(low_keep, low_pass)
reduced_backward.defvjp(back_keep, back_low)

def norm_rows(value_rows, scales):
    return value_rows * lax.rsqrt(lax.optimization_barrier(jnp.mean(value_rows * value_rows, axis=-1, keepdims=True)) + norm_eps) * scales

def rotate(value_rows, cosine, sine_table):
    half_width = value_rows.shape[-1] // 2
    turned = jnp.concatenate([-value_rows[..., half_width:], value_rows[..., :half_width]], axis=-1)
    return value_rows * cosine + turned * sine_table

def doc_tables(doc_lengths, pad_lengths):
    doc_ends = jnp.cumsum(doc_lengths).astype(jnp.int32)
    starts = (doc_ends - doc_lengths).astype(jnp.int32)
    return (starts, doc_ends, (doc_ends - pad_lengths).astype(jnp.int32))

def token_info(token_index, tables):
    starts, doc_ends, pad_start = tables
    inside = (token_index[:, None] >= starts[None, :]) & (token_index[:, None] < doc_ends[None, :])
    numbers = jnp.arange(1, starts.shape[0] + 1, dtype=jnp.int32)
    doc_ids = lax.optimization_barrier(jnp.sum(jnp.where(inside, numbers[None, :], 0), axis=1)).astype(jnp.int32) - 1
    offset = lax.optimization_barrier(jnp.sum(jnp.where(inside, starts[None, :], 0), axis=1)).astype(jnp.int32)
    padded = lax.optimization_barrier(jnp.sum(jnp.where(inside & (token_index[:, None] >= pad_start[None, :]), 1, 0), axis=1)) > 0
    return (doc_ids, (token_index - offset).astype(jnp.int32), padded)

def rope_tables(positions):
    inv_freq = rope_base ** (-jnp.arange(HEAD_WIDTH // 2, dtype=jnp.float32) * 2.0 / HEAD_WIDTH)
    angles = positions.astype(jnp.float32)[:, None] * inv_freq[None, :]
    cosine = jnp.concatenate([jnp.cos(angles), jnp.cos(angles)], axis=-1)[:, None, :]
    sine_table = jnp.concatenate([jnp.sin(angles), jnp.sin(angles)], axis=-1)[:, None, :]
    return (cosine, sine_table)

def allowed(q_index, k_index, q_doc, k_doc, k_pad):
    return (q_doc[:, None] == k_doc[None, :]) & (k_doc[None, :] >= 0) & (k_index[None, :] <= q_index[:, None]) & (q_index[:, None] - k_index[None, :] < WINDOW_TOKENS) & (jnp.logical_not(k_pad)[None, :] | (k_index[None, :] == q_index[:, None]))

def attention(query_rows, keys, value_rows, doc_ids, padded):
    group_count = QUERY_HEADS // KEY_VALUE_HEADS
    scaling = HEAD_WIDTH ** (-0.5)
    grouped_heads = query_rows.reshape(TOKEN_TOTAL, KEY_VALUE_HEADS, group_count, HEAD_WIDTH)
    empty_rows = jnp.zeros((WINDOW_TOKENS, KEY_VALUE_HEADS, HEAD_WIDTH), jnp.float32)
    keys_ext = jnp.concatenate([empty_rows, keys], axis=0)
    values_ext = jnp.concatenate([empty_rows, value_rows], axis=0)
    docs_ext = jnp.concatenate([jnp.full((WINDOW_TOKENS,), -1, jnp.int32), doc_ids])
    pads_ext = jnp.concatenate([jnp.zeros((WINDOW_TOKENS,), bool), padded])

    def one_block(number):
        first_row = number * QBLOCK
        q_blk = lax.dynamic_slice_in_dim(grouped_heads, first_row, QBLOCK, 0)
        k_blk = lax.dynamic_slice_in_dim(keys_ext, first_row, QBLOCK + WINDOW_TOKENS, 0)
        v_blk = lax.dynamic_slice_in_dim(values_ext, first_row, QBLOCK + WINDOW_TOKENS, 0)
        q_doc = lax.dynamic_slice_in_dim(doc_ids, first_row, QBLOCK, 0)
        k_doc = lax.dynamic_slice_in_dim(docs_ext, first_row, QBLOCK + WINDOW_TOKENS, 0)
        k_pad = lax.dynamic_slice_in_dim(pads_ext, first_row, QBLOCK + WINDOW_TOKENS, 0)
        q_index = first_row + jnp.arange(QBLOCK, dtype=jnp.int32)
        k_index = first_row - WINDOW_TOKENS + jnp.arange(QBLOCK + WINDOW_TOKENS, dtype=jnp.int32)
        pairs = allowed(q_index, k_index, q_doc, k_doc, k_pad)
        raw_scores = reduced_backward(jnp.einsum('qhgd,khd->hgqk', q_blk, k_blk, precision=lax.Precision.HIGHEST))
        logits = jnp.where(pairs[None, None], raw_scores * scaling, masked_score)
        row_max = lax.optimization_barrier(jnp.max(logits, axis=-1, keepdims=True))
        weights_exp = jnp.where(pairs[None, None], jnp.exp(logits - row_max), 0.0)
        probs = reduced_precision(weights_exp / lax.optimization_barrier(jnp.sum(weights_exp, axis=-1, keepdims=True)))
        return jnp.einsum('hgqk,khd->qhgd', probs, v_blk, precision=lax.Precision.HIGHEST)
    blocks = lax.map(jax.checkpoint(one_block), jnp.arange(TOKEN_TOTAL // QBLOCK, dtype=jnp.int32))
    return blocks.reshape(TOKEN_TOTAL, QUERY_HEADS, HEAD_WIDTH)

def reference(hidden_in, doc_lengths, pad_lengths, w_query, key_matrix, value_matrix, w_output, w_gate, w_up, w_down, attn_gain, mlp_gain, query_gain, key_gain, out_grad):
    tables = doc_tables(doc_lengths, pad_lengths)
    doc_ids, positions, padded = token_info(jnp.arange(TOKEN_TOTAL, dtype=jnp.int32), tables)
    cosine, sine_table = rope_tables(positions)
    highest_precision = lax.Precision.HIGHEST

    def forward(inputs, wq_master, key_weight_primary, value_weight_primary, wo_master, wg_master, wu_master, wd_master, ga_master, gm_master, gq_master, gk_master):
        normalized_input = reduced_precision(norm_rows(inputs, reduced_precision(ga_master)))
        q_proj = reduced_backward(jnp.dot(normalized_input, reduced_precision(wq_master), precision=highest_precision)).reshape(TOKEN_TOTAL, QUERY_HEADS, HEAD_WIDTH)
        key_projected = reduced_backward(jnp.dot(normalized_input, reduced_precision(key_weight_primary), precision=highest_precision)).reshape(TOKEN_TOTAL, KEY_VALUE_HEADS, HEAD_WIDTH)
        value_rows = reduced_precision(reduced_backward(jnp.dot(normalized_input, reduced_precision(value_weight_primary), precision=highest_precision))).reshape(TOKEN_TOTAL, KEY_VALUE_HEADS, HEAD_WIDTH)
        query_rows = reduced_precision(reduced_backward(rotate(norm_rows(q_proj, reduced_precision(gq_master)), cosine, sine_table)))
        keys = reduced_precision(reduced_backward(rotate(norm_rows(key_projected, reduced_precision(gk_master)), cosine, sine_table)))
        attn_out = attention(query_rows, keys, value_rows, doc_ids, padded)
        attn_flat = reduced_precision(reduced_backward(attn_out)).reshape(TOKEN_TOTAL, QUERY_HEADS * HEAD_WIDTH)
        middle = inputs + reduced_backward(jnp.dot(attn_flat, reduced_precision(wo_master), precision=highest_precision))
        normed_mid = reduced_precision(norm_rows(middle, reduced_precision(gm_master)))
        gate_act = reduced_backward(jnp.dot(normed_mid, reduced_precision(wg_master), precision=highest_precision))
        up_act = reduced_backward(jnp.dot(normed_mid, reduced_precision(wu_master), precision=highest_precision))
        mixed_act = reduced_precision(gate_act * (1.0 / (1.0 + jnp.exp(-gate_act))) * up_act)
        return middle + reduced_backward(jnp.dot(mixed_act, reduced_precision(wd_master), precision=highest_precision))
    output_act, pullback = jax.vjp(forward, hidden_in.astype(jnp.float32), w_query.astype(jnp.float32), key_matrix.astype(jnp.float32), value_matrix.astype(jnp.float32), w_output.astype(jnp.float32), w_gate.astype(jnp.float32), w_up.astype(jnp.float32), w_down.astype(jnp.float32), attn_gain.astype(jnp.float32), mlp_gain.astype(jnp.float32), query_gain.astype(jnp.float32), key_gain.astype(jnp.float32))
    gradients = pullback(out_grad.astype(jnp.float32))
    return (output_act.astype(jnp.bfloat16), gradients[0].astype(jnp.bfloat16), gradients[1], gradients[2], gradients[3], gradients[4], gradients[5], gradients[6], gradients[7], gradients[8], gradients[9], gradients[10], gradients[11])
```

```python
import functools

import jax
import jax.numpy as jnp
from jax import lax
from jax.experimental import pallas as pl
from jax.experimental.pallas import tpu as pltpu
from jax.sharding import Mesh, PartitionSpec as P

QUERY_HEADS = 16
KEY_VALUE_HEADS = 8
HEAD_WIDTH = 128
FEEDFWD_UNITS = 3072
WINDOW_TOKENS = 1024
QROWS = 256
GROUP = QUERY_HEADS // KEY_VALUE_HEADS
SPAN_CHUNKS = (QROWS + WINDOW_TOKENS) // QROWS

norm_eps = 1e-06
rope_base = 1000000.0
score_scale = HEAD_WIDTH**-0.5
log2_e = 1.4426950408889634
bf16 = jnp.bfloat16
f32 = jnp.float32


def nt_dot(left, right):
    return lax.dot_general(left, right, (((1,), (1,)), ((), ())), preferred_element_type=f32)


def tn_dot(left, right):
    return lax.dot_general(left, right, (((0,), (0,)), ((), ())), preferred_element_type=f32)


def nn_dot(left, right):
    return jnp.dot(left, right, preferred_element_type=f32)


def chunk_mask(bounds_ref, chunk):
    low = bounds_ref[0:1, :]
    high = bounds_ref[1:2, :]
    key = lax.broadcasted_iota(jnp.int32, (QROWS, QROWS), 0) + chunk * QROWS
    mask = (key >= low) & (key <= high)
    if chunk == SPAN_CHUNKS - 1:
        own = lax.broadcasted_iota(jnp.int32, (QROWS, QROWS), 1) + WINDOW_TOKENS
        mask = mask | (key == own)
    return mask


def attend_kernel(q_ref, k_ref, v_ref, bounds_ref, out_ref, total_ref):
    base = pl.multiple_of(pl.program_id(1) * QROWS, QROWS)
    heads = [q_ref[:, g * HEAD_WIDTH : (g + 1) * HEAD_WIDTH] for g in range(GROUP)]
    sums = [jnp.zeros((1, QROWS), f32) for g in range(GROUP)]
    outs = [jnp.zeros((HEAD_WIDTH, QROWS), f32) for g in range(GROUP)]
    for chunk in range(SPAN_CHUNKS):
        rows = pl.ds(base + chunk * QROWS, QROWS)
        keys = k_ref[rows, :]
        values = v_ref[rows, :]
        mask = chunk_mask(bounds_ref, chunk)
        for g in range(GROUP):
            scores = nt_dot(keys, heads[g])
            weights = jnp.where(mask, jnp.exp2(scores * (score_scale * log2_e)), 0.0)
            sums[g] = sums[g] + jnp.sum(weights, axis=0, keepdims=True)
            outs[g] = outs[g] + tn_dot(values, weights.astype(bf16))
    for g in range(GROUP):
        normed = outs[g] * (1.0 / sums[g])
        out_ref[:, g * HEAD_WIDTH : (g + 1) * HEAD_WIDTH] = normed.T.astype(bf16)
        total_ref[g : g + 1, :] = sums[g]


def attend(queries, kv_ext, bounds):
    rows = queries.shape[0]
    ext = kv_ext.shape[0]
    kv_heads = kv_ext.shape[1] // (2 * HEAD_WIDTH)
    blocks = rows // QROWS
    wide = GROUP * HEAD_WIDTH
    pairs = blocks * kv_heads * GROUP * SPAN_CHUNKS * QROWS * QROWS
    return pl.pallas_call(
        attend_kernel,
        grid=(kv_heads, blocks),
        in_specs=[
            pl.BlockSpec((QROWS, wide), lambda j, i: (i, j)),
            pl.BlockSpec((ext, HEAD_WIDTH), lambda j, i: (0, j)),
            pl.BlockSpec((ext, HEAD_WIDTH), lambda j, i: (0, kv_heads + j)),
            pl.BlockSpec((None, 8, QROWS), lambda j, i: (i, 0, 0)),
        ],
        out_specs=[
            pl.BlockSpec((QROWS, wide), lambda j, i: (i, j)),
            pl.BlockSpec((None, None, 8, QROWS), lambda j, i: (j, i, 0, 0)),
        ],
        out_shape=[
            jax.ShapeDtypeStruct((rows, kv_heads * wide), bf16),
            jax.ShapeDtypeStruct((kv_heads, blocks, 8, QROWS), f32),
        ],
        cost_estimate=pl.CostEstimate(
            flops=4 * pairs * HEAD_WIDTH, bytes_accessed=4 << 20, transcendentals=pairs
        ),
        name="attend",
    )(queries, kv_ext, kv_ext, bounds)


def attend_back_kernel(
    q_ref, k_ref, v_ref, bounds_ref, total_ref, out_ref, d_out_ref, d_q_ref, d_k_ref, d_v_ref
):
    block = pl.program_id(1)
    base = pl.multiple_of(block * QROWS, QROWS)

    @pl.when(block == 0)
    def clear():
        d_k_ref[...] = jnp.zeros_like(d_k_ref)
        d_v_ref[...] = jnp.zeros_like(d_v_ref)

    spans = [slice(g * HEAD_WIDTH, (g + 1) * HEAD_WIDTH) for g in range(GROUP)]
    heads = [q_ref[:, s] for s in spans]
    d_outs = [d_out_ref[:, s] for s in spans]
    shares = [1.0 / total_ref[g : g + 1, :] for g in range(GROUP)]
    deltas = []
    for g in range(GROUP):
        product = d_outs[g].astype(f32) * out_ref[:, spans[g]].astype(f32)
        deltas.append(jnp.sum(product.T, axis=0, keepdims=True))
    d_queries = [jnp.zeros((HEAD_WIDTH, QROWS), f32) for g in range(GROUP)]
    for chunk in range(SPAN_CHUNKS):
        rows = pl.ds(base + chunk * QROWS, QROWS)
        keys = k_ref[rows, :]
        values = v_ref[rows, :]
        mask = chunk_mask(bounds_ref, chunk)
        d_key = jnp.zeros((QROWS, HEAD_WIDTH), f32)
        d_value = jnp.zeros((QROWS, HEAD_WIDTH), f32)
        for g in range(GROUP):
            scores = nt_dot(keys, heads[g])
            probs = jnp.where(
                mask, jnp.exp2(scores * (score_scale * log2_e)) * shares[g], 0.0
            )
            d_probs = nt_dot(values, d_outs[g])
            d_scores = (probs * (d_probs - deltas[g]) * score_scale).astype(bf16)
            d_value = d_value + nn_dot(probs.astype(bf16), d_outs[g])
            d_key = d_key + nn_dot(d_scores, heads[g])
            d_queries[g] = d_queries[g] + tn_dot(keys, d_scores)
        d_k_ref[rows, :] += d_key
        d_v_ref[rows, :] += d_value
    for g in range(GROUP):
        d_q_ref[:, spans[g]] = d_queries[g].T.astype(bf16)


def attend_back(queries, kv_ext, bounds, totals, outs, d_outs):
    rows = queries.shape[0]
    ext = kv_ext.shape[0]
    kv_heads = kv_ext.shape[1] // (2 * HEAD_WIDTH)
    blocks = rows // QROWS
    wide = GROUP * HEAD_WIDTH
    pairs = blocks * kv_heads * GROUP * SPAN_CHUNKS * QROWS * QROWS
    block_spec = pl.BlockSpec((QROWS, wide), lambda j, i: (i, j))
    return pl.pallas_call(
        attend_back_kernel,
        grid=(kv_heads, blocks),
        in_specs=[
            block_spec,
            pl.BlockSpec((ext, HEAD_WIDTH), lambda j, i: (0, j)),
            pl.BlockSpec((ext, HEAD_WIDTH), lambda j, i: (0, kv_heads + j)),
            pl.BlockSpec((None, 8, QROWS), lambda j, i: (i, 0, 0)),
            pl.BlockSpec((None, None, 8, QROWS), lambda j, i: (j, i, 0, 0)),
            block_spec,
            block_spec,
        ],
        out_specs=[
            block_spec,
            pl.BlockSpec((ext, HEAD_WIDTH), lambda j, i: (0, j)),
            pl.BlockSpec((ext, HEAD_WIDTH), lambda j, i: (0, j)),
        ],
        out_shape=[
            jax.ShapeDtypeStruct((rows, kv_heads * wide), bf16),
            jax.ShapeDtypeStruct((ext, kv_heads * HEAD_WIDTH), f32),
            jax.ShapeDtypeStruct((ext, kv_heads * HEAD_WIDTH), f32),
        ],
        cost_estimate=pl.CostEstimate(
            flops=10 * pairs * HEAD_WIDTH, bytes_accessed=12 << 20, transcendentals=pairs
        ),
        name="attend_back",
    )(queries, kv_ext, kv_ext, bounds, totals, outs, d_outs)


def norm_stats(rows):
    return lax.rsqrt(jnp.mean(rows * rows, axis=-1, keepdims=True) + norm_eps)


def norm_back(d_normed, rows, stats, gains):
    scaled = d_normed * gains
    unit = rows * stats
    return stats * (scaled - unit * jnp.mean(scaled * unit, axis=-1, keepdims=True))


def rotate(rows, cosine, sine):
    half = rows.shape[-1] // 2
    turned = jnp.concatenate([-rows[..., half:], rows[..., :half]], axis=-1)
    return rows * cosine + turned * sine


def rotate_back(d_rows, cosine, sine):
    half = d_rows.shape[-1] // 2
    turned = jnp.concatenate([d_rows[..., half:], -d_rows[..., :half]], axis=-1)
    return d_rows * cosine + turned * sine


def body(
    hidden_in,
    doc_lengths,
    pad_lengths,
    w_query,
    key_matrix,
    value_matrix,
    w_output,
    w_gate,
    w_up,
    w_down,
    attn_gain,
    mlp_gain,
    query_gain,
    key_gain,
    out_grad,
):
    dp_axes = ("q", "c")
    core = lax.axis_index("c")
    group = lax.axis_index("q") * 2 + core
    part = lax.axis_index("seq")
    groups = lax.axis_size("q") * 2
    parts = lax.axis_size("seq")
    tokens, width = hidden_in.shape
    group_rows = tokens * parts
    slice_rows = width // groups
    units = FEEDFWD_UNITS // 2
    q_cols = QUERY_HEADS * HEAD_WIDTH // parts
    kv_cols = KEY_VALUE_HEADS * HEAD_WIDTH // parts
    attn_cols = q_cols + 2 * kv_cols
    pack_cols = attn_cols + q_cols
    core_swap = [(0, 1), (1, 0)]

    hidden_all = lax.all_to_all(
        jnp.broadcast_to(hidden_in[None], (parts, tokens, width)), "seq", 0, 0, tiled=True
    ).reshape(group_rows, width)

    def head_cols(matrix, count):
        return lax.dynamic_slice_in_dim(matrix, part * count, count, 1)

    gain_cols = jnp.stack(
        [
            attn_gain,
            mlp_gain,
            jnp.pad(query_gain, (0, slice_rows - query_gain.shape[0])),
            jnp.pad(key_gain, (0, slice_rows - key_gain.shape[0])),
        ],
        axis=1,
    )
    packed = jnp.concatenate(
        [
            head_cols(w_query, q_cols),
            head_cols(key_matrix, kv_cols),
            head_cols(value_matrix, kv_cols),
            lax.dynamic_slice_in_dim(w_output, part * q_cols, q_cols, 0).T,
            jnp.pad(gain_cols, ((0, 0), (0, HEAD_WIDTH - gain_cols.shape[1]))),
        ],
        axis=1,
    ).astype(bf16)
    attn_w = lax.all_gather(packed, dp_axes, axis=0, tiled=True)
    w_qkv = attn_w[:, :attn_cols]
    w_out_t = attn_w[:, attn_cols:pack_cols]
    gains = attn_w[:, pack_cols : pack_cols + 4].astype(f32).T
    ga = gains[0]
    gm = gains[1]
    head_piece = query_gain.shape[0]
    gq = gains[2].reshape(groups, slice_rows)[:, :head_piece].reshape(HEAD_WIDTH)
    gk = gains[3].reshape(groups, slice_rows)[:, :head_piece].reshape(HEAD_WIDTH)

    def halves(matrix):
        return matrix.astype(bf16).reshape(slice_rows, 2, units).transpose(1, 0, 2)

    mlp_pack = jnp.concatenate([halves(w_gate), halves(w_up), halves(w_down.T)], axis=2)
    mlp_pack = lax.all_to_all(mlp_pack, "c", 0, 0, tiled=True).reshape(2 * slice_rows, 3 * units)
    mlp_w = lax.all_gather(mlp_pack, "q", axis=0, tiled=True)
    w_gu = mlp_w[:, : 2 * units]
    w_down_t = mlp_w[:, 2 * units :]
    grad_pair = jnp.concatenate([out_grad, lax.ppermute(out_grad, "c", core_swap)], axis=0)

    doc_ends = jnp.cumsum(doc_lengths)
    doc_starts = doc_ends - doc_lengths
    pad_starts = doc_ends - pad_lengths
    first = group * group_rows
    token = first + jnp.arange(group_rows, dtype=jnp.int32)
    inside = (token[:, None] >= doc_starts[None, :]) & (token[:, None] < doc_ends[None, :])
    start = jnp.sum(jnp.where(inside, doc_starts[None, :], 0), axis=1)
    pad_start = jnp.sum(jnp.where(inside, pad_starts[None, :], 0), axis=1)
    inv_freq = rope_base ** (-jnp.arange(HEAD_WIDTH // 2, dtype=f32) * 2.0 / HEAD_WIDTH)
    angles = (token - start).astype(f32)[:, None] * inv_freq[None, :]
    cosine = jnp.tile(jnp.cos(angles), (1, 2))[:, None, :]
    sine = jnp.tile(jnp.sin(angles), (1, 2))[:, None, :]
    blocks = group_rows // QROWS
    offset = (token // QROWS) * QROWS - WINDOW_TOKENS
    low = jnp.maximum(start, token - (WINDOW_TOKENS - 1)) - offset
    high = jnp.minimum(token, pad_start - 1) - offset
    bounds = jnp.pad(
        jnp.stack([low.reshape(blocks, QROWS), high.reshape(blocks, QROWS)], axis=1),
        ((0, 0), (0, 6), (0, 0)),
    )

    rows_all = hidden_all.astype(f32)
    stats_all = norm_stats(rows_all)
    normed_all = (rows_all * stats_all * ga).astype(bf16)
    qkv_proj = nn_dot(normed_all, w_qkv)
    qk_proj = qkv_proj[:, : q_cols + kv_cols].reshape(group_rows, -1, HEAD_WIDTH)
    qk_gain = jnp.concatenate(
        [
            jnp.broadcast_to(gq, (q_cols // HEAD_WIDTH, HEAD_WIDTH)),
            jnp.broadcast_to(gk, (kv_cols // HEAD_WIDTH, HEAD_WIDTH)),
        ],
        axis=0,
    )
    qk_stats = norm_stats(qk_proj)
    qk_rows = rotate(qk_proj * qk_stats * qk_gain, cosine, sine).astype(bf16)
    qk_rows = qk_rows.reshape(group_rows, q_cols + kv_cols)
    queries = qk_rows[:, :q_cols]
    kv_own = jnp.concatenate(
        [qk_rows[:, q_cols:], qkv_proj[:, q_cols + kv_cols :].astype(bf16)], axis=1
    )
    tail = lax.ppermute(
        kv_own[group_rows - WINDOW_TOKENS :], dp_axes, [(i, i + 1) for i in range(groups - 1)]
    )
    kv_ext = jnp.concatenate([tail, kv_own], axis=0)
    attn, totals = attend(queries, kv_ext, bounds)

    attn_part = nt_dot(attn, w_out_t).astype(bf16)
    attn_sum = lax.psum_scatter(attn_part, "seq", scatter_dimension=0, tiled=True)
    middle = hidden_in.astype(f32) + attn_sum.astype(f32)
    mid_stats = norm_stats(middle)
    normed_mid = (middle * mid_stats * gm).astype(bf16)

    mid_pair = jnp.concatenate([normed_mid, lax.ppermute(normed_mid, "c", core_swap)], axis=0)
    gate_up = nn_dot(mid_pair, w_gu)
    gate = gate_up[:, :units]
    up = gate_up[:, units:]
    sig = 1.0 / (1.0 + jnp.exp(-gate))
    mixed = (gate * sig * up).astype(bf16)
    d_mixed = nn_dot(grad_pair, w_down_t)
    d_gate = (d_mixed * up * sig * (1.0 + gate * (1.0 - sig))).astype(bf16)
    d_up = (d_mixed * gate * sig).astype(bf16)
    d_gate_up = jnp.concatenate([d_gate, d_up], axis=1)
    d_mid_part = nt_dot(d_gate_up, w_gu)
    d_mid_other = lax.ppermute(d_mid_part[tokens:].astype(bf16), "c", core_swap)
    d_normed_mid = d_mid_part[:tokens] + d_mid_other.astype(f32)
    d_middle = out_grad.astype(f32) + norm_back(d_normed_mid, middle, mid_stats, gm)
    d_mlp_gain = jnp.sum(d_normed_mid * middle * mid_stats, axis=0)
    d_proj = d_middle.astype(bf16)
    d_proj_all = lax.all_to_all(
        jnp.broadcast_to(d_proj[None], (parts, tokens, width)), "seq", 0, 0, tiled=True
    ).reshape(group_rows, width)

    out_part = nt_dot(mixed, w_down_t)
    out_other = lax.ppermute(out_part[tokens:].astype(bf16), "c", core_swap)
    output_act = (middle + out_part[:tokens] + out_other.astype(f32)).astype(bf16)

    mlp_grad = jnp.concatenate(
        [tn_dot(mid_pair, d_gate_up), tn_dot(grad_pair, mixed)], axis=1
    ).astype(bf16)
    mlp_grad = lax.psum_scatter(mlp_grad, "q", scatter_dimension=0, tiled=True)
    mlp_grad = lax.psum(mlp_grad, "seq")
    mlp_grad = lax.all_to_all(
        mlp_grad.reshape(2, slice_rows, 3 * units), "c", 0, 0, tiled=True
    )

    def unhalve(column):
        return (
            mlp_grad[:, :, column * units : (column + 1) * units]
            .transpose(1, 0, 2)
            .reshape(slice_rows, 2 * units)
            .astype(f32)
        )

    d_attn = nn_dot(d_proj_all, w_out_t).astype(bf16)
    w_out_grad = tn_dot(d_proj_all, attn)
    d_queries, d_k_ext, d_v_ext = attend_back(queries, kv_ext, bounds, totals, attn, d_attn)
    d_kv_ext = jnp.concatenate([d_k_ext, d_v_ext], axis=1)
    d_kv_tail = lax.ppermute(
        d_kv_ext[:WINDOW_TOKENS].astype(bf16), dp_axes, [(i + 1, i) for i in range(groups - 1)]
    )
    d_kv = d_kv_ext[WINDOW_TOKENS:]
    d_kv = jnp.concatenate(
        [
            d_kv[: group_rows - WINDOW_TOKENS],
            d_kv[group_rows - WINDOW_TOKENS :] + d_kv_tail.astype(f32),
        ],
        axis=0,
    ).astype(bf16)

    d_qk = jnp.concatenate([d_queries, d_kv[:, :kv_cols]], axis=1).astype(f32)
    d_qk = rotate_back(d_qk.reshape(group_rows, -1, HEAD_WIDTH), cosine, sine)
    d_qk_gain = jnp.sum(d_qk * qk_proj * qk_stats, axis=0)
    q_heads = q_cols // HEAD_WIDTH
    d_query_gain = jnp.sum(d_qk_gain[:q_heads], axis=0)
    d_key_gain = jnp.sum(d_qk_gain[q_heads:], axis=0)
    d_qk_proj = norm_back(d_qk, qk_proj, qk_stats, qk_gain).astype(bf16)
    d_qkv = jnp.concatenate(
        [d_qk_proj.reshape(group_rows, q_cols + kv_cols), d_kv[:, kv_cols:]], axis=1
    )
    d_in_part = nt_dot(d_qkv, w_qkv)
    d_attn_gain = jnp.sum(d_in_part * rows_all * stats_all, axis=0)
    d_normed_in = lax.psum_scatter(
        d_in_part.astype(bf16), "seq", scatter_dimension=0, tiled=True
    ).astype(f32)
    rows_own = hidden_in.astype(f32)
    in_grad = (
        d_middle + norm_back(d_normed_in, rows_own, norm_stats(rows_own), ga)
    ).astype(bf16)

    def spread(head_gain):
        return jnp.pad(
            head_gain.reshape(groups, head_piece), ((0, 0), (0, slice_rows - head_piece))
        ).reshape(width)

    gain_grads = jnp.stack(
        [d_attn_gain, d_mlp_gain, spread(d_query_gain), spread(d_key_gain)], axis=1
    )
    attn_grad = jnp.concatenate(
        [
            tn_dot(normed_all, d_qkv),
            w_out_grad,
            jnp.pad(gain_grads, ((0, 0), (0, HEAD_WIDTH - gain_grads.shape[1]))),
        ],
        axis=1,
    ).astype(bf16)
    by_core = attn_grad.reshape(groups // 2, 2, slice_rows, -1)
    keep = lax.dynamic_index_in_dim(by_core, core, 1, keepdims=False)
    give = lax.dynamic_index_in_dim(by_core, 1 - core, 1, keepdims=False)
    chip_sum = keep.astype(f32) + lax.ppermute(give, "c", core_swap).astype(f32)
    chip_sum = chip_sum.astype(bf16).reshape(width // 2, -1)
    attn_grad = lax.psum_scatter(chip_sum, "q", scatter_dimension=0, tiled=True)
    attn_grad = lax.all_gather(attn_grad, "seq", axis=0)
    attn_grad = attn_grad.astype(f32)

    def joined(begin, count):
        return (
            attn_grad[:, :, begin : begin + count].transpose(1, 0, 2).reshape(slice_rows, -1)
        )

    gain_sums = jnp.sum(attn_grad[:, :, pack_cols : pack_cols + 4], axis=0)
    return (
        output_act,
        in_grad,
        joined(0, q_cols),
        joined(q_cols, kv_cols),
        joined(q_cols + kv_cols, kv_cols),
        joined(attn_cols, q_cols).T,
        unhalve(0),
        unhalve(1),
        unhalve(2).T,
        gain_sums[:, 0],
        gain_sums[:, 1],
        gain_sums[:head_piece, 2],
        gain_sums[:head_piece, 3],
    )


def solution(mesh):
    groups, parts = mesh.devices.shape
    mesh = Mesh(mesh.devices.reshape(groups // 2, 2, parts), ("q", "c", "seq"))
    dp = ("q", "c")
    tokens = P(("q", "c", "seq"), None)
    rows = P(dp, None)
    cols = P(None, dp)
    in_specs = (
        tokens, P(), P(), rows, rows, rows, cols, rows, rows, cols,
        P(dp), P(dp), P(dp), P(dp), tokens,
    )
    out_specs = (
        tokens, tokens, rows, rows, rows, cols, rows, rows, cols, P(dp), P(dp), P(dp), P(dp),
    )
    return jax.shard_map(body, mesh=mesh, in_specs=in_specs, out_specs=out_specs, check_vma=False)
```

```python
import functools

import jax
import jax.numpy as jnp
from jax import lax
from jax.experimental import pallas as pl
from jax.experimental.pallas import tpu as pltpu
from jax.sharding import Mesh, PartitionSpec as P

QUERY_HEADS = 16
KEY_VALUE_HEADS = 8
HEAD_WIDTH = 128
FEEDFWD_UNITS = 3072
WINDOW_TOKENS = 1024
QROWS = 256
GROUP = QUERY_HEADS // KEY_VALUE_HEADS
TAIL_CHUNKS = WINDOW_TOKENS // QROWS

norm_eps = 1e-06
rope_base = 1000000.0
score_scale = HEAD_WIDTH**-0.5
log2_e = 1.4426950408889634
bf16 = jnp.bfloat16
f32 = jnp.float32
dp_axes = ("q", "c")
core_swap = [(0, 1), (1, 0)]


def nt_dot(left, right):
    return lax.dot_general(left, right, (((1,), (1,)), ((), ())), preferred_element_type=f32)


def tn_dot(left, right):
    return lax.dot_general(left, right, (((0,), (0,)), ((), ())), preferred_element_type=f32)


def nn_dot(left, right):
    return jnp.dot(left, right, preferred_element_type=f32)


def shape_of(dims, kind):
    return jax.ShapeDtypeStruct(dims, kind)


def cost(flops, moved, exps=0):
    return pl.CostEstimate(flops=int(flops), bytes_accessed=int(moved), transcendentals=int(exps))


def norm_stats(rows):
    return lax.rsqrt(jnp.mean(rows * rows, axis=-1, keepdims=True) + norm_eps)


def norm_back(d_normed, rows, stats, gains):
    scaled = d_normed * gains
    unit = rows * stats
    return stats * (scaled - unit * jnp.mean(scaled * unit, axis=-1, keepdims=True))


def pack_attn_kernel(part_ref, wq_ref, wk_ref, wv_ref, wo_ref, gains_ref, out_ref):
    column = 0
    for piece in (
        wq_ref[...].astype(bf16),
        wk_ref[...].astype(bf16),
        wv_ref[...].astype(bf16),
        wo_ref[...].T.astype(bf16),
        gains_ref[...].astype(bf16),
    ):
        out_ref[:, column : column + piece.shape[1]] = piece
        column += piece.shape[1]


def pack_attn(part, parts, w_query, key_matrix, value_matrix, w_output, gain_cols):
    rows = w_query.shape[0]
    q_cols = w_query.shape[1] // parts
    kv_cols = key_matrix.shape[1] // parts
    total = 2 * q_cols + 2 * kv_cols + HEAD_WIDTH
    return pl.pallas_call(
        pack_attn_kernel,
        grid_spec=pltpu.PrefetchScalarGridSpec(
            num_scalar_prefetch=1,
            grid=(1,),
            in_specs=[
                pl.BlockSpec((rows, q_cols), lambda i, p: (0, p[0])),
                pl.BlockSpec((rows, kv_cols), lambda i, p: (0, p[0])),
                pl.BlockSpec((rows, kv_cols), lambda i, p: (0, p[0])),
                pl.BlockSpec((q_cols, rows), lambda i, p: (p[0], 0)),
                pl.BlockSpec((rows, HEAD_WIDTH), lambda i, p: (0, 0)),
            ],
            out_specs=pl.BlockSpec((rows, total), lambda i, p: (0, 0)),
        ),
        out_shape=shape_of((rows, total), bf16),
        cost_estimate=cost(0, rows * total * 6),
        name="pack_attn",
    )(part, w_query, key_matrix, value_matrix, w_output, gain_cols)


def pack_mlp_kernel(core_ref, wg_ref, wu_ref, wd_ref, own_ref, give_ref):
    units = wg_ref.shape[1]

    def fill(out_ref):
        out_ref[:, :units] = wg_ref[...].astype(bf16)
        out_ref[:, units : 2 * units] = wu_ref[...].astype(bf16)
        out_ref[:, 2 * units :] = wd_ref[...].T.astype(bf16)

    @pl.when(pl.program_id(0) == 0)
    def first():
        fill(give_ref)

    @pl.when(pl.program_id(0) == 1)
    def second():
        fill(own_ref)


def pack_mlp(core, w_gate, w_up, w_down):
    rows = w_gate.shape[0]
    units = w_gate.shape[1] // 2
    half = lambda i, c: (c[0] + 1 - i) % 2
    return pl.pallas_call(
        pack_mlp_kernel,
        grid_spec=pltpu.PrefetchScalarGridSpec(
            num_scalar_prefetch=1,
            grid=(2,),
            in_specs=[
                pl.BlockSpec((rows, units), lambda i, c: (0, half(i, c))),
                pl.BlockSpec((rows, units), lambda i, c: (0, half(i, c))),
                pl.BlockSpec((units, rows), lambda i, c: (half(i, c), 0)),
            ],
            out_specs=[
                pl.BlockSpec((rows, 3 * units), lambda i, c: (c[0], 0)),
                pl.BlockSpec((rows, 3 * units), lambda i, c: (0, 0)),
            ],
        ),
        out_shape=[shape_of((2 * rows, 3 * units), bf16), shape_of((rows, 3 * units), bf16)],
        cost_estimate=cost(0, rows * units * 36),
        name="pack_mlp",
    )(core, w_gate, w_up, w_down)


def unpack_mlp_kernel(core_ref, own_ref, got_ref, gate_ref, up_ref, down_ref):
    units = gate_ref.shape[1]

    def fill(in_ref):
        gate_ref[...] = in_ref[:, :units].astype(f32)
        up_ref[...] = in_ref[:, units : 2 * units].astype(f32)
        down_ref[...] = in_ref[:, 2 * units :].astype(f32).T

    @pl.when(pl.program_id(0) == 0)
    def first():
        fill(own_ref)

    @pl.when(pl.program_id(0) == 1)
    def second():
        fill(got_ref)


def unpack_mlp(core, sums, got):
    rows = got.shape[0]
    units = got.shape[1] // 3
    half = lambda i, c: (c[0] + i) % 2
    return pl.pallas_call(
        unpack_mlp_kernel,
        grid_spec=pltpu.PrefetchScalarGridSpec(
            num_scalar_prefetch=1,
            grid=(2,),
            in_specs=[
                pl.BlockSpec((rows, 3 * units), lambda i, c: (c[0], 0)),
                pl.BlockSpec((rows, 3 * units), lambda i, c: (0, 0)),
            ],
            out_specs=[
                pl.BlockSpec((rows, units), lambda i, c: (0, half(i, c))),
                pl.BlockSpec((rows, units), lambda i, c: (0, half(i, c))),
                pl.BlockSpec((units, rows), lambda i, c: (half(i, c), 0)),
            ],
        ),
        out_shape=[
            shape_of((rows, 2 * units), f32),
            shape_of((rows, 2 * units), f32),
            shape_of((2 * units, rows), f32),
        ],
        cost_estimate=cost(0, rows * units * 36),
        name="unpack_mlp",
    )(core, sums, got)


def unpack_attn_kernel(in_ref, wq_ref, wk_ref, wv_ref, wo_ref):
    column = 0
    for out_ref in (wq_ref, wk_ref, wv_ref):
        count = out_ref.shape[1]
        out_ref[...] = in_ref[:, column : column + count].astype(f32)
        column += count
    wo_ref[...] = in_ref[:, column : column + wo_ref.shape[0]].astype(f32).T


def unpack_attn(gathered, q_cols, kv_cols):
    parts, rows, total = gathered.shape
    return pl.pallas_call(
        unpack_attn_kernel,
        grid=(parts,),
        in_specs=[pl.BlockSpec((None, rows, total), lambda i: (i, 0, 0))],
        out_specs=[
            pl.BlockSpec((rows, q_cols), lambda i: (0, i)),
            pl.BlockSpec((rows, kv_cols), lambda i: (0, i)),
            pl.BlockSpec((rows, kv_cols), lambda i: (0, i)),
            pl.BlockSpec((q_cols, rows), lambda i: (i, 0)),
        ],
        out_shape=[
            shape_of((rows, parts * q_cols), f32),
            shape_of((rows, parts * kv_cols), f32),
            shape_of((rows, parts * kv_cols), f32),
            shape_of((parts * q_cols, rows), f32),
        ],
        cost_estimate=cost(0, parts * rows * total * 6),
        name="unpack_attn",
    )(gathered)


def pick(refs, scratch):
    for k, ref in enumerate(refs):

        @pl.when(pl.program_id(0) == k)
        def take(ref=ref):
            scratch[...] = ref[...]


def turn(rows):
    half = HEAD_WIDTH // 2
    return jnp.concatenate([rows[:, half:], rows[:, :half]], axis=1)


def project_kernel(parts, q_cols, kv_cols, part_ref, *refs):
    blocks = refs[:parts]
    w_ref, ga_ref, gqk_ref, cos_ref, sin_ref, normed_ref, q_ref, kv_ref, proj_ref, x_ref = refs[parts:]
    pick(blocks, x_ref)
    rows = x_ref[...].astype(f32)
    normed = (rows * norm_stats(rows) * ga_ref[...]).astype(bf16)
    normed_ref[...] = normed
    cosine = cos_ref[...]
    sine = sin_ref[...]
    qk_cols = q_cols + kv_cols
    proj = nn_dot(normed, w_ref[...])
    proj_ref[...] = proj[:, :qk_cols]
    kv_ref[:, kv_cols:] = proj[:, qk_cols:].astype(bf16)
    for column in range(0, qk_cols, HEAD_WIDTH):
        head = proj[:, column : column + HEAD_WIDTH]
        gain = gqk_ref[0:1, :] if column < q_cols else gqk_ref[1:2, :]
        head = head * norm_stats(head) * gain
        head = (head * cosine + turn(head) * sine).astype(bf16)
        if column < q_cols:
            q_ref[:, column : column + HEAD_WIDTH] = head
        else:
            kv_ref[:, column - q_cols : column - q_cols + HEAD_WIDTH] = head


def project(part, blocks, attn_w, ga, gqk, cosine, sine, q_cols, kv_cols):
    parts = len(blocks)
    tokens, width = blocks[0].shape
    attn_cols = q_cols + 2 * kv_cols
    place = lambda k, p: ((p[0] + parts - k) % parts, 0)
    fixed = lambda k, p: (0, 0)
    rows = parts * tokens
    return pl.pallas_call(
        functools.partial(project_kernel, parts, q_cols, kv_cols),
        grid_spec=pltpu.PrefetchScalarGridSpec(
            num_scalar_prefetch=1,
            grid=(parts,),
            in_specs=[pl.BlockSpec((tokens, width), fixed)] * parts
            + [
                pl.BlockSpec((width, attn_cols), fixed),
                pl.BlockSpec((1, width), fixed),
                pl.BlockSpec((2, HEAD_WIDTH), fixed),
                pl.BlockSpec((tokens, HEAD_WIDTH), place),
                pl.BlockSpec((tokens, HEAD_WIDTH), place),
            ],
            out_specs=[
                pl.BlockSpec((tokens, width), place),
                pl.BlockSpec((tokens, q_cols), place),
                pl.BlockSpec((tokens, 2 * kv_cols), place),
                pl.BlockSpec((tokens, q_cols + kv_cols), place),
            ],
            scratch_shapes=[pltpu.VMEM((tokens, width), bf16)],
        ),
        out_shape=[
            shape_of((rows, width), bf16),
            shape_of((rows, q_cols), bf16),
            shape_of((rows, 2 * kv_cols), bf16),
            shape_of((rows, q_cols + kv_cols), f32),
        ],
        cost_estimate=cost(2 * rows * width * attn_cols, 12 << 20),
        name="project",
    )(part, *blocks, attn_w, ga, gqk, cosine, sine)


def project_back_kernel(
    parts, tail_from, q_cols, kv_cols, part_ref, dq_ref, dkv_ref, tail_ref, proj_ref,
    w_ref, gqk_ref, cos_ref, sin_ref, *refs
):
    blocks = refs[:parts]
    outs = refs[parts : 2 * parts]
    dqkv_ref, gain_ref, head_gain_ref, x_ref = refs[2 * parts :]
    step = pl.program_id(0)
    pick(blocks, x_ref)
    block = (part_ref[0] + step) % parts

    @pl.when(step == 0)
    def clear():
        gain_ref[...] = jnp.zeros_like(gain_ref)
        head_gain_ref[...] = jnp.zeros_like(head_gain_ref)

    cosine = cos_ref[...]
    sine = sin_ref[...]
    has_tail = jnp.where(block >= tail_from, 1.0, 0.0)
    dkv = (dkv_ref[...] + tail_ref[...].astype(f32) * has_tail).astype(bf16)
    dqkv_ref[:, q_cols + kv_cols :] = dkv[:, kv_cols:]
    for column in range(0, q_cols + kv_cols, HEAD_WIDTH):
        index = 0 if column < q_cols else 1
        if index == 0:
            d_head = dq_ref[:, column : column + HEAD_WIDTH].astype(f32)
        else:
            d_head = dkv[:, column - q_cols : column - q_cols + HEAD_WIDTH].astype(f32)
        d_head = d_head * cosine + turn(d_head * sine)
        head = proj_ref[:, column : column + HEAD_WIDTH]
        stats = norm_stats(head)
        unit = head * stats
        head_gain_ref[index : index + 1, :] += jnp.sum(d_head * unit, axis=0, keepdims=True)
        scaled = d_head * gqk_ref[index : index + 1, :]
        d_proj = stats * (scaled - unit * jnp.mean(scaled * unit, axis=-1, keepdims=True))
        dqkv_ref[:, column : column + HEAD_WIDTH] = d_proj.astype(bf16)
    d_in = nt_dot(dqkv_ref[...], w_ref[...])
    rows = x_ref[...].astype(f32)
    gain_ref[0:1, :] += jnp.sum(d_in * (rows * norm_stats(rows)), axis=0, keepdims=True)
    d_in = d_in.astype(bf16)
    for k, out_ref in enumerate(outs):

        @pl.when(step == k)
        def put(out_ref=out_ref):
            out_ref[...] = d_in


def project_back(part, blocks, dq, dkv, tail, proj, attn_w, gqk, cosine, sine):
    parts = len(blocks)
    rows, q_cols = dq.shape
    kv_cols = dkv.shape[1] // 2
    tokens, width = blocks[0].shape
    attn_cols = q_cols + 2 * kv_cols
    tail_from = (rows - WINDOW_TOKENS) // tokens
    place = lambda k, p: ((p[0] + k) % parts, 0)
    tail_place = lambda k, p: (jnp.maximum((p[0] + k) % parts - tail_from, 0), 0)
    fixed = lambda k, p: (0, 0)
    return pl.pallas_call(
        functools.partial(project_back_kernel, parts, tail_from, q_cols, kv_cols),
        grid_spec=pltpu.PrefetchScalarGridSpec(
            num_scalar_prefetch=1,
            grid=(parts,),
            in_specs=[
                pl.BlockSpec((tokens, q_cols), place),
                pl.BlockSpec((tokens, 2 * kv_cols), place),
                pl.BlockSpec((tokens, 2 * kv_cols), tail_place),
                pl.BlockSpec((tokens, q_cols + kv_cols), place),
                pl.BlockSpec((width, attn_cols), fixed),
                pl.BlockSpec((2, HEAD_WIDTH), fixed),
                pl.BlockSpec((tokens, HEAD_WIDTH), place),
                pl.BlockSpec((tokens, HEAD_WIDTH), place),
            ]
            + [pl.BlockSpec((tokens, width), fixed)] * parts,
            out_specs=[pl.BlockSpec((tokens, width), fixed)] * parts
            + [
                pl.BlockSpec((tokens, attn_cols), place),
                pl.BlockSpec((8, width), fixed),
                pl.BlockSpec((8, HEAD_WIDTH), fixed),
            ],
            scratch_shapes=[pltpu.VMEM((tokens, width), bf16)],
        ),
        out_shape=[shape_of((tokens, width), bf16)] * parts
        + [
            shape_of((rows, attn_cols), bf16),
            shape_of((8, width), f32),
            shape_of((8, HEAD_WIDTH), f32),
        ],
        cost_estimate=cost(2 * rows * width * attn_cols, 16 << 20),
        name="project_back",
    )(part, dq, dkv, tail, proj, attn_w, gqk, cosine, sine, *blocks)


def out_proj_kernel(parts, part_ref, attn_ref, w_ref, *outs):
    result = nt_dot(attn_ref[...], w_ref[...]).astype(bf16)
    for k, out_ref in enumerate(outs):

        @pl.when(pl.program_id(0) == k)
        def put(out_ref=out_ref):
            out_ref[...] = result


def out_proj(part, parts, attn, attn_w, w_block):
    rows, q_cols = attn.shape
    width = attn_w.shape[0]
    tokens = rows // parts
    return pl.pallas_call(
        functools.partial(out_proj_kernel, parts),
        grid_spec=pltpu.PrefetchScalarGridSpec(
            num_scalar_prefetch=1,
            grid=(parts,),
            in_specs=[
                pl.BlockSpec((tokens, q_cols), lambda k, p: ((p[0] + k) % parts, 0)),
                pl.BlockSpec((width, q_cols), lambda k, p: (0, w_block)),
            ],
            out_specs=[pl.BlockSpec((tokens, width), lambda k, p: (0, 0))] * parts,
        ),
        out_shape=[shape_of((tokens, width), bf16)] * parts,
        cost_estimate=cost(2 * rows * width * q_cols, 4 << 20),
        name="out_proj",
    )(part, attn, attn_w)


def out_proj_back_kernel(parts, part_ref, *refs):
    blocks = refs[:parts]
    attn_ref, w_ref, d_attn_ref, d_w_ref, x_ref = refs[parts:]
    pick(blocks, x_ref)
    d_proj = x_ref[...]
    d_attn_ref[...] = nn_dot(d_proj, w_ref[...]).astype(bf16)

    @pl.when(pl.program_id(0) == 0)
    def clear():
        d_w_ref[...] = jnp.zeros_like(d_w_ref)

    d_w_ref[...] += tn_dot(d_proj, attn_ref[...])


def out_proj_back(part, blocks, attn, attn_w, w_block):
    parts = len(blocks)
    rows, q_cols = attn.shape
    tokens, width = blocks[0].shape
    place = lambda k, p: ((p[0] + parts - k) % parts, 0)
    fixed = lambda k, p: (0, 0)
    return pl.pallas_call(
        functools.partial(out_proj_back_kernel, parts),
        grid_spec=pltpu.PrefetchScalarGridSpec(
            num_scalar_prefetch=1,
            grid=(parts,),
            in_specs=[pl.BlockSpec((tokens, width), fixed)] * parts
            + [
                pl.BlockSpec((tokens, q_cols), place),
                pl.BlockSpec((width, q_cols), lambda k, p: (0, w_block)),
            ],
            out_specs=[
                pl.BlockSpec((tokens, q_cols), place),
                pl.BlockSpec((width, q_cols), fixed),
            ],
            scratch_shapes=[pltpu.VMEM((tokens, width), bf16)],
        ),
        out_shape=[shape_of((rows, q_cols), bf16), shape_of((width, q_cols), f32)],
        cost_estimate=cost(4 * rows * width * q_cols, 8 << 20),
        name="out_proj_back",
    )(part, *blocks, attn, attn_w)


def chunk_mask(bounds_ref, block, chunk):
    low = bounds_ref[block, 0:1, :]
    high = bounds_ref[block, 1:2, :]
    key = lax.broadcasted_iota(jnp.int32, (QROWS, QROWS), 0) + chunk * QROWS
    mask = (key >= low) & (key <= high)
    if chunk == TAIL_CHUNKS:
        own = lax.broadcasted_iota(jnp.int32, (QROWS, QROWS), 1) + WINDOW_TOKENS
        mask = mask | (key == own)
    return mask


def head_span(g):
    return slice(g * HEAD_WIDTH, (g + 1) * HEAD_WIDTH)


def chunk_forward(q_ref, k_ref, v_ref, bounds_ref, block, chunk, row, sums, outs):
    here = slice(block * QROWS, (block + 1) * QROWS)
    there = slice(row, row + QROWS)
    mask = chunk_mask(bounds_ref, block, chunk)
    keys = k_ref[there, :]
    values = v_ref[there, :]
    for g in range(GROUP):
        scores = nt_dot(keys, q_ref[here, head_span(g)])
        weights = jnp.where(mask, jnp.exp2(scores * (score_scale * log2_e)), 0.0)
        sums[g] = sums[g] + jnp.sum(weights, axis=0, keepdims=True)
        outs[g] = outs[g] + tn_dot(values, weights.astype(bf16))


def attend_own_kernel(q_ref, k_ref, v_ref, bounds_ref, out_ref, total_ref):
    for block in range(q_ref.shape[0] // QROWS):
        here = slice(block * QROWS, (block + 1) * QROWS)
        sums = [jnp.zeros((1, QROWS), f32) for g in range(GROUP)]
        outs = [jnp.zeros((HEAD_WIDTH, QROWS), f32) for g in range(GROUP)]
        for chunk in range(max(TAIL_CHUNKS - block, 0), TAIL_CHUNKS + 1):
            row = (block + chunk - TAIL_CHUNKS) * QROWS
            chunk_forward(q_ref, k_ref, v_ref, bounds_ref, block, chunk, row, sums, outs)
        for g in range(GROUP):
            out_ref[head_span(g), here] = outs[g]
            total_ref[g : g + 1, here] = sums[g]


def attend_tail_kernel(
    q_ref, k_ref, v_ref, bounds_ref, part_ref, part_total_ref, out_ref, total_ref
):
    for block in range(q_ref.shape[0] // QROWS):
        here = slice(block * QROWS, (block + 1) * QROWS)
        sums = [part_total_ref[g : g + 1, here] for g in range(GROUP)]
        outs = [part_ref[head_span(g), here] for g in range(GROUP)]
        for chunk in range(0, max(TAIL_CHUNKS - block, 0)):
            row = (block + chunk) * QROWS
            chunk_forward(q_ref, k_ref, v_ref, bounds_ref, block, chunk, row, sums, outs)
        for g in range(GROUP):
            out_ref[here, head_span(g)] = (outs[g] * (1.0 / sums[g])).T.astype(bf16)
            total_ref[g : g + 1, here] = sums[g]


def attend_specs(rows, kv_rows, kv_heads, blocks):
    wide = GROUP * HEAD_WIDTH
    return [
        pl.BlockSpec((rows, wide), lambda j: (0, j)),
        pl.BlockSpec((kv_rows, HEAD_WIDTH), lambda j: (0, j)),
        pl.BlockSpec((kv_rows, HEAD_WIDTH), lambda j: (0, kv_heads + j)),
        pl.BlockSpec((blocks, 8, QROWS), lambda j: (0, 0, 0)),
    ]


def counts(rows, kv_heads):
    blocks = rows // QROWS
    own = sum(min(block, TAIL_CHUNKS) + 1 for block in range(blocks))
    tail = sum(max(TAIL_CHUNKS - block, 0) for block in range(blocks))
    unit = kv_heads * GROUP * QROWS * QROWS
    return own * unit, tail * unit


def attend(queries, kv_own, kv_tail, bounds):
    rows = queries.shape[0]
    kv_heads = kv_own.shape[1] // (2 * HEAD_WIDTH)
    blocks = rows // QROWS
    wide = GROUP * HEAD_WIDTH
    own_pairs, tail_pairs = counts(rows, kv_heads)
    turned_spec = pl.BlockSpec((wide, rows), lambda j: (j, 0))
    total_spec = pl.BlockSpec((None, 8, rows), lambda j: (j, 0, 0))
    turned_shape = shape_of((kv_heads * wide, rows), f32)
    total_shape = shape_of((kv_heads, 8, rows), f32)
    outs, totals = pl.pallas_call(
        attend_own_kernel,
        grid=(kv_heads,),
        in_specs=attend_specs(rows, rows, kv_heads, blocks),
        out_specs=[turned_spec, total_spec],
        out_shape=[turned_shape, total_shape],
        cost_estimate=cost(4 * own_pairs * HEAD_WIDTH, 4 << 20, own_pairs),
        name="attend_own",
    )(queries, kv_own, kv_own, bounds)
    return pl.pallas_call(
        attend_tail_kernel,
        grid=(kv_heads,),
        in_specs=attend_specs(rows, WINDOW_TOKENS, kv_heads, blocks) + [turned_spec, total_spec],
        out_specs=[pl.BlockSpec((rows, wide), lambda j: (0, j)), total_spec],
        out_shape=[shape_of((rows, kv_heads * wide), bf16), total_shape],
        cost_estimate=cost(4 * tail_pairs * HEAD_WIDTH, 4 << 20, tail_pairs),
        name="attend_tail",
    )(queries, kv_tail, kv_tail, bounds, outs, totals)


def chunk_backward(
    q_ref, k_ref, v_ref, bounds_ref, d_out_ref, block, chunk, row, shares, deltas, d_queries
):
    here = slice(block * QROWS, (block + 1) * QROWS)
    there = slice(row, row + QROWS)
    mask = chunk_mask(bounds_ref, block, chunk)
    keys = k_ref[there, :]
    values = v_ref[there, :]
    d_key = None
    d_value = None
    for g in range(GROUP):
        query = q_ref[here, head_span(g)]
        d_out = d_out_ref[here, head_span(g)]
        scores = nt_dot(keys, query)
        probs = jnp.where(mask, jnp.exp2(scores * (score_scale * log2_e)) * shares[g], 0.0)
        d_probs = nt_dot(values, d_out)
        d_scores = (probs * (d_probs - deltas[g]) * score_scale).astype(bf16)
        d_value_now = nn_dot(probs.astype(bf16), d_out)
        d_key_now = nn_dot(d_scores, query)
        d_value = d_value_now if g == 0 else d_value + d_value_now
        d_key = d_key_now if g == 0 else d_key + d_key_now
        d_queries[g] = d_queries[g] + tn_dot(keys, d_scores)
    return d_key, d_value


def attend_back_tail_kernel(
    q_ref, k_ref, v_ref, bounds_ref, total_ref, out_ref, d_out_ref,
    d_q_ref, d_k_ref, d_v_ref, delta_ref, dk_ref, dv_ref
):
    for block in range(q_ref.shape[0] // QROWS):
        here = slice(block * QROWS, (block + 1) * QROWS)
        shares = [1.0 / total_ref[g : g + 1, here] for g in range(GROUP)]
        deltas = []
        for g in range(GROUP):
            product = d_out_ref[here, head_span(g)].astype(f32) * out_ref[
                here, head_span(g)
            ].astype(f32)
            delta = jnp.sum(product.T, axis=0, keepdims=True)
            deltas.append(delta)
            delta_ref[g : g + 1, here] = delta
        d_queries = [jnp.zeros((HEAD_WIDTH, QROWS), f32) for g in range(GROUP)]
        for chunk in range(0, max(TAIL_CHUNKS - block, 0)):
            row = (block + chunk) * QROWS
            there = slice(row, row + QROWS)
            d_key, d_value = chunk_backward(
                q_ref, k_ref, v_ref, bounds_ref, d_out_ref, block, chunk, row,
                shares, deltas, d_queries,
            )
            if block == 0:
                dk_ref[there, :] = d_key
                dv_ref[there, :] = d_value
            else:
                dk_ref[there, :] += d_key
                dv_ref[there, :] += d_value
        for g in range(GROUP):
            d_q_ref[head_span(g), here] = d_queries[g]
    d_k_ref[...] = dk_ref[...].astype(bf16)
    d_v_ref[...] = dv_ref[...].astype(bf16)


def attend_back_own_kernel(
    q_ref, k_ref, v_ref, bounds_ref, total_ref, d_out_ref, d_q_part_ref, delta_ref,
    d_q_ref, d_k_ref, d_v_ref
):
    for block in range(q_ref.shape[0] // QROWS):
        here = slice(block * QROWS, (block + 1) * QROWS)
        shares = [1.0 / total_ref[g : g + 1, here] for g in range(GROUP)]
        deltas = [delta_ref[g : g + 1, here] for g in range(GROUP)]
        d_queries = [d_q_part_ref[head_span(g), here] for g in range(GROUP)]
        for chunk in range(max(TAIL_CHUNKS - block, 0), TAIL_CHUNKS + 1):
            row = (block + chunk - TAIL_CHUNKS) * QROWS
            there = slice(row, row + QROWS)
            d_key, d_value = chunk_backward(
                q_ref, k_ref, v_ref, bounds_ref, d_out_ref, block, chunk, row,
                shares, deltas, d_queries,
            )
            if chunk == TAIL_CHUNKS:
                d_k_ref[there, :] = d_key
                d_v_ref[there, :] = d_value
            else:
                d_k_ref[there, :] += d_key
                d_v_ref[there, :] += d_value
        for g in range(GROUP):
            d_q_ref[here, head_span(g)] = d_queries[g].T.astype(bf16)


def attend_back_tail(queries, kv_tail, bounds, totals, outs, d_outs):
    rows = queries.shape[0]
    kv_heads = kv_tail.shape[1] // (2 * HEAD_WIDTH)
    blocks = rows // QROWS
    wide = GROUP * HEAD_WIDTH
    own_pairs, tail_pairs = counts(rows, kv_heads)
    total_spec = pl.BlockSpec((None, 8, rows), lambda j: (j, 0, 0))
    head_spec = pl.BlockSpec((rows, wide), lambda j: (0, j))
    kv_spec = pl.BlockSpec((WINDOW_TOKENS, HEAD_WIDTH), lambda j: (0, j))
    kv_shape = shape_of((WINDOW_TOKENS, kv_heads * HEAD_WIDTH), bf16)
    return pl.pallas_call(
        attend_back_tail_kernel,
        grid=(kv_heads,),
        in_specs=attend_specs(rows, WINDOW_TOKENS, kv_heads, blocks)
        + [total_spec, head_spec, head_spec],
        out_specs=[pl.BlockSpec((wide, rows), lambda j: (j, 0)), kv_spec, kv_spec, total_spec],
        out_shape=[
            shape_of((kv_heads * wide, rows), f32),
            kv_shape,
            kv_shape,
            shape_of((kv_heads, 8, rows), f32),
        ],
        scratch_shapes=[pltpu.VMEM((WINDOW_TOKENS, HEAD_WIDTH), f32)] * 2,
        cost_estimate=cost(10 * tail_pairs * HEAD_WIDTH, 8 << 20, tail_pairs),
        name="attend_back_tail",
    )(queries, kv_tail, kv_tail, bounds, totals, outs, d_outs)


def attend_back_own(queries, kv_own, bounds, totals, d_outs, d_q_part, deltas):
    rows = queries.shape[0]
    kv_heads = kv_own.shape[1] // (2 * HEAD_WIDTH)
    blocks = rows // QROWS
    wide = GROUP * HEAD_WIDTH
    own_pairs, tail_pairs = counts(rows, kv_heads)
    total_spec = pl.BlockSpec((None, 8, rows), lambda j: (j, 0, 0))
    head_spec = pl.BlockSpec((rows, wide), lambda j: (0, j))
    kv_spec = pl.BlockSpec((rows, HEAD_WIDTH), lambda j: (0, j))
    kv_shape = shape_of((rows, kv_heads * HEAD_WIDTH), f32)
    return pl.pallas_call(
        attend_back_own_kernel,
        grid=(kv_heads,),
        in_specs=attend_specs(rows, rows, kv_heads, blocks)
        + [total_spec, head_spec, pl.BlockSpec((wide, rows), lambda j: (j, 0)), total_spec],
        out_specs=[head_spec, kv_spec, kv_spec],
        out_shape=[shape_of((rows, kv_heads * wide), bf16), kv_shape, kv_shape],
        cost_estimate=cost(10 * own_pairs * HEAD_WIDTH, 8 << 20, own_pairs),
        name="attend_back_own",
    )(queries, kv_own, kv_own, bounds, totals, d_outs, d_q_part, deltas)


def body(
    hidden_in,
    doc_lengths,
    pad_lengths,
    w_query,
    key_matrix,
    value_matrix,
    w_output,
    w_gate,
    w_up,
    w_down,
    attn_gain,
    mlp_gain,
    query_gain,
    key_gain,
    out_grad,
):
    core = lax.axis_index("c")
    group = lax.axis_index("q") * 2 + core
    part = lax.axis_index("seq")
    groups = lax.axis_size("q") * 2
    parts = lax.axis_size("seq")
    tokens, width = hidden_in.shape
    group_rows = tokens * parts
    slice_rows = width // groups
    units = FEEDFWD_UNITS // 2
    q_cols = QUERY_HEADS * HEAD_WIDTH // parts
    kv_cols = KEY_VALUE_HEADS * HEAD_WIDTH // parts
    attn_cols = q_cols + 2 * kv_cols
    pack_cols = attn_cols + q_cols
    w_block = attn_cols // q_cols
    core_at = core.astype(jnp.int32).reshape(1)
    part_at = part.astype(jnp.int32).reshape(1)

    def sent(value, shift):
        return lax.ppermute(value, "seq", [(i, (i + shift) % parts) for i in range(parts)])

    def from_all(value):
        return [value] + [sent(value, shift) for shift in range(1, parts)]

    def to_all(values):
        return [values[0]] + [sent(values[shift], shift) for shift in range(1, parts)]

    gain_cols = jnp.stack(
        [
            attn_gain,
            mlp_gain,
            jnp.pad(query_gain, (0, slice_rows - query_gain.shape[0])),
            jnp.pad(key_gain, (0, slice_rows - key_gain.shape[0])),
        ],
        axis=1,
    )
    gain_cols = jnp.pad(gain_cols, ((0, 0), (0, HEAD_WIDTH - gain_cols.shape[1])))
    packed = pack_attn(
        part_at, parts, w_query, key_matrix, value_matrix, w_output, gain_cols
    )
    attn_w = lax.all_gather(packed, dp_axes, axis=0, tiled=True)

    hidden_blocks = from_all(hidden_in)

    mlp_pack, mlp_give = pack_mlp(core_at, w_gate, w_up, w_down)
    mlp_got = lax.ppermute(mlp_give, "c", core_swap)
    mlp_pack = lax.dynamic_update_slice_in_dim(mlp_pack, mlp_got, (1 - core) * slice_rows, 0)
    mlp_w = lax.all_gather(mlp_pack, "q", axis=0, tiled=True)
    w_gu = mlp_w[:, : 2 * units]
    w_down_t = mlp_w[:, 2 * units :]
    grad_pair = jnp.concatenate([out_grad, lax.ppermute(out_grad, "c", core_swap)], axis=0)

    gains = attn_w[:, pack_cols : pack_cols + 4].astype(f32).T
    head_piece = query_gain.shape[0]
    ga = gains[0:1]
    gm = gains[1:2]
    gqk = gains[2:4].reshape(2, groups, slice_rows)[:, :, :head_piece].reshape(2, HEAD_WIDTH)

    doc_ends = jnp.cumsum(doc_lengths)
    doc_starts = doc_ends - doc_lengths
    pad_starts = doc_ends - pad_lengths
    first = group * group_rows
    token = first + jnp.arange(group_rows, dtype=jnp.int32)
    inside = (token[:, None] >= doc_starts[None, :]) & (token[:, None] < doc_ends[None, :])
    start = jnp.sum(jnp.where(inside, doc_starts[None, :], 0), axis=1)
    pad_start = jnp.sum(jnp.where(inside, pad_starts[None, :], 0), axis=1)
    inv_freq = rope_base ** (-jnp.arange(HEAD_WIDTH // 2, dtype=f32) * 2.0 / HEAD_WIDTH)
    angles = (token - start).astype(f32)[:, None] * inv_freq[None, :]
    cosine = jnp.cos(angles)
    sine = jnp.sin(angles)
    cosine = jnp.concatenate([cosine, cosine], axis=1)
    sine = jnp.concatenate([-sine, sine], axis=1)
    blocks = group_rows // QROWS
    offset = (token // QROWS) * QROWS - WINDOW_TOKENS
    low = jnp.maximum(start, token - (WINDOW_TOKENS - 1)) - offset
    high = jnp.minimum(token, pad_start - 1) - offset
    bounds = jnp.pad(
        jnp.stack([low.reshape(blocks, QROWS), high.reshape(blocks, QROWS)], axis=1),
        ((0, 0), (0, 6), (0, 0)),
    )

    normed_all, queries, kv_own, qk_proj = project(
        part_at, hidden_blocks, attn_w, ga, gqk, cosine, sine, q_cols, kv_cols
    )
    kv_tail = lax.ppermute(
        kv_own[group_rows - WINDOW_TOKENS :], dp_axes, [(i, i + 1) for i in range(groups - 1)]
    )
    attn, totals = attend(queries, kv_own, kv_tail, bounds)
    attn_terms = to_all(out_proj(part_at, parts, attn, attn_w, w_block))
    rows_own = hidden_in.astype(f32)
    middle = rows_own
    for term in attn_terms:
        middle = middle + term.astype(f32)
    mid_stats = norm_stats(middle)
    normed_mid = (middle * mid_stats * gm).astype(bf16)

    mid_pair = jnp.concatenate([normed_mid, lax.ppermute(normed_mid, "c", core_swap)], axis=0)
    gate_up = nn_dot(mid_pair, w_gu)
    gate = gate_up[:, :units]
    up = gate_up[:, units:]
    sig = 1.0 / (1.0 + jnp.exp(-gate))
    mixed = (gate * sig * up).astype(bf16)
    d_mixed = nn_dot(grad_pair, w_down_t)
    d_gate = (d_mixed * up * sig * (1.0 + gate * (1.0 - sig))).astype(bf16)
    d_up = (d_mixed * gate * sig).astype(bf16)
    d_gate_up = jnp.concatenate([d_gate, d_up], axis=1)
    d_mid_part = nt_dot(d_gate_up, w_gu)
    d_mid_other = lax.ppermute(d_mid_part[tokens:].astype(bf16), "c", core_swap)
    d_normed_mid = d_mid_part[:tokens] + d_mid_other.astype(f32)
    d_middle = out_grad.astype(f32) + norm_back(d_normed_mid, middle, mid_stats, gm)
    d_mlp_gain = jnp.sum(d_normed_mid * middle * mid_stats, axis=0)
    d_proj_blocks = from_all(d_middle.astype(bf16))

    out_part = nt_dot(mixed, w_down_t)
    out_other = lax.ppermute(out_part[tokens:].astype(bf16), "c", core_swap)
    output_act = (middle + out_part[:tokens] + out_other.astype(f32)).astype(bf16)

    mlp_grad = jnp.concatenate(
        [tn_dot(mid_pair, d_gate_up), tn_dot(grad_pair, mixed)], axis=1
    ).astype(bf16)
    mlp_grad = lax.psum_scatter(mlp_grad, "q", scatter_dimension=0, tiled=True)
    mlp_grad = lax.psum(mlp_grad, "seq")
    grad_give = lax.dynamic_slice_in_dim(mlp_grad, (1 - core) * slice_rows, slice_rows, 0)
    grad_got = lax.ppermute(grad_give, "c", core_swap)
    grad_gate, grad_up, grad_down = unpack_mlp(core_at, mlp_grad, grad_got)

    d_attn, w_out_grad = out_proj_back(part_at, d_proj_blocks, attn, attn_w, w_block)
    d_q_part, d_k_tail, d_v_tail, deltas = attend_back_tail(
        queries, kv_tail, bounds, totals, attn, d_attn
    )
    d_kv_tail = lax.ppermute(
        jnp.concatenate([d_k_tail, d_v_tail], axis=1),
        dp_axes,
        [(i + 1, i) for i in range(groups - 1)],
    )
    d_queries, d_k, d_v = attend_back_own(
        queries, kv_own, bounds, totals, d_attn, d_q_part, deltas
    )
    *d_in_terms, d_qkv, attn_gain_rows, head_gain_rows = project_back(
        part_at, [hidden_blocks[(parts - k) % parts] for k in range(parts)], d_queries,
        jnp.concatenate([d_k, d_v], axis=1), d_kv_tail, qk_proj, attn_w, gqk, cosine, sine,
    )
    d_normed_in = jnp.zeros((tokens, width), f32)
    for term in to_all(d_in_terms):
        d_normed_in = d_normed_in + term.astype(f32)
    in_grad = (d_middle + norm_back(d_normed_in, rows_own, norm_stats(rows_own), ga)).astype(bf16)

    def spread(head_gain):
        return jnp.pad(
            head_gain.reshape(groups, head_piece), ((0, 0), (0, slice_rows - head_piece))
        ).reshape(width)

    gain_grads = jnp.stack(
        [attn_gain_rows[0], d_mlp_gain, spread(head_gain_rows[0]), spread(head_gain_rows[1])],
        axis=1,
    )
    attn_grad = jnp.concatenate(
        [
            tn_dot(normed_all, d_qkv),
            w_out_grad,
            jnp.pad(gain_grads, ((0, 0), (0, HEAD_WIDTH - gain_grads.shape[1]))),
        ],
        axis=1,
    ).astype(bf16)
    by_core = attn_grad.reshape(groups // 2, 2, slice_rows, -1)
    keep = lax.dynamic_index_in_dim(by_core, core, 1, keepdims=False)
    give = lax.dynamic_index_in_dim(by_core, 1 - core, 1, keepdims=False)
    chip_sum = keep.astype(f32) + lax.ppermute(give, "c", core_swap).astype(f32)
    chip_sum = chip_sum.astype(bf16).reshape(width // 2, -1)
    attn_grad = lax.psum_scatter(chip_sum, "q", scatter_dimension=0, tiled=True)
    attn_grad = lax.all_gather(attn_grad, "seq", axis=0)
    gain_sums = jnp.sum(attn_grad[:, :, pack_cols : pack_cols + 4].astype(f32), axis=0)
    grad_query, grad_key, grad_value, grad_output = unpack_attn(attn_grad, q_cols, kv_cols)
    return (
        output_act,
        in_grad,
        grad_query,
        grad_key,
        grad_value,
        grad_output,
        grad_gate,
        grad_up,
        grad_down,
        gain_sums[:, 0],
        gain_sums[:, 1],
        gain_sums[:head_piece, 2],
        gain_sums[:head_piece, 3],
    )


def solution(mesh):
    groups, parts = mesh.devices.shape
    mesh = Mesh(mesh.devices.reshape(groups // 2, 2, parts), ("q", "c", "seq"))
    tokens = P(("q", "c", "seq"), None)
    rows = P(dp_axes, None)
    cols = P(None, dp_axes)
    flat = P(dp_axes)
    in_specs = (
        tokens, P(), P(), rows, rows, rows, cols, rows, rows, cols, flat, flat, flat, flat, tokens,
    )
    out_specs = (
        tokens, tokens, rows, rows, rows, cols, rows, rows, cols, flat, flat, flat, flat,
    )
    return jax.shard_map(body, mesh=mesh, in_specs=in_specs, out_specs=out_specs, check_vma=False)
```

```python
import functools

import jax
import jax.numpy as jnp
from jax import lax
from jax.experimental import pallas as pl
from jax.experimental.pallas import tpu as pltpu
from jax.sharding import Mesh, PartitionSpec as P

QUERY_HEADS = 16
KEY_VALUE_HEADS = 8
HEAD_WIDTH = 128
FEEDFWD_UNITS = 3072
WINDOW_TOKENS = 1024
QROWS = 256
GROUP = QUERY_HEADS // KEY_VALUE_HEADS
TAIL_CHUNKS = WINDOW_TOKENS // QROWS

norm_eps = 1e-06
rope_base = 1000000.0
score_scale = HEAD_WIDTH**-0.5
log2_e = 1.4426950408889634
bf16 = jnp.bfloat16
f32 = jnp.float32
dp_axes = ("q", "c")
core_swap = [(0, 1), (1, 0)]


def nt_dot(left, right):
    return lax.dot_general(left, right, (((1,), (1,)), ((), ())), preferred_element_type=f32)


def tn_dot(left, right):
    return lax.dot_general(left, right, (((0,), (0,)), ((), ())), preferred_element_type=f32)


def nn_dot(left, right):
    return jnp.dot(left, right, preferred_element_type=f32)


def shape_of(dims, kind):
    return jax.ShapeDtypeStruct(dims, kind)


def call(
    kernel, args, *, grid, in_specs, out_specs, out_shape, name, estimate, prefetch=0, scratch=(),
    mib=32, after=()
):
    count = prefetch + len(in_specs)

    def body_of(*refs):
        kernel(*refs[:count], *refs[count + len(after) :])

    return pl.pallas_call(
        body_of,
        grid_spec=pltpu.PrefetchScalarGridSpec(
            num_scalar_prefetch=prefetch,
            grid=grid,
            in_specs=list(in_specs) + [pl.BlockSpec(memory_space=pl.ANY)] * len(after),
            out_specs=out_specs,
            scratch_shapes=list(scratch),
        ),
        out_shape=out_shape,
        compiler_params=pltpu.CompilerParams(vmem_limit_bytes=mib << 20),
        cost_estimate=estimate,
        name=name,
    )(*args, *after)


def cost(flops, moved, exps=0, scale=100):
    flops, moved, exps = flops * scale, moved * scale, exps * scale
    return pl.CostEstimate(flops=int(flops), bytes_accessed=int(moved), transcendentals=int(exps))


def norm_stats(rows):
    return lax.rsqrt(jnp.mean(rows * rows, axis=-1, keepdims=True) + norm_eps)


def norm_back(d_normed, rows, stats, gains):
    scaled = d_normed * gains
    unit = rows * stats
    return stats * (scaled - unit * jnp.mean(scaled * unit, axis=-1, keepdims=True))


def pack_attn_kernel(
    part_ref, wq_ref, wk_ref, wv_ref, wo_ref, ga_ref, gm_ref, gq_ref, gk_ref, out_ref, gains_ref
):
    gains_ref[...] = jnp.zeros_like(gains_ref)
    for row, gain_ref in enumerate((ga_ref, gm_ref, gq_ref, gk_ref)):
        gains_ref[row : row + 1, : gain_ref.shape[1]] = gain_ref[...]
    column = 0
    for piece in (
        wq_ref[...].astype(bf16),
        wk_ref[...].astype(bf16),
        wv_ref[...].astype(bf16),
        wo_ref[...].T.astype(bf16),
    ):
        out_ref[:, column : column + piece.shape[1]] = piece
        column += piece.shape[1]
    gains = gains_ref[...].T
    rest = jnp.zeros((gains.shape[0], HEAD_WIDTH - gains.shape[1]), f32)
    out_ref[:, column:] = jnp.concatenate([gains, rest], axis=1).astype(bf16)


def pack_attn(part, parts, w_query, key_matrix, value_matrix, w_output, gains, after=()):
    gains = [gain[None] for gain in gains]
    rows = w_query.shape[0]
    q_cols = w_query.shape[1] // parts
    kv_cols = key_matrix.shape[1] // parts
    total = 2 * q_cols + 2 * kv_cols + HEAD_WIDTH
    return call(
        pack_attn_kernel,
        (part, w_query, key_matrix, value_matrix, w_output, *gains),
        prefetch=1,
        grid=(1,),
        in_specs=[
            pl.BlockSpec((rows, q_cols), lambda i, p: (0, p[0])),
            pl.BlockSpec((rows, kv_cols), lambda i, p: (0, p[0])),
            pl.BlockSpec((rows, kv_cols), lambda i, p: (0, p[0])),
            pl.BlockSpec((q_cols, rows), lambda i, p: (p[0], 0)),
        ]
        + [pl.BlockSpec(gain.shape, lambda i, p: (0, 0)) for gain in gains],
        scratch=[pltpu.VMEM((8, rows), f32)],
        mib=60,
        out_specs=pl.BlockSpec((rows, total), lambda i, p: (0, 0)),
        out_shape=shape_of((rows, total), bf16),
        estimate=cost(0, rows * total * 6),
        name="pack_attn",
        after=after,
    )


def add_kernel(left_ref, right_ref, out_ref):
    out_ref[...] = (left_ref[...].astype(f32) + right_ref[...].astype(f32)).astype(bf16)


def add(left, right, after=()):
    rows, cols = left.shape
    spec = pl.BlockSpec((rows // 4, cols), lambda i: (i, 0))
    return call(
        add_kernel,
        (left, right),
        grid=(4,),
        in_specs=[spec, spec],
        out_specs=spec,
        out_shape=shape_of((rows, cols), bf16),
        estimate=cost(rows * cols, 6 * rows * cols),
        name="add",
        after=after,
    )


def touch_kernel(in_ref, out_ref):
    out_ref[...] = in_ref[...]


def touch(value, after):
    rows, cols = value.shape
    spec = pl.BlockSpec((rows // 4, cols), lambda i: (i, 0))
    return call(
        touch_kernel,
        (value,),
        grid=(4,),
        in_specs=[spec],
        out_specs=spec,
        out_shape=shape_of((rows, cols), value.dtype),
        estimate=cost(0, 4 * rows * cols),
        name="touch",
        after=after,
    )


def sum_kernel(*refs):
    total = refs[0][...].astype(f32)
    for ref in refs[1:-1]:
        total = total + ref[...].astype(f32)
    refs[-1][...] = total.astype(bf16)


def sum_all(terms, after=()):
    rows, cols = terms[0].shape
    steps = 4 if rows % 64 == 0 else 1
    spec = pl.BlockSpec((rows // steps, cols), lambda i: (i, 0))
    return call(
        sum_kernel,
        tuple(terms),
        grid=(steps,),
        in_specs=[spec] * len(terms),
        out_specs=spec,
        out_shape=shape_of((rows, cols), bf16),
        estimate=cost(len(terms) * rows * cols, 2 * (len(terms) + 1) * rows * cols),
        name="sum_all",
        after=after,
    )


def finish_in_kernel(d_normed_ref, d_middle_ref, x_ref, gain_ref, out_ref):
    rows = x_ref[...].astype(f32)
    back = norm_back(d_normed_ref[...].astype(f32), rows, norm_stats(rows), gain_ref[...])
    out_ref[...] = (d_middle_ref[...] + back).astype(bf16)


def finish_in(d_normed, d_middle, hidden, gain, after=()):
    rows, cols = hidden.shape
    spec = pl.BlockSpec((rows // 4, cols), lambda i: (i, 0))
    return call(
        finish_in_kernel,
        (d_normed, d_middle, hidden, gain),
        grid=(4,),
        in_specs=[spec] * 3 + [pl.BlockSpec((1, cols), lambda i: (0, 0))],
        out_specs=spec,
        out_shape=shape_of((rows, cols), bf16),
        estimate=cost(20 * rows * cols, 12 * rows * cols, scale=1),
        name="finish_in",
        after=after,
    )


def sum_blocks_kernel(in_ref, out_ref):
    total = in_ref[0].astype(f32)
    for index in range(1, in_ref.shape[0]):
        total = total + in_ref[index].astype(f32)
    out_ref[...] = total.astype(bf16)


def sum_blocks(stacked, after=()):
    count, rows, cols = stacked.shape
    return call(
        sum_blocks_kernel,
        (stacked,),
        grid=(4,),
        in_specs=[pl.BlockSpec((count, rows // 4, cols), lambda i: (0, i, 0))],
        out_specs=pl.BlockSpec((rows // 4, cols), lambda i: (i, 0)),
        out_shape=shape_of((rows, cols), bf16),
        estimate=cost(count * rows * cols, 2 * (count + 1) * rows * cols),
        name="sum_blocks",
        after=after,
    )


def read_gains_kernel(in_ref, out_ref):
    out_ref[...] = in_ref[...].astype(f32).T[:8, :]


def read_gains(attn_w, column, after=()):
    width = attn_w.shape[0]
    return call(
        read_gains_kernel,
        (attn_w,),
        grid=(1,),
        in_specs=[pl.BlockSpec((width, HEAD_WIDTH), lambda i: (0, column // HEAD_WIDTH))],
        out_specs=pl.BlockSpec((8, width), lambda i: (0, 0)),
        out_shape=shape_of((8, width), f32),
        estimate=cost(0, width * HEAD_WIDTH * 4),
        name="read_gains",
        after=after,
    )


def pack_mlp_kernel(core_ref, wg_ref, wu_ref, wd_ref, own_ref, give_ref):
    units = wg_ref.shape[1]

    def fill(out_ref):
        out_ref[:, :units] = wg_ref[...].astype(bf16)
        out_ref[:, units : 2 * units] = wu_ref[...].astype(bf16)
        out_ref[:, 2 * units :] = wd_ref[...].T.astype(bf16)

    @pl.when(pl.program_id(0) == 0)
    def first():
        fill(give_ref)

    @pl.when(pl.program_id(0) == 1)
    def second():
        fill(own_ref)


def pack_mlp(core, w_gate, w_up, w_down, after=()):
    rows = w_gate.shape[0]
    units = w_gate.shape[1] // 2
    half = lambda i, c: (c[0] + 1 - i) % 2
    return call(
        pack_mlp_kernel,
        (core, w_gate, w_up, w_down,),
        prefetch=1,
        grid=(2,),
        in_specs=[
            pl.BlockSpec((rows, units), lambda i, c: (0, half(i, c))),
            pl.BlockSpec((rows, units), lambda i, c: (0, half(i, c))),
            pl.BlockSpec((units, rows), lambda i, c: (half(i, c), 0)),
        ],
        out_specs=[
            pl.BlockSpec((rows, 3 * units), lambda i, c: (c[0], 0)),
            pl.BlockSpec((rows, 3 * units), lambda i, c: (0, 0)),
        ],
        out_shape=[shape_of((2 * rows, 3 * units), bf16), shape_of((rows, 3 * units), bf16)],
        estimate=cost(0, rows * units * 36),
        name="pack_mlp",
        after=after,
    )


def unpack_half_kernel(turned, core_ref, own_ref, got_ref, out_ref):
    def fill(in_ref):
        rows = in_ref[...].astype(f32)
        out_ref[...] = rows.T if turned else rows

    @pl.when(pl.program_id(0) == 0)
    def first():
        fill(own_ref)

    @pl.when(pl.program_id(0) == 1)
    def second():
        fill(got_ref)


def unpack_half(core, sums, got, column, turned, after=()):
    rows, units = got.shape
    half = lambda i, c: (c[0] + i) % 2
    if turned:
        out_spec = pl.BlockSpec((units, rows), lambda i, c: (half(i, c), 0))
        out_shape = shape_of((2 * units, rows), f32)
    else:
        out_spec = pl.BlockSpec((rows, units), lambda i, c: (0, half(i, c)))
        out_shape = shape_of((rows, 2 * units), f32)
    return call(
        functools.partial(unpack_half_kernel, turned),
        (core, sums, got,),
        prefetch=1,
        grid=(2,),
        in_specs=[
            pl.BlockSpec((rows, units), lambda i, c: (c[0], column)),
            pl.BlockSpec((rows, units), lambda i, c: (0, 0)),
        ],
        out_specs=out_spec,
        out_shape=out_shape,
        estimate=cost(0, rows * units * 12, scale=1),
        name="unpack_half",
        after=after,
    )


def unpack_attn_kernel(in_ref, wq_ref, wk_ref, wv_ref, wo_ref):
    column = 0
    for out_ref in (wq_ref, wk_ref, wv_ref):
        count = out_ref.shape[1]
        out_ref[...] = in_ref[:, column : column + count].astype(f32)
        column += count
    wo_ref[...] = in_ref[:, column : column + wo_ref.shape[0]].astype(f32).T


def unpack_attn(gathered, q_cols, kv_cols, after=()):
    parts, rows, total = gathered.shape
    return call(
        unpack_attn_kernel,
        (gathered,),
        grid=(parts,),
        in_specs=[pl.BlockSpec((None, rows, total), lambda i: (i, 0, 0))],
        out_specs=[
            pl.BlockSpec((rows, q_cols), lambda i: (0, i)),
            pl.BlockSpec((rows, kv_cols), lambda i: (0, i)),
            pl.BlockSpec((rows, kv_cols), lambda i: (0, i)),
            pl.BlockSpec((q_cols, rows), lambda i: (i, 0)),
        ],
        out_shape=[
            shape_of((rows, parts * q_cols), f32),
            shape_of((rows, parts * kv_cols), f32),
            shape_of((rows, parts * kv_cols), f32),
            shape_of((parts * q_cols, rows), f32),
        ],
        estimate=cost(0, parts * rows * total * 6, scale=1),
        name="unpack_attn",
        after=after,
    )


def pick(refs, scratch):
    for k, ref in enumerate(refs):

        @pl.when(pl.program_id(0) == k)
        def take(ref=ref):
            scratch[...] = ref[...]


def turn(rows):
    half = HEAD_WIDTH // 2
    return jnp.concatenate([rows[:, half:], rows[:, :half]], axis=1)


def project_kernel(parts, q_cols, kv_cols, part_ref, *refs):
    blocks = refs[:parts]
    w_ref, ga_ref, gqk_ref, cos_ref, sin_ref, normed_ref, q_ref, kv_ref, proj_ref, x_ref = refs[parts:]
    pick(blocks, x_ref)
    rows = x_ref[...].astype(f32)
    normed = (rows * norm_stats(rows) * ga_ref[...]).astype(bf16)
    normed_ref[...] = normed
    cosine = cos_ref[...]
    sine = sin_ref[...]
    qk_cols = q_cols + kv_cols
    proj = nn_dot(normed, w_ref[...])
    proj_ref[...] = proj[:, :qk_cols]
    kv_ref[:, kv_cols:] = proj[:, qk_cols:].astype(bf16)
    for column in range(0, qk_cols, HEAD_WIDTH):
        head = proj[:, column : column + HEAD_WIDTH]
        gain = gqk_ref[0:1, :] if column < q_cols else gqk_ref[1:2, :]
        head = head * norm_stats(head) * gain
        head = (head * cosine + turn(head) * sine).astype(bf16)
        if column < q_cols:
            q_ref[:, column : column + HEAD_WIDTH] = head
        else:
            kv_ref[:, column - q_cols : column - q_cols + HEAD_WIDTH] = head


def project(part, blocks, attn_w, ga, gqk, cosine, sine, q_cols, kv_cols, after=()):
    parts = len(blocks)
    tokens, width = blocks[0].shape
    attn_cols = q_cols + 2 * kv_cols
    place = lambda k, p: ((p[0] + parts - k) % parts, 0)
    fixed = lambda k, p: (0, 0)
    rows = parts * tokens
    return call(
        functools.partial(project_kernel, parts, q_cols, kv_cols),
        (part, *blocks, attn_w, ga, gqk, cosine, sine,),
        prefetch=1,
        grid=(parts,),
        in_specs=[pl.BlockSpec((tokens, width), fixed)] * parts
        + [
            pl.BlockSpec((width, attn_cols), fixed),
            pl.BlockSpec((1, width), fixed),
            pl.BlockSpec((2, HEAD_WIDTH), fixed),
            pl.BlockSpec((tokens, HEAD_WIDTH), place),
            pl.BlockSpec((tokens, HEAD_WIDTH), place),
        ],
        out_specs=[
            pl.BlockSpec((tokens, width), place),
            pl.BlockSpec((tokens, q_cols), place),
            pl.BlockSpec((tokens, 2 * kv_cols), place),
            pl.BlockSpec((tokens, q_cols + kv_cols), place),
        ],
        scratch=[pltpu.VMEM((tokens, width), bf16)],
        out_shape=[
            shape_of((rows, width), bf16),
            shape_of((rows, q_cols), bf16),
            shape_of((rows, 2 * kv_cols), bf16),
            shape_of((rows, q_cols + kv_cols), f32),
        ],
        mib=32,
        estimate=cost(2 * rows * width * attn_cols, 12 << 20),
        name="project",
        after=after,
    )


def project_back_kernel(
    parts, groups, tail_from, q_cols, kv_cols, part_ref, *refs
):
    blocks = refs[:parts]
    (dq_ref, d_kv_ref, tail_ref, proj_ref, w_ref, gqk_ref, cos_ref, sin_ref, normed_ref,
     w_out_ref, mlp_gain_ref, out_ref, term_ref,
     x_ref, dqkv_ref, acc_ref, gain_ref, head_gain_ref) = refs[parts:]
    step = pl.program_id(0)
    block = (part_ref[0] + step) % parts
    pick(blocks, x_ref)

    @pl.when(step == 0)
    def clear():
        gain_ref[...] = jnp.zeros_like(gain_ref)
        head_gain_ref[...] = jnp.zeros_like(head_gain_ref)
        acc_ref[...] = jnp.zeros_like(acc_ref)

    cosine = cos_ref[...]
    sine = sin_ref[...]
    has_tail = jnp.where(block >= tail_from, 1.0, 0.0)
    dk = (d_kv_ref[0] + tail_ref[0].astype(f32) * has_tail).astype(bf16)
    dqkv_ref[:, q_cols + kv_cols :] = (
        d_kv_ref[1] + tail_ref[1].astype(f32) * has_tail
    ).astype(bf16)
    head_gains = [jnp.zeros((1, HEAD_WIDTH), f32) for _ in range(2)]
    for column in range(0, q_cols + kv_cols, HEAD_WIDTH):
        index = 0 if column < q_cols else 1
        if index == 0:
            d_head = dq_ref[:, column : column + HEAD_WIDTH].astype(f32)
        else:
            d_head = dk[:, column - q_cols : column - q_cols + HEAD_WIDTH].astype(f32)
        d_head = d_head * cosine + turn(d_head * sine)
        head = proj_ref[:, column : column + HEAD_WIDTH]
        stats = norm_stats(head)
        unit = head * stats
        head_gains[index] = head_gains[index] + jnp.sum(d_head * unit, axis=0, keepdims=True)
        scaled = d_head * gqk_ref[index : index + 1, :]
        d_proj = stats * (scaled - unit * jnp.mean(scaled * unit, axis=-1, keepdims=True))
        dqkv_ref[:, column : column + HEAD_WIDTH] = d_proj.astype(bf16)
    head_gain_ref[0:1, :] += head_gains[0]
    head_gain_ref[1:2, :] += head_gains[1]
    d_in = nt_dot(dqkv_ref[...], w_ref[...])
    rows = x_ref[...].astype(f32)
    gain_ref[0:1, :] += jnp.sum(d_in * (rows * norm_stats(rows)), axis=0, keepdims=True)
    out_ref[...] = d_in.astype(bf16)
    acc_ref[...] += tn_dot(normed_ref[...], dqkv_ref[...])

    @pl.when(step == parts - 1)
    def finish():
        attn_cols = acc_ref.shape[1]
        term_ref[:, :attn_cols] = acc_ref[...].astype(bf16)
        term_ref[:, attn_cols : attn_cols + q_cols] = w_out_ref[...]
        gain_ref[1:2, :] = mlp_gain_ref[0:1, :]
        piece = HEAD_WIDTH // groups
        slice_rows = gain_ref.shape[1] // groups
        for index in range(2):
            for group in range(groups):
                gain_ref[2 + index : 3 + index, group * slice_rows : group * slice_rows + piece] = (
                    head_gain_ref[index : index + 1, group * piece : (group + 1) * piece]
                )
        gains = gain_ref[...].T
        rest = jnp.zeros((gains.shape[0], HEAD_WIDTH - gains.shape[1]), f32)
        term_ref[:, attn_cols + q_cols :] = jnp.concatenate([gains, rest], axis=1).astype(bf16)


def project_back(
    part, groups, hidden, dq, d_kv, tail, proj, attn_w, gqk, cosine, sine, normed,
    w_out_grad, mlp_gain_rows, after=()
):
    parts = len(hidden)
    tokens, width = hidden[0].shape
    rows, q_cols = dq.shape
    kv_cols = d_kv.shape[2]
    attn_cols = q_cols + 2 * kv_cols
    tail_from = (rows - WINDOW_TOKENS) // tokens
    place = lambda k, p: ((p[0] + k) % parts, 0)
    kv_place = lambda k, p: (0, (p[0] + k) % parts, 0)
    tail_place = lambda k, p: (0, jnp.maximum((p[0] + k) % parts - tail_from, 0), 0)
    fixed = lambda k, p: (0, 0)
    total = attn_cols + q_cols + HEAD_WIDTH
    return call(
        functools.partial(project_back_kernel, parts, groups, tail_from, q_cols, kv_cols),
        (part, *hidden, dq, d_kv, tail, proj, attn_w, gqk, cosine, sine, normed, w_out_grad, mlp_gain_rows),
        prefetch=1,
        grid=(parts,),
        in_specs=[pl.BlockSpec((tokens, width), fixed)] * parts
        + [
            pl.BlockSpec((tokens, q_cols), place),
            pl.BlockSpec((2, tokens, kv_cols), kv_place),
            pl.BlockSpec((2, tokens, kv_cols), tail_place),
            pl.BlockSpec((tokens, q_cols + kv_cols), place),
            pl.BlockSpec((width, attn_cols), fixed),
            pl.BlockSpec((2, HEAD_WIDTH), fixed),
            pl.BlockSpec((tokens, HEAD_WIDTH), place),
            pl.BlockSpec((tokens, HEAD_WIDTH), place),
            pl.BlockSpec((tokens, width), place),
            pl.BlockSpec((width, q_cols), fixed),
            pl.BlockSpec((8, width), fixed),
        ],
        out_specs=[
            pl.BlockSpec((tokens, width), place),
            pl.BlockSpec((width, total), fixed),
        ],
        scratch=[
            pltpu.VMEM((tokens, width), bf16),
            pltpu.VMEM((tokens, attn_cols), bf16),
            pltpu.VMEM((width, attn_cols), f32),
            pltpu.VMEM((8, width), f32),
            pltpu.VMEM((8, HEAD_WIDTH), f32),
        ],
        mib=48,
        out_shape=[
            shape_of((rows, width), bf16),
            shape_of((width, total), bf16),
        ],
        estimate=cost(4 * rows * width * attn_cols, 16 << 20, scale=1),
        name="project_back",
        after=after,
    )


def out_grad_kernel(parts, *refs):
    d_projs = refs[:parts]
    attns = refs[parts : 2 * parts]
    out_ref = refs[2 * parts]
    total = None
    for d_proj, attn in zip(d_projs, attns):
        term = tn_dot(d_proj[...], attn[...])
        total = term if total is None else total + term
    out_ref[...] = total.astype(bf16)


def out_grad_sums(d_projs, attns, after=()):
    parts = len(attns)
    tokens, q_cols = attns[0].shape
    width = d_projs[0].shape[1]
    cols = width // 4
    return call(
        functools.partial(out_grad_kernel, parts),
        (*d_projs, *attns,),
        grid=(4,),
        in_specs=[pl.BlockSpec((tokens, cols), lambda i: (0, i))] * parts
        + [pl.BlockSpec((tokens, q_cols), lambda i: (0, 0))] * parts,
        out_specs=pl.BlockSpec((cols, q_cols), lambda i: (i, 0)),
        out_shape=shape_of((width, q_cols), bf16),
        mib=32,
        estimate=cost(2 * parts * tokens * width * q_cols, 4 << 20, scale=1),
        name="out_grad",
        after=after,
    )


def chunk_mask(low, high, chunk):
    key = lax.broadcasted_iota(jnp.int32, (QROWS, QROWS), 0) + chunk * QROWS
    mask = (key >= low) & (key <= high)
    if chunk == TAIL_CHUNKS:
        own = lax.broadcasted_iota(jnp.int32, (QROWS, QROWS), 1) + WINDOW_TOKENS
        mask = mask | (key == own)
    return mask


def head_span(g):
    return slice(g * HEAD_WIDTH, (g + 1) * HEAD_WIDTH)


def attend_own_kernel(q_ref, k_ref, v_ref, bounds_ref, out_ref, total_ref):
    for block in range(q_ref.shape[0] // QROWS):
        here = slice(block * QROWS, (block + 1) * QROWS)
        sums = [jnp.zeros((1, QROWS), f32) for g in range(GROUP)]
        outs = [jnp.zeros((HEAD_WIDTH, QROWS), f32) for g in range(GROUP)]
        for chunk in range(max(TAIL_CHUNKS - block, 0), TAIL_CHUNKS + 1):
            row = (block + chunk - TAIL_CHUNKS) * QROWS
            there = slice(row, row + QROWS)
            mask = chunk_mask(bounds_ref[block, 0:1, :], bounds_ref[block, 1:2, :], chunk)
            for g in range(GROUP):
                scores = nt_dot(k_ref[there, :], q_ref[here, head_span(g)])
                weights = jnp.where(mask, jnp.exp2(scores * (score_scale * log2_e)), 0.0)
                sums[g] = sums[g] + jnp.sum(weights, axis=0, keepdims=True)
                outs[g] = outs[g] + tn_dot(v_ref[there, :], weights.astype(bf16))
        for g in range(GROUP):
            out_ref[head_span(g), here] = outs[g]
            total_ref[g : g + 1, here] = sums[g]


def chunk_pairs(chunks, kv_heads):
    return chunks * kv_heads * GROUP * QROWS * QROWS


def attend_own(queries, kv_own, bounds, after=()):
    rows = queries.shape[0]
    kv_heads = kv_own.shape[1] // (2 * HEAD_WIDTH)
    blocks = rows // QROWS
    wide = GROUP * HEAD_WIDTH
    pairs = chunk_pairs(sum(min(b, TAIL_CHUNKS) + 1 for b in range(blocks)), kv_heads)
    return call(
        attend_own_kernel,
        (queries, kv_own, kv_own, bounds,),
        grid=(kv_heads,),
        in_specs=[
            pl.BlockSpec((rows, wide), lambda j: (0, j)),
            pl.BlockSpec((rows, HEAD_WIDTH), lambda j: (0, j)),
            pl.BlockSpec((rows, HEAD_WIDTH), lambda j: (0, kv_heads + j)),
            pl.BlockSpec((blocks, 8, QROWS), lambda j: (0, 0, 0)),
        ],
        out_specs=[
            pl.BlockSpec((wide, rows), lambda j: (j, 0)),
            pl.BlockSpec((None, 8, rows), lambda j: (j, 0, 0)),
        ],
        out_shape=[shape_of((kv_heads * wide, rows), f32), shape_of((kv_heads, 8, rows), f32)],
        mib=32,
        estimate=cost(4 * pairs * HEAD_WIDTH, 4 << 20, pairs),
        name="attend_own",
        after=after,
    )


def attend_tail_kernel(
    shift, parts, part_ref, q_ref, k_ref, v_ref, bounds_ref, own_ref, own_total_ref, w_ref,
    attn_ref, total_ref, proj_ref, out_ref, acc_ref
):
    block = (part_ref[0] + shift) % parts
    out_ref[...] = own_ref[...]
    total_ref[...] = own_total_ref[...]
    for chunk in range(TAIL_CHUNKS):

        @pl.when(block + chunk < TAIL_CHUNKS)
        def add(chunk=chunk):
            there = pl.ds(pl.multiple_of((block + chunk) * QROWS, QROWS), QROWS)
            keys = k_ref[there, :]
            values = v_ref[there, :]
            mask = chunk_mask(bounds_ref[0:1, :], bounds_ref[1:2, :], chunk)
            for g in range(GROUP):
                scores = nt_dot(keys, q_ref[:, head_span(g)])
                weights = jnp.where(mask, jnp.exp2(scores * (score_scale * log2_e)), 0.0)
                total_ref[g : g + 1, :] += jnp.sum(weights, axis=0, keepdims=True)
                out_ref[head_span(g), :] += tn_dot(values, weights.astype(bf16))

    for g in range(GROUP):
        share = 1.0 / total_ref[g : g + 1, :]
        attn_ref[:, head_span(g)] = (out_ref[head_span(g), :] * share).T.astype(bf16)
    term = nt_dot(attn_ref[...], w_ref[...])
    last = pl.num_programs(0) - 1

    @pl.when(pl.program_id(0) == 0)
    def start():
        acc_ref[...] = term

    @pl.when(pl.program_id(0) > 0)
    def add_up():
        acc_ref[...] += term

    @pl.when(pl.program_id(0) == last)
    def finish():
        proj_ref[...] = acc_ref[...].astype(bf16)


def attend_tail(shift, part, parts, queries, kv_tail, bounds, outs, totals, attn_w, attn_cols, after=()):
    q_cols = queries.shape[1]
    width = attn_w.shape[0]
    kv_heads = kv_tail.shape[1] // (2 * HEAD_WIDTH)
    wide = GROUP * HEAD_WIDTH
    at = lambda p: (p[0] + shift) % parts
    pairs = chunk_pairs(TAIL_CHUNKS // 2, kv_heads)
    return call(
        functools.partial(attend_tail_kernel, shift, parts),
        (part, queries, kv_tail, kv_tail, bounds, outs, totals, attn_w,),
        prefetch=1,
        grid=(kv_heads,),
        in_specs=[
            pl.BlockSpec((QROWS, wide), lambda j, p: (at(p), j)),
            pl.BlockSpec((WINDOW_TOKENS, HEAD_WIDTH), lambda j, p: (0, j)),
            pl.BlockSpec((WINDOW_TOKENS, HEAD_WIDTH), lambda j, p: (0, kv_heads + j)),
            pl.BlockSpec((None, 8, QROWS), lambda j, p: (at(p), 0, 0)),
            pl.BlockSpec((wide, QROWS), lambda j, p: (j, at(p))),
            pl.BlockSpec((None, 8, QROWS), lambda j, p: (j, 0, at(p))),
            pl.BlockSpec((width, wide), lambda j, p: (0, attn_cols // wide + j)),
        ],
        out_specs=[
            pl.BlockSpec((QROWS, wide), lambda j, p: (0, j)),
            pl.BlockSpec((None, 8, QROWS), lambda j, p: (j, 0, 0)),
            pl.BlockSpec((QROWS, width), lambda j, p: (0, 0)),
        ],
        scratch=[pltpu.VMEM((wide, QROWS), f32), pltpu.VMEM((QROWS, width), f32)],
        out_shape=[
            shape_of((QROWS, q_cols), bf16),
            shape_of((kv_heads, 8, QROWS), f32),
            shape_of((QROWS, width), bf16),
        ],
        mib=32,
        estimate=cost(
            4 * pairs * HEAD_WIDTH + 2 * QROWS * width * q_cols, 4 << 20, pairs
        ),
        name="attend_tail",
        after=after,
    )


def chunk_backward(keys, values, queries, d_outs, mask, shares, deltas, turned):
    d_key = None
    d_value = None
    for g in range(GROUP):
        scores = nt_dot(keys, queries[g])
        probs = jnp.where(mask, jnp.exp2(scores * (score_scale * log2_e)) * shares[g], 0.0)
        d_probs = nt_dot(values, d_outs[g])
        d_scores = (probs * (d_probs - deltas[g]) * score_scale).astype(bf16)
        d_value_now = nn_dot(probs.astype(bf16), d_outs[g])
        d_key_now = nn_dot(d_scores, queries[g])
        d_value = d_value_now if g == 0 else d_value + d_value_now
        d_key = d_key_now if g == 0 else d_key + d_key_now
        turned[g] = turned[g] + tn_dot(keys, d_scores)
    return d_key, d_value


def attend_back_tail_kernel(
    q_ref, k_ref, v_ref, bounds_ref, total_ref, attn_ref, d_proj_ref, w_ref,
    d_out_ref, turned_ref, delta_ref, d_kv_ref, dk_ref, dv_ref
):
    d_out_ref[...] = nn_dot(d_proj_ref[...], w_ref[...]).astype(bf16)
    for block in range(q_ref.shape[0] // QROWS):
        here = slice(block * QROWS, (block + 1) * QROWS)
        shares = [1.0 / total_ref[g : g + 1, here] for g in range(GROUP)]
        queries = [q_ref[here, head_span(g)] for g in range(GROUP)]
        d_outs = [d_out_ref[here, head_span(g)] for g in range(GROUP)]
        deltas = []
        for g in range(GROUP):
            product = d_outs[g].astype(f32) * attn_ref[here, head_span(g)].astype(f32)
            deltas.append(jnp.sum(product.T, axis=0, keepdims=True))
            delta_ref[g : g + 1, here] = deltas[g]
        turned = [jnp.zeros((HEAD_WIDTH, QROWS), f32) for g in range(GROUP)]
        for chunk in range(0, max(TAIL_CHUNKS - block, 0)):
            there = slice((block + chunk) * QROWS, (block + chunk + 1) * QROWS)
            mask = chunk_mask(bounds_ref[block, 0:1, :], bounds_ref[block, 1:2, :], chunk)
            d_key, d_value = chunk_backward(
                k_ref[there, :], v_ref[there, :], queries, d_outs, mask, shares, deltas, turned
            )
            if block == 0:
                dk_ref[there, :] = d_key
                dv_ref[there, :] = d_value
            else:
                dk_ref[there, :] += d_key
                dv_ref[there, :] += d_value
        for g in range(GROUP):
            turned_ref[head_span(g), here] = turned[g]
    d_kv_ref[0] = dk_ref[...].astype(bf16)
    d_kv_ref[1] = dv_ref[...].astype(bf16)


def attend_back_own_kernel(
    q_ref, k_ref, v_ref, bounds_ref, total_ref, d_out_ref, turned_ref, delta_ref, dq_ref, d_kv_ref
):
    for block in range(q_ref.shape[0] // QROWS):
        here = slice(block * QROWS, (block + 1) * QROWS)
        shares = [1.0 / total_ref[g : g + 1, here] for g in range(GROUP)]
        queries = [q_ref[here, head_span(g)] for g in range(GROUP)]
        d_outs = [d_out_ref[here, head_span(g)] for g in range(GROUP)]
        deltas = [delta_ref[g : g + 1, here] for g in range(GROUP)]
        turned = [turned_ref[head_span(g), here] for g in range(GROUP)]
        for chunk in range(max(TAIL_CHUNKS - block, 0), TAIL_CHUNKS + 1):
            row = (block + chunk - TAIL_CHUNKS) * QROWS
            there = slice(row, row + QROWS)
            mask = chunk_mask(bounds_ref[block, 0:1, :], bounds_ref[block, 1:2, :], chunk)
            d_key, d_value = chunk_backward(
                k_ref[there, :], v_ref[there, :], queries, d_outs, mask, shares, deltas, turned
            )
            if chunk == TAIL_CHUNKS:
                d_kv_ref[0, there, :] = d_key
                d_kv_ref[1, there, :] = d_value
            else:
                d_kv_ref[0, there, :] += d_key
                d_kv_ref[1, there, :] += d_value
        for g in range(GROUP):
            dq_ref[here, head_span(g)] = turned[g].T.astype(bf16)


def attend_back_tail(
    queries, kv_tail, bounds, totals, attn, d_proj, attn_w, attn_cols, after=()
):
    rows, q_cols = queries.shape
    width = attn_w.shape[0]
    kv_heads = kv_tail.shape[1] // (2 * HEAD_WIDTH)
    blocks = rows // QROWS
    wide = GROUP * HEAD_WIDTH
    pairs = chunk_pairs(sum(max(TAIL_CHUNKS - b, 0) for b in range(blocks)), kv_heads)
    head_spec = pl.BlockSpec((rows, wide), lambda j: (0, j))
    row_spec = pl.BlockSpec((None, 8, rows), lambda j: (j, 0, 0))
    return call(
        attend_back_tail_kernel,
        (queries, kv_tail, kv_tail, bounds, totals, attn, d_proj, attn_w),
        grid=(kv_heads,),
        in_specs=[
            head_spec,
            pl.BlockSpec((WINDOW_TOKENS, HEAD_WIDTH), lambda j: (0, j)),
            pl.BlockSpec((WINDOW_TOKENS, HEAD_WIDTH), lambda j: (0, kv_heads + j)),
            pl.BlockSpec((blocks, 8, QROWS), lambda j: (0, 0, 0)),
            row_spec,
            head_spec,
            pl.BlockSpec((rows, width), lambda j: (0, 0)),
            pl.BlockSpec((width, wide), lambda j: (0, attn_cols // wide + j)),
        ],
        out_specs=[
            head_spec,
            pl.BlockSpec((wide, rows), lambda j: (j, 0)),
            row_spec,
            pl.BlockSpec((2, WINDOW_TOKENS, HEAD_WIDTH), lambda j: (0, 0, j)),
        ],
        scratch=[pltpu.VMEM((WINDOW_TOKENS, HEAD_WIDTH), f32)] * 2,
        out_shape=[
            shape_of((rows, q_cols), bf16),
            shape_of((kv_heads * wide, rows), f32),
            shape_of((kv_heads, 8, rows), f32),
            shape_of((2, WINDOW_TOKENS, kv_heads * HEAD_WIDTH), bf16),
        ],
        mib=40,
        estimate=cost(10 * pairs * HEAD_WIDTH + 2 * rows * width * q_cols, 8 << 20, pairs),
        name="attend_back_tail",
        after=after,
    )


def attend_back_own(queries, kv_own, bounds, totals, d_outs, turned, deltas, after=()):
    rows, q_cols = queries.shape
    kv_heads = kv_own.shape[1] // (2 * HEAD_WIDTH)
    blocks = rows // QROWS
    wide = GROUP * HEAD_WIDTH
    pairs = chunk_pairs(sum(min(b, TAIL_CHUNKS) + 1 for b in range(blocks)), kv_heads)
    head_spec = pl.BlockSpec((rows, wide), lambda j: (0, j))
    row_spec = pl.BlockSpec((None, 8, rows), lambda j: (j, 0, 0))
    return call(
        attend_back_own_kernel,
        (queries, kv_own, kv_own, bounds, totals, d_outs, turned, deltas),
        grid=(kv_heads,),
        in_specs=[
            head_spec,
            pl.BlockSpec((rows, HEAD_WIDTH), lambda j: (0, j)),
            pl.BlockSpec((rows, HEAD_WIDTH), lambda j: (0, kv_heads + j)),
            pl.BlockSpec((blocks, 8, QROWS), lambda j: (0, 0, 0)),
            row_spec,
            head_spec,
            pl.BlockSpec((wide, rows), lambda j: (j, 0)),
            row_spec,
        ],
        out_specs=[
            head_spec,
            pl.BlockSpec((2, rows, HEAD_WIDTH), lambda j: (0, 0, j)),
        ],
        out_shape=[
            shape_of((rows, q_cols), bf16),
            shape_of((2, rows, kv_heads * HEAD_WIDTH), f32),
        ],
        mib=40,
        estimate=cost(10 * pairs * HEAD_WIDTH, 8 << 20, pairs, scale=1),
        name="attend_back_own",
        after=after,
    )


def mid_norm_kernel(x_ref, gain_ref, *refs):
    middle = x_ref[...].astype(f32)
    for ref in refs[:-2]:
        middle = middle + ref[...].astype(f32)
    refs[-2][...] = middle
    refs[-1][...] = (middle * norm_stats(middle) * gain_ref[...]).astype(bf16)


def mid_norm(hidden, gain, terms, after=()):
    rows, cols = hidden.shape
    spec = pl.BlockSpec((rows // 4, cols), lambda i: (i, 0))
    return call(
        mid_norm_kernel,
        (hidden, gain, *terms),
        grid=(4,),
        in_specs=[spec, pl.BlockSpec((1, cols), lambda i: (0, 0))] + [spec] * len(terms),
        out_specs=[spec, spec],
        out_shape=[shape_of((rows, cols), f32), shape_of((rows, cols), bf16)],
        estimate=cost(20 * rows * cols, 20 * rows * cols),
        name="mid_norm",
        after=after,
    )


def mid_back_kernel(own_ref, got_ref, middle_ref, grad_ref, gain_ref, out_ref, low_ref, sum_ref):
    @pl.when(pl.program_id(0) == 0)
    def clear():
        sum_ref[...] = jnp.zeros_like(sum_ref)

    d_normed = own_ref[...] + got_ref[...].astype(f32)
    middle = middle_ref[...]
    stats = norm_stats(middle)
    sum_ref[0:1, :] += jnp.sum(d_normed * (middle * stats), axis=0, keepdims=True)
    d_middle = grad_ref[...].astype(f32) + norm_back(d_normed, middle, stats, gain_ref[...])
    out_ref[...] = d_middle
    low_ref[...] = d_middle.astype(bf16)


def mid_back(own, got, middle, out_grad, gain, after=()):
    rows, cols = own.shape
    spec = pl.BlockSpec((rows // 4, cols), lambda i: (i, 0))
    return call(
        mid_back_kernel,
        (own, got, middle, out_grad, gain),
        grid=(4,),
        in_specs=[spec] * 4 + [pl.BlockSpec((1, cols), lambda i: (0, 0))],
        out_specs=[spec, spec, pl.BlockSpec((8, cols), lambda i: (0, 0))],
        out_shape=[
            shape_of((rows, cols), f32),
            shape_of((rows, cols), bf16),
            shape_of((8, cols), f32),
        ],
        estimate=cost(30 * rows * cols, 20 * rows * cols),
        name="mid_back",
        after=after,
    )


def mlp_kernel(
    x_own_ref, x_got_ref, g_own_ref, g_got_ref, wg_ref, wu_ref, wd_ref,
    mixed_ref, d_gate_ref, d_up_ref, d_mid_ref, d_mid_give_ref, out_ref, out_give_ref,
    x_ref, g_ref, d_mid_acc, out_acc
):
    step = pl.program_id(0)
    tokens = x_own_ref.shape[0]

    @pl.when(step == 0)
    def start():
        x_ref[:tokens, :] = x_own_ref[...]
        x_ref[tokens:, :] = x_got_ref[...]
        g_ref[:tokens, :] = g_own_ref[...]
        g_ref[tokens:, :] = g_got_ref[...]
        d_mid_acc[...] = jnp.zeros_like(d_mid_acc)
        out_acc[...] = jnp.zeros_like(out_acc)

    gate = nn_dot(x_ref[...], wg_ref[...])
    up = nn_dot(x_ref[...], wu_ref[...])
    d_mixed = nn_dot(g_ref[...], wd_ref[...])
    sig = 1.0 / (1.0 + jnp.exp(-gate))
    gated = gate * sig
    mixed = (gated * up).astype(bf16)
    d_gate = (d_mixed * up * sig * (1.0 + gate * (1.0 - sig))).astype(bf16)
    d_up = (d_mixed * gated).astype(bf16)
    mixed_ref[...] = mixed
    d_gate_ref[...] = d_gate
    d_up_ref[...] = d_up
    d_mid_acc[...] += nt_dot(d_gate, wg_ref[...]) + nt_dot(d_up, wu_ref[...])
    out_acc[...] += nt_dot(mixed, wd_ref[...])

    @pl.when(step == pl.num_programs(0) - 1)
    def finish():
        d_mid_ref[...] = d_mid_acc[:tokens, :]
        d_mid_give_ref[...] = d_mid_acc[tokens:, :].astype(bf16)
        out_ref[...] = out_acc[:tokens, :]
        out_give_ref[...] = out_acc[tokens:, :].astype(bf16)


def mlp(x_own, x_got, g_own, g_got, mlp_w, after=()):
    tokens, width = x_own.shape
    units = mlp_w.shape[1] // 3
    tile = 512
    steps = units // tile
    fixed = lambda j: (0, 0)
    rows_spec = pl.BlockSpec((tokens, width), fixed)
    tile_spec = pl.BlockSpec((2 * tokens, tile), lambda j: (0, j))
    tile_shape = shape_of((2 * tokens, units), bf16)
    return call(
        mlp_kernel,
        (x_own, x_got, g_own, g_got, mlp_w, mlp_w, mlp_w,),
        grid=(steps,),
        in_specs=[rows_spec] * 4
        + [
            pl.BlockSpec((width, tile), lambda j: (0, j)),
            pl.BlockSpec((width, tile), lambda j: (0, steps + j)),
            pl.BlockSpec((width, tile), lambda j: (0, 2 * steps + j)),
        ],
        out_specs=[tile_spec] * 3 + [rows_spec] * 4,
        out_shape=[tile_shape] * 3
        + [
            shape_of((tokens, width), f32),
            shape_of((tokens, width), bf16),
            shape_of((tokens, width), f32),
            shape_of((tokens, width), bf16),
        ],
        scratch=[
            pltpu.VMEM((2 * tokens, width), bf16),
            pltpu.VMEM((2 * tokens, width), bf16),
            pltpu.VMEM((2 * tokens, width), f32),
            pltpu.VMEM((2 * tokens, width), f32),
        ],
        mib=48,
        estimate=cost(12 * 2 * tokens * width * units, 16 << 20),
        name="mlp",
        after=after,
    )


def mlp_grad_kernel(own_ref, got_ref, d_ref, out_ref, turned_ref):
    tokens = own_ref.shape[0]

    @pl.when(pl.program_id(0) == 0)
    def start():
        turned_ref[:, :tokens] = own_ref[...].T
        turned_ref[:, tokens:] = got_ref[...].T

    out_ref[...] = nn_dot(turned_ref[...], d_ref[...]).astype(bf16)


def mlp_grad(own, got, d_units, after=()):
    tokens, width = own.shape
    units = d_units.shape[1]
    tile = 512
    fixed = lambda j: (0, 0)
    return call(
        mlp_grad_kernel,
        (own, got, d_units,),
        grid=(units // tile,),
        in_specs=[
            pl.BlockSpec((tokens, width), fixed),
            pl.BlockSpec((tokens, width), fixed),
            pl.BlockSpec((2 * tokens, tile), lambda j: (0, j)),
        ],
        out_specs=pl.BlockSpec((width, tile), lambda j: (0, j)),
        out_shape=shape_of((width, units), bf16),
        scratch=[pltpu.VMEM((width, 2 * tokens), bf16)],
        mib=32,
        estimate=cost(4 * tokens * width * units, 8 << 20),
        name="mlp_grad",
        after=after,
    )


def mlp_grad_pair_kernel(
    steps, own_a_ref, got_a_ref, d_a_ref, own_b_ref, got_b_ref, d_b_ref, out_ref, turned_ref
):
    step = pl.program_id(0)
    tokens = own_a_ref.shape[0]

    @pl.when(step == 0)
    def first():
        turned_ref[:, :tokens] = own_a_ref[...].T
        turned_ref[:, tokens:] = got_a_ref[...].T

    @pl.when(step == steps)
    def second():
        turned_ref[:, :tokens] = own_b_ref[...].T
        turned_ref[:, tokens:] = got_b_ref[...].T

    @pl.when(step < steps)
    def left():
        out_ref[...] = nn_dot(turned_ref[...], d_a_ref[...]).astype(bf16)

    @pl.when(step >= steps)
    def right():
        out_ref[...] = nn_dot(turned_ref[...], d_b_ref[...]).astype(bf16)


def mlp_grad_pair(own_a, got_a, d_a, own_b, got_b, d_b, after=()):
    tokens, width = own_a.shape
    units = d_a.shape[1]
    tile = 512
    steps = units // tile
    rows = pl.BlockSpec((tokens, width), lambda j: (0, 0))
    return call(
        functools.partial(mlp_grad_pair_kernel, steps),
        (own_a, got_a, d_a, own_b, got_b, d_b),
        grid=(2 * steps,),
        in_specs=[
            rows,
            rows,
            pl.BlockSpec((2 * tokens, tile), lambda j: (0, jnp.minimum(j, steps - 1))),
            rows,
            rows,
            pl.BlockSpec((2 * tokens, tile), lambda j: (0, jnp.maximum(j - steps, 0))),
        ],
        out_specs=pl.BlockSpec((width, tile), lambda j: (0, j)),
        scratch=[pltpu.VMEM((width, 2 * tokens), bf16)],
        out_shape=shape_of((width, 2 * units), bf16),
        mib=48,
        estimate=cost(8 * tokens * width * units, 16 << 20),
        name="mlp_grad_pair",
        after=after,
    )


def body(
    hidden_in,
    doc_lengths,
    pad_lengths,
    w_query,
    key_matrix,
    value_matrix,
    w_output,
    w_gate,
    w_up,
    w_down,
    attn_gain,
    mlp_gain,
    query_gain,
    key_gain,
    out_grad,
):
    core = lax.axis_index("c")
    chip = lax.axis_index("q")
    chips = lax.axis_size("q")
    group = chip * 2 + core
    part = lax.axis_index("seq")
    groups = chips * 2
    parts = lax.axis_size("seq")
    tokens, width = hidden_in.shape
    group_rows = tokens * parts
    slice_rows = width // groups
    units = FEEDFWD_UNITS // 2
    q_cols = QUERY_HEADS * HEAD_WIDTH // parts
    kv_cols = KEY_VALUE_HEADS * HEAD_WIDTH // parts
    attn_cols = q_cols + 2 * kv_cols
    pack_cols = attn_cols + q_cols
    core_at = core.astype(jnp.int32).reshape(1)
    part_at = part.astype(jnp.int32).reshape(1)
    chip_at = chip.astype(jnp.int32).reshape(1)

    def swapped(value):
        return lax.ppermute(value, "c", core_swap)

    def sent(value, shift):
        return lax.ppermute(value, "seq", [(i, (i + shift) % parts) for i in range(parts)])

    def from_all(value):
        return [value] + [sent(value, shift) for shift in range(1, parts)]

    def sent_chips(value, shift):
        return lax.ppermute(value, "q", [(i, (i + shift) % chips) for i in range(chips)])

    def line_step(value, step):
        return lax.ppermute(value, "seq", [(step - 1, step), (parts - step, parts - step - 1)])

    hidden_blocks = from_all(hidden_in)

    packed = pack_attn(
        part_at, parts, w_query, key_matrix, value_matrix, w_output,
        (attn_gain, mlp_gain, query_gain, key_gain),
    )
    attn_w = lax.all_gather(packed, dp_axes, axis=0, tiled=True)

    mlp_pack, mlp_give = pack_mlp(core_at, w_gate, w_up, w_down, after=(packed,))
    mlp_pack = lax.dynamic_update_slice_in_dim(
        mlp_pack, swapped(mlp_give), (1 - core) * slice_rows, 0
    )
    mlp_w = lax.all_gather(mlp_pack, "q", axis=0, tiled=True)
    grad_spread = jnp.where(
        (jnp.arange(2) == core)[:, None, None], jnp.zeros((), bf16), out_grad[None]
    )
    grad_got = lax.psum_scatter(grad_spread, "c", scatter_dimension=0, tiled=True)
    grad_got = grad_got.reshape(tokens, width)

    gains = read_gains(attn_w, pack_cols)
    head_piece = query_gain.shape[0]
    ga = gains[0:1]
    gm = gains[1:2]
    gqk = gains[2:4].reshape(2, groups, slice_rows)[:, :, :head_piece].reshape(2, HEAD_WIDTH)

    doc_ends = jnp.cumsum(doc_lengths)
    doc_starts = doc_ends - doc_lengths
    pad_starts = doc_ends - pad_lengths
    first = group * group_rows
    token = first + jnp.arange(group_rows, dtype=jnp.int32)
    inside = (token[:, None] >= doc_starts[None, :]) & (token[:, None] < doc_ends[None, :])
    start = jnp.sum(jnp.where(inside, doc_starts[None, :], 0), axis=1)
    pad_start = jnp.sum(jnp.where(inside, pad_starts[None, :], 0), axis=1)
    inv_freq = rope_base ** (-jnp.arange(HEAD_WIDTH // 2, dtype=f32) * 2.0 / HEAD_WIDTH)
    angles = (token - start).astype(f32)[:, None] * inv_freq[None, :]
    cosine = jnp.cos(angles)
    sine = jnp.sin(angles)
    cosine = jnp.concatenate([cosine, cosine], axis=1)
    sine = jnp.concatenate([-sine, sine], axis=1)
    offset = (token // QROWS) * QROWS - WINDOW_TOKENS
    low = jnp.maximum(start, token - (WINDOW_TOKENS - 1)) - offset
    high = jnp.minimum(token, pad_start - 1) - offset
    bounds = jnp.pad(
        jnp.stack([low.reshape(parts, QROWS), high.reshape(parts, QROWS)], axis=1),
        ((0, 0), (0, 6), (0, 0)),
    )

    normed_all, queries, kv_own, qk_proj = project(
        part_at, hidden_blocks, attn_w, ga, gqk, cosine, sine, q_cols, kv_cols
    )
    kv_tail = lax.ppermute(
        kv_own[group_rows - WINDOW_TOKENS :], dp_axes, [(i, i + 1) for i in range(groups - 1)]
    )
    own_outs, own_totals = attend_own(queries, kv_own, bounds)
    terms = []
    attn = [None] * parts
    totals = [None] * parts
    order = [shift for shift in range(1, parts)] + [0]
    for shift in order:
        attn[shift], totals[shift], term = attend_tail(
            shift, part_at, parts, queries, kv_tail, bounds, own_outs, own_totals, attn_w, attn_cols
        )
        terms.append(sent(term, shift) if shift else term)
    attn_all = jnp.zeros((group_rows, q_cols), bf16)
    totals_all = jnp.zeros((kv_cols // HEAD_WIDTH, 8, group_rows), f32)
    for shift in range(parts):
        row = (part + shift) % parts * tokens
        attn_all = lax.dynamic_update_slice_in_dim(attn_all, attn[shift], row, 0)
        totals_all = lax.dynamic_update_slice_in_dim(totals_all, totals[shift], row, 2)
    middle, normed_mid = mid_norm(hidden_in, gm, terms)

    mid_got = swapped(normed_mid)
    mixed, d_gate, d_up, d_mid, d_mid_give, out_part, out_give = mlp(
        normed_mid, mid_got, out_grad, grad_got, mlp_w
    )
    d_middle, d_proj, mlp_gain_rows = mid_back(
        d_mid, swapped(d_mid_give), middle, out_grad, gm
    )
    term_pair = mlp_grad_pair(
        out_grad, grad_got, mixed, normed_mid, mid_got, d_gate, after=(d_proj,)
    )
    d_proj_all = lax.all_gather(d_proj, "seq", axis=0, tiled=True)
    output_act = (middle + out_part + swapped(out_give).astype(f32)).astype(bf16)

    def chip_sums(grad):
        return lax.psum_scatter(grad, "q", scatter_dimension=0, tiled=True)

    own_pair = chip_sums(term_pair)
    term_up = mlp_grad(normed_mid, mid_got, d_up, after=(d_proj,))
    own_up = chip_sums(term_up)
    line = list(range(parts))

    def unpacked(sums, column, turned, after=()):
        give = lax.dynamic_slice(
            sums, ((1 - core) * slice_rows, column * units), (slice_rows, units)
        )
        return unpack_half(core_at, sums, swapped(give), column, turned, after=after)

    d_attn, turned, deltas, d_tail = attend_back_tail(
        queries, kv_tail, bounds, totals_all, attn_all, d_proj_all, attn_w, attn_cols,
        after=(term_up,),
    )
    d_tail = lax.ppermute(d_tail, dp_axes, [(i + 1, i) for i in range(groups - 1)])
    d_queries, d_kv = attend_back_own(
        queries, kv_own, bounds, totals_all, d_attn, turned, deltas
    )
    own_pair = touch(own_pair, after=(d_attn,))
    sum_pair = lax.psum(own_pair, "seq")
    w_out_grad = out_grad_sums([d_proj_all], [attn_all], after=(d_queries,))
    d_in, attn_term = project_back(
        part_at, groups, [hidden_blocks[(parts - k) % parts] for k in range(parts)],
        d_queries, d_kv, d_tail, qk_proj, attn_w, gqk, cosine, sine, normed_all, w_out_grad,
        mlp_gain_rows,
    )
    d_in = lax.psum_scatter(d_in, "seq", scatter_dimension=0, tiled=True)

    attn_grad = lax.psum_scatter(attn_term, dp_axes, scatter_dimension=0, tiled=True)
    got_up = [line_step(own_up, 1)]
    grad_down = unpacked(sum_pair, 0, True)
    grad_gate = unpacked(sum_pair, 1, False, after=(grad_down,))
    last = grad_gate
    for step in range(2, parts):
        last = add(own_up, got_up[-1], after=(last,))
        got_up.append(line_step(last, step))
    attn_grad = touch(attn_grad, after=(last,))
    attn_grads = lax.all_gather(attn_grad, "seq", axis=0)
    in_grad = finish_in(d_in, d_middle, hidden_in, ga)
    sum_up = sum_all([own_up, *got_up], after=(attn_grad,))
    grad_up = unpacked(sum_up, 0, False)
    gain_sums = jnp.sum(attn_grads[:, :, pack_cols : pack_cols + 4].astype(f32), axis=0)
    grad_query, grad_key, grad_value, grad_output = unpack_attn(
        attn_grads, q_cols, kv_cols, after=(grad_up, in_grad)
    )
    return (
        output_act,
        in_grad,
        grad_query,
        grad_key,
        grad_value,
        grad_output,
        grad_gate,
        grad_up,
        grad_down,
        gain_sums[:, 0],
        gain_sums[:, 1],
        gain_sums[:head_piece, 2],
        gain_sums[:head_piece, 3],
    )


def solution(mesh):
    groups, parts = mesh.devices.shape
    mesh = Mesh(mesh.devices.reshape(groups // 2, 2, parts), ("q", "c", "seq"))
    tokens = P(("q", "c", "seq"), None)
    rows = P(dp_axes, None)
    cols = P(None, dp_axes)
    flat = P(dp_axes)
    in_specs = (
        tokens, P(), P(), rows, rows, rows, cols, rows, rows, cols, flat, flat, flat, flat, tokens,
    )
    out_specs = (
        tokens, tokens, rows, rows, rows, cols, rows, rows, cols, flat, flat, flat, flat,
    )
    return jax.shard_map(body, mesh=mesh, in_specs=in_specs, out_specs=out_specs, check_vma=False)
```

```python
import functools

import jax
import jax.numpy as jnp
from jax import lax
from jax.experimental import pallas as pl
from jax.experimental.pallas import tpu as pltpu
from jax.sharding import Mesh, PartitionSpec as P

QUERY_HEADS = 16
KEY_VALUE_HEADS = 8
HEAD_WIDTH = 128
FEEDFWD_UNITS = 3072
WINDOW_TOKENS = 1024
QROWS = 256
GROUP = QUERY_HEADS // KEY_VALUE_HEADS
TAIL_CHUNKS = WINDOW_TOKENS // QROWS

norm_eps = 1e-06
rope_base = 1000000.0
score_scale = HEAD_WIDTH**-0.5
log2_e = 1.4426950408889634
bf16 = jnp.bfloat16
f32 = jnp.float32
dp_axes = ("q", "c")
core_swap = [(0, 1), (1, 0)]


def nt_dot(left, right):
    return lax.dot_general(left, right, (((1,), (1,)), ((), ())), preferred_element_type=f32)


def tn_dot(left, right):
    return lax.dot_general(left, right, (((0,), (0,)), ((), ())), preferred_element_type=f32)


def nn_dot(left, right):
    return jnp.dot(left, right, preferred_element_type=f32)


def shape_of(dims, kind):
    return jax.ShapeDtypeStruct(dims, kind)


def call(
    kernel, args, *, grid, in_specs, out_specs, out_shape, name, estimate, prefetch=0, scratch=(),
    mib=32, after=()
):
    count = prefetch + len(in_specs)

    def body_of(*refs):
        kernel(*refs[:count], *refs[count + len(after) :])

    return pl.pallas_call(
        body_of,
        grid_spec=pltpu.PrefetchScalarGridSpec(
            num_scalar_prefetch=prefetch,
            grid=grid,
            in_specs=list(in_specs) + [pl.BlockSpec(memory_space=pl.ANY)] * len(after),
            out_specs=out_specs,
            scratch_shapes=list(scratch),
        ),
        out_shape=out_shape,
        compiler_params=pltpu.CompilerParams(vmem_limit_bytes=mib << 20),
        cost_estimate=estimate,
        name=name,
    )(*args, *after)


def cost(flops, moved, exps=0, scale=100):
    flops, moved, exps = flops * scale, moved * scale, exps * scale
    return pl.CostEstimate(flops=int(flops), bytes_accessed=int(moved), transcendentals=int(exps))


def norm_stats(rows):
    return lax.rsqrt(jnp.mean(rows * rows, axis=-1, keepdims=True) + norm_eps)


def norm_back(d_normed, rows, stats, gains):
    scaled = d_normed * gains
    unit = rows * stats
    return stats * (scaled - unit * jnp.mean(scaled * unit, axis=-1, keepdims=True))


def pack_attn_kernel(
    part_ref, wq_ref, wk_ref, wv_ref, wo_ref, ga_ref, gm_ref, gq_ref, gk_ref, out_ref, gains_ref
):
    gains_ref[...] = jnp.zeros_like(gains_ref)
    for row, gain_ref in enumerate((ga_ref, gm_ref, gq_ref, gk_ref)):
        gains_ref[row : row + 1, : gain_ref.shape[1]] = gain_ref[...]
    column = 0
    for piece in (
        wq_ref[...].astype(bf16),
        wk_ref[...].astype(bf16),
        wv_ref[...].astype(bf16),
        wo_ref[...].T.astype(bf16),
    ):
        out_ref[:, column : column + piece.shape[1]] = piece
        column += piece.shape[1]
    gains = gains_ref[...].T
    rest = jnp.zeros((gains.shape[0], HEAD_WIDTH - gains.shape[1]), f32)
    out_ref[:, column:] = jnp.concatenate([gains, rest], axis=1).astype(bf16)


def pack_attn(part, parts, w_query, key_matrix, value_matrix, w_output, gains, after=()):
    gains = [gain[None] for gain in gains]
    rows = w_query.shape[0]
    q_cols = w_query.shape[1] // parts
    kv_cols = key_matrix.shape[1] // parts
    total = 2 * q_cols + 2 * kv_cols + HEAD_WIDTH
    return call(
        pack_attn_kernel,
        (part, w_query, key_matrix, value_matrix, w_output, *gains),
        prefetch=1,
        grid=(1,),
        in_specs=[
            pl.BlockSpec((rows, q_cols), lambda i, p: (0, p[0])),
            pl.BlockSpec((rows, kv_cols), lambda i, p: (0, p[0])),
            pl.BlockSpec((rows, kv_cols), lambda i, p: (0, p[0])),
            pl.BlockSpec((q_cols, rows), lambda i, p: (p[0], 0)),
        ]
        + [pl.BlockSpec(gain.shape, lambda i, p: (0, 0)) for gain in gains],
        scratch=[pltpu.VMEM((8, rows), f32)],
        mib=60,
        out_specs=pl.BlockSpec((rows, total), lambda i, p: (0, 0)),
        out_shape=shape_of((rows, total), bf16),
        estimate=cost(0, rows * total * 6),
        name="pack_attn",
        after=after,
    )


def touch_kernel(in_ref, out_ref):
    out_ref[...] = in_ref[...]


def touch(value, after):
    rows, cols = value.shape
    spec = pl.BlockSpec((rows // 4, cols), lambda i: (i, 0))
    return call(
        touch_kernel,
        (value,),
        grid=(4,),
        in_specs=[spec],
        out_specs=spec,
        out_shape=shape_of((rows, cols), value.dtype),
        estimate=cost(0, 4 * rows * cols),
        name="touch",
        after=after,
    )


def finish_in_kernel(d_normed_ref, d_middle_ref, x_ref, gain_ref, out_ref):
    rows = x_ref[...].astype(f32)
    back = norm_back(d_normed_ref[...].astype(f32), rows, norm_stats(rows), gain_ref[...])
    out_ref[...] = (d_middle_ref[...] + back).astype(bf16)


def finish_in(d_normed, d_middle, hidden, gain, after=()):
    rows, cols = hidden.shape
    spec = pl.BlockSpec((rows // 4, cols), lambda i: (i, 0))
    return call(
        finish_in_kernel,
        (d_normed, d_middle, hidden, gain),
        grid=(4,),
        in_specs=[spec] * 3 + [pl.BlockSpec((1, cols), lambda i: (0, 0))],
        out_specs=spec,
        out_shape=shape_of((rows, cols), bf16),
        estimate=cost(20 * rows * cols, 12 * rows * cols, scale=1),
        name="finish_in",
        after=after,
    )


def read_gains_kernel(in_ref, out_ref):
    out_ref[...] = in_ref[...].astype(f32).T[:8, :]


def read_gains(attn_w, column, after=()):
    width = attn_w.shape[0]
    return call(
        read_gains_kernel,
        (attn_w,),
        grid=(1,),
        in_specs=[pl.BlockSpec((width, HEAD_WIDTH), lambda i: (0, column // HEAD_WIDTH))],
        out_specs=pl.BlockSpec((8, width), lambda i: (0, 0)),
        out_shape=shape_of((8, width), f32),
        estimate=cost(0, width * HEAD_WIDTH * 4),
        name="read_gains",
        after=after,
    )


def pack_mlp_kernel(core_ref, wg_ref, wu_ref, wd_ref, own_ref, give_ref):
    units = wg_ref.shape[1]

    def fill(out_ref):
        out_ref[:, :units] = wg_ref[...].astype(bf16)
        out_ref[:, units : 2 * units] = wu_ref[...].astype(bf16)
        out_ref[:, 2 * units :] = wd_ref[...].T.astype(bf16)

    @pl.when(pl.program_id(0) == 0)
    def first():
        fill(give_ref)

    @pl.when(pl.program_id(0) == 1)
    def second():
        fill(own_ref)


def pack_mlp(core, w_gate, w_up, w_down, after=()):
    rows = w_gate.shape[0]
    units = w_gate.shape[1] // 2
    half = lambda i, c: (c[0] + 1 - i) % 2
    return call(
        pack_mlp_kernel,
        (core, w_gate, w_up, w_down,),
        prefetch=1,
        grid=(2,),
        in_specs=[
            pl.BlockSpec((rows, units), lambda i, c: (0, half(i, c))),
            pl.BlockSpec((rows, units), lambda i, c: (0, half(i, c))),
            pl.BlockSpec((units, rows), lambda i, c: (half(i, c), 0)),
        ],
        out_specs=[
            pl.BlockSpec((rows, 3 * units), lambda i, c: (c[0], 0)),
            pl.BlockSpec((rows, 3 * units), lambda i, c: (0, 0)),
        ],
        out_shape=[shape_of((2 * rows, 3 * units), bf16), shape_of((rows, 3 * units), bf16)],
        estimate=cost(0, rows * units * 36),
        name="pack_mlp",
        after=after,
    )


def unpack_half_kernel(turned, core_ref, own_ref, got_ref, out_ref):
    def fill(in_ref):
        rows = in_ref[...].astype(f32)
        out_ref[...] = rows.T if turned else rows

    @pl.when(pl.program_id(0) == 0)
    def first():
        fill(own_ref)

    @pl.when(pl.program_id(0) == 1)
    def second():
        fill(got_ref)


def unpack_half(core, sums, got, column, turned, after=()):
    rows, units = got.shape
    half = lambda i, c: (c[0] + i) % 2
    if turned:
        out_spec = pl.BlockSpec((units, rows), lambda i, c: (half(i, c), 0))
        out_shape = shape_of((2 * units, rows), f32)
    else:
        out_spec = pl.BlockSpec((rows, units), lambda i, c: (0, half(i, c)))
        out_shape = shape_of((rows, 2 * units), f32)
    return call(
        functools.partial(unpack_half_kernel, turned),
        (core, sums, got,),
        prefetch=1,
        grid=(2,),
        in_specs=[
            pl.BlockSpec((rows, units), lambda i, c: (c[0], column)),
            pl.BlockSpec((rows, units), lambda i, c: (0, 0)),
        ],
        out_specs=out_spec,
        out_shape=out_shape,
        estimate=cost(0, rows * units * 12, scale=1),
        name="unpack_half",
        after=after,
    )


def join_halves_kernel(core_ref, own_ref, got_ref, out_ref):
    @pl.when(pl.program_id(0) == 0)
    def first():
        out_ref[...] = own_ref[...]

    @pl.when(pl.program_id(0) == 1)
    def second():
        out_ref[...] = got_ref[...]


def join_halves(core, sums, got, after=()):
    rows, units = got.shape
    return call(
        join_halves_kernel,
        (core, sums, got),
        prefetch=1,
        grid=(2,),
        in_specs=[
            pl.BlockSpec((rows, units), lambda i, c: (c[0], 0)),
            pl.BlockSpec((rows, units), lambda i, c: (0, 0)),
        ],
        out_specs=pl.BlockSpec((rows, units), lambda i, c: (0, (c[0] + i) % 2)),
        out_shape=shape_of((rows, 2 * units), bf16),
        estimate=cost(0, rows * units * 8, scale=1),
        name="join_halves",
        after=after,
    )


def widened_kernel(in_ref, out_ref):
    out_ref[...] = in_ref[...].astype(f32)


def widened(value, after=()):
    rows, cols = value.shape
    spec = pl.BlockSpec((rows, cols // 2), lambda i: (0, i))
    return call(
        widened_kernel,
        (value,),
        grid=(2,),
        in_specs=[spec],
        out_specs=spec,
        out_shape=shape_of((rows, cols), f32),
        estimate=cost(0, rows * cols * 6, scale=1),
        name="widened",
        after=after,
    )


def unpack_attn_kernel(in_ref, wq_ref, wk_ref, wv_ref, wo_ref):
    column = 0
    for out_ref in (wq_ref, wk_ref, wv_ref):
        count = out_ref.shape[1]
        out_ref[...] = in_ref[:, column : column + count].astype(f32)
        column += count
    wo_ref[...] = in_ref[:, column : column + wo_ref.shape[0]].astype(f32).T


def unpack_attn(gathered, q_cols, kv_cols, after=()):
    parts, rows, total = gathered.shape
    return call(
        unpack_attn_kernel,
        (gathered,),
        grid=(parts,),
        in_specs=[pl.BlockSpec((None, rows, total), lambda i: (i, 0, 0))],
        out_specs=[
            pl.BlockSpec((rows, q_cols), lambda i: (0, i)),
            pl.BlockSpec((rows, kv_cols), lambda i: (0, i)),
            pl.BlockSpec((rows, kv_cols), lambda i: (0, i)),
            pl.BlockSpec((q_cols, rows), lambda i: (i, 0)),
        ],
        out_shape=[
            shape_of((rows, parts * q_cols), f32),
            shape_of((rows, parts * kv_cols), f32),
            shape_of((rows, parts * kv_cols), f32),
            shape_of((parts * q_cols, rows), f32),
        ],
        estimate=cost(0, parts * rows * total * 6, scale=1),
        name="unpack_attn",
        after=after,
    )


def pick(refs, scratch):
    for k, ref in enumerate(refs):

        @pl.when(pl.program_id(0) == k)
        def take(ref=ref):
            scratch[...] = ref[...]


def turn(rows):
    half = HEAD_WIDTH // 2
    return jnp.concatenate([rows[:, half:], rows[:, :half]], axis=1)


def project_kernel(parts, q_cols, kv_cols, part_ref, *refs):
    blocks = refs[:parts]
    w_ref, ga_ref, gqk_ref, cos_ref, sin_ref, normed_ref, q_ref, kv_ref, proj_ref, x_ref = refs[parts:]
    pick(blocks, x_ref)
    rows = x_ref[...].astype(f32)
    normed = (rows * norm_stats(rows) * ga_ref[...]).astype(bf16)
    normed_ref[...] = normed
    cosine = cos_ref[...]
    sine = sin_ref[...]
    qk_cols = q_cols + kv_cols
    proj = nn_dot(normed, w_ref[...])
    proj_ref[...] = proj[:, :qk_cols]
    kv_ref[:, kv_cols:] = proj[:, qk_cols:].astype(bf16)
    for column in range(0, qk_cols, HEAD_WIDTH):
        head = proj[:, column : column + HEAD_WIDTH]
        gain = gqk_ref[0:1, :] if column < q_cols else gqk_ref[1:2, :]
        head = head * norm_stats(head) * gain
        head = (head * cosine + turn(head) * sine).astype(bf16)
        if column < q_cols:
            q_ref[:, column : column + HEAD_WIDTH] = head
        else:
            kv_ref[:, column - q_cols : column - q_cols + HEAD_WIDTH] = head


def project(part, blocks, attn_w, ga, gqk, cosine, sine, q_cols, kv_cols, after=()):
    parts = len(blocks)
    tokens, width = blocks[0].shape
    attn_cols = q_cols + 2 * kv_cols
    place = lambda k, p: ((p[0] + parts - k) % parts, 0)
    fixed = lambda k, p: (0, 0)
    rows = parts * tokens
    return call(
        functools.partial(project_kernel, parts, q_cols, kv_cols),
        (part, *blocks, attn_w, ga, gqk, cosine, sine,),
        prefetch=1,
        grid=(parts,),
        in_specs=[pl.BlockSpec((tokens, width), fixed)] * parts
        + [
            pl.BlockSpec((width, attn_cols), fixed),
            pl.BlockSpec((1, width), fixed),
            pl.BlockSpec((2, HEAD_WIDTH), fixed),
            pl.BlockSpec((tokens, HEAD_WIDTH), place),
            pl.BlockSpec((tokens, HEAD_WIDTH), place),
        ],
        out_specs=[
            pl.BlockSpec((tokens, width), place),
            pl.BlockSpec((tokens, q_cols), place),
            pl.BlockSpec((tokens, 2 * kv_cols), place),
            pl.BlockSpec((tokens, q_cols + kv_cols), place),
        ],
        scratch=[pltpu.VMEM((tokens, width), bf16)],
        out_shape=[
            shape_of((rows, width), bf16),
            shape_of((rows, q_cols), bf16),
            shape_of((rows, 2 * kv_cols), bf16),
            shape_of((rows, q_cols + kv_cols), f32),
        ],
        mib=32,
        estimate=cost(2 * rows * width * attn_cols, 12 << 20),
        name="project",
        after=after,
    )


def project_back_kernel(
    parts, groups, tail_from, q_cols, kv_cols, part_ref, *refs
):
    blocks = refs[:parts]
    (dq_ref, d_kv_ref, tail_ref, proj_ref, w_ref, gqk_ref, cos_ref, sin_ref, normed_ref,
     w_out_ref, mlp_gain_ref, out_ref, term_ref,
     x_ref, dqkv_ref, acc_ref, gain_ref, head_gain_ref) = refs[parts:]
    step = pl.program_id(0)
    block = (part_ref[0] + step) % parts
    pick(blocks, x_ref)

    @pl.when(step == 0)
    def clear():
        gain_ref[...] = jnp.zeros_like(gain_ref)
        head_gain_ref[...] = jnp.zeros_like(head_gain_ref)
        acc_ref[...] = jnp.zeros_like(acc_ref)

    cosine = cos_ref[...]
    sine = sin_ref[...]
    has_tail = jnp.where(block >= tail_from, 1.0, 0.0)
    dk = (d_kv_ref[0] + tail_ref[0].astype(f32) * has_tail).astype(bf16)
    dqkv_ref[:, q_cols + kv_cols :] = (
        d_kv_ref[1] + tail_ref[1].astype(f32) * has_tail
    ).astype(bf16)
    head_gains = [jnp.zeros((1, HEAD_WIDTH), f32) for _ in range(2)]
    for column in range(0, q_cols + kv_cols, HEAD_WIDTH):
        index = 0 if column < q_cols else 1
        if index == 0:
            d_head = dq_ref[:, column : column + HEAD_WIDTH].astype(f32)
        else:
            d_head = dk[:, column - q_cols : column - q_cols + HEAD_WIDTH].astype(f32)
        d_head = d_head * cosine + turn(d_head * sine)
        head = proj_ref[:, column : column + HEAD_WIDTH]
        stats = norm_stats(head)
        unit = head * stats
        head_gains[index] = head_gains[index] + jnp.sum(d_head * unit, axis=0, keepdims=True)
        scaled = d_head * gqk_ref[index : index + 1, :]
        d_proj = stats * (scaled - unit * jnp.mean(scaled * unit, axis=-1, keepdims=True))
        dqkv_ref[:, column : column + HEAD_WIDTH] = d_proj.astype(bf16)
    head_gain_ref[0:1, :] += head_gains[0]
    head_gain_ref[1:2, :] += head_gains[1]
    d_in = nt_dot(dqkv_ref[...], w_ref[...])
    rows = x_ref[...].astype(f32)
    gain_ref[0:1, :] += jnp.sum(d_in * (rows * norm_stats(rows)), axis=0, keepdims=True)
    out_ref[...] = d_in.astype(bf16)
    acc_ref[...] += tn_dot(normed_ref[...], dqkv_ref[...])

    @pl.when(step == parts - 1)
    def finish():
        attn_cols = acc_ref.shape[1]
        term_ref[:, :attn_cols] = acc_ref[...].astype(bf16)
        term_ref[:, attn_cols : attn_cols + q_cols] = w_out_ref[...]
        gain_ref[1:2, :] = mlp_gain_ref[0:1, :]
        piece = HEAD_WIDTH // groups
        slice_rows = gain_ref.shape[1] // groups
        for index in range(2):
            for group in range(groups):
                gain_ref[2 + index : 3 + index, group * slice_rows : group * slice_rows + piece] = (
                    head_gain_ref[index : index + 1, group * piece : (group + 1) * piece]
                )
        gains = gain_ref[...].T
        rest = jnp.zeros((gains.shape[0], HEAD_WIDTH - gains.shape[1]), f32)
        term_ref[:, attn_cols + q_cols :] = jnp.concatenate([gains, rest], axis=1).astype(bf16)


def project_back(
    part, groups, hidden, dq, d_kv, tail, proj, attn_w, gqk, cosine, sine, normed,
    w_out_grad, mlp_gain_rows, after=()
):
    parts = len(hidden)
    tokens, width = hidden[0].shape
    rows, q_cols = dq.shape
    kv_cols = d_kv.shape[2]
    attn_cols = q_cols + 2 * kv_cols
    tail_from = (rows - WINDOW_TOKENS) // tokens
    place = lambda k, p: ((p[0] + k) % parts, 0)
    kv_place = lambda k, p: (0, (p[0] + k) % parts, 0)
    tail_place = lambda k, p: (0, jnp.maximum((p[0] + k) % parts - tail_from, 0), 0)
    fixed = lambda k, p: (0, 0)
    total = attn_cols + q_cols + HEAD_WIDTH
    return call(
        functools.partial(project_back_kernel, parts, groups, tail_from, q_cols, kv_cols),
        (part, *hidden, dq, d_kv, tail, proj, attn_w, gqk, cosine, sine, normed, w_out_grad, mlp_gain_rows),
        prefetch=1,
        grid=(parts,),
        in_specs=[pl.BlockSpec((tokens, width), fixed)] * parts
        + [
            pl.BlockSpec((tokens, q_cols), place),
            pl.BlockSpec((2, tokens, kv_cols), kv_place),
            pl.BlockSpec((2, tokens, kv_cols), tail_place),
            pl.BlockSpec((tokens, q_cols + kv_cols), place),
            pl.BlockSpec((width, attn_cols), fixed),
            pl.BlockSpec((2, HEAD_WIDTH), fixed),
            pl.BlockSpec((tokens, HEAD_WIDTH), place),
            pl.BlockSpec((tokens, HEAD_WIDTH), place),
            pl.BlockSpec((tokens, width), place),
            pl.BlockSpec((width, q_cols), fixed),
            pl.BlockSpec((8, width), fixed),
        ],
        out_specs=[
            pl.BlockSpec((tokens, width), place),
            pl.BlockSpec((width, total), fixed),
        ],
        scratch=[
            pltpu.VMEM((tokens, width), bf16),
            pltpu.VMEM((tokens, attn_cols), bf16),
            pltpu.VMEM((width, attn_cols), f32),
            pltpu.VMEM((8, width), f32),
            pltpu.VMEM((8, HEAD_WIDTH), f32),
        ],
        mib=48,
        out_shape=[
            shape_of((rows, width), bf16),
            shape_of((width, total), bf16),
        ],
        estimate=cost(4 * rows * width * attn_cols, 16 << 20, scale=1),
        name="project_back",
        after=after,
    )


def out_grad_kernel(parts, *refs):
    d_projs = refs[:parts]
    attns = refs[parts : 2 * parts]
    out_ref = refs[2 * parts]
    total = None
    for d_proj, attn in zip(d_projs, attns):
        term = tn_dot(d_proj[...], attn[...])
        total = term if total is None else total + term
    out_ref[...] = total.astype(bf16)


def out_grad_sums(d_projs, attns, after=()):
    parts = len(attns)
    tokens, q_cols = attns[0].shape
    width = d_projs[0].shape[1]
    cols = width // 4
    return call(
        functools.partial(out_grad_kernel, parts),
        (*d_projs, *attns,),
        grid=(4,),
        in_specs=[pl.BlockSpec((tokens, cols), lambda i: (0, i))] * parts
        + [pl.BlockSpec((tokens, q_cols), lambda i: (0, 0))] * parts,
        out_specs=pl.BlockSpec((cols, q_cols), lambda i: (i, 0)),
        out_shape=shape_of((width, q_cols), bf16),
        mib=32,
        estimate=cost(2 * parts * tokens * width * q_cols, 4 << 20, scale=1),
        name="out_grad",
        after=after,
    )


def chunk_mask(low, high, chunk):
    key = lax.broadcasted_iota(jnp.int32, (QROWS, QROWS), 0) + chunk * QROWS
    mask = (key >= low) & (key <= high)
    if chunk == TAIL_CHUNKS:
        own = lax.broadcasted_iota(jnp.int32, (QROWS, QROWS), 1) + WINDOW_TOKENS
        mask = mask | (key == own)
    return mask


def head_span(g):
    return slice(g * HEAD_WIDTH, (g + 1) * HEAD_WIDTH)


def attend_own_kernel(q_ref, k_ref, v_ref, bounds_ref, out_ref, total_ref):
    for block in range(q_ref.shape[0] // QROWS):
        here = slice(block * QROWS, (block + 1) * QROWS)
        sums = [jnp.zeros((1, QROWS), f32) for g in range(GROUP)]
        outs = [jnp.zeros((HEAD_WIDTH, QROWS), f32) for g in range(GROUP)]
        for chunk in range(max(TAIL_CHUNKS - block, 0), TAIL_CHUNKS + 1):
            row = (block + chunk - TAIL_CHUNKS) * QROWS
            there = slice(row, row + QROWS)
            mask = chunk_mask(bounds_ref[block, 0:1, :], bounds_ref[block, 1:2, :], chunk)
            for g in range(GROUP):
                scores = nt_dot(k_ref[there, :], q_ref[here, head_span(g)])
                weights = jnp.where(mask, jnp.exp2(scores * (score_scale * log2_e)), 0.0)
                sums[g] = sums[g] + jnp.sum(weights, axis=0, keepdims=True)
                outs[g] = outs[g] + tn_dot(v_ref[there, :], weights.astype(bf16))
        for g in range(GROUP):
            out_ref[head_span(g), here] = outs[g]
            total_ref[g : g + 1, here] = sums[g]


def chunk_pairs(chunks, kv_heads):
    return chunks * kv_heads * GROUP * QROWS * QROWS


def attend_own(queries, kv_own, bounds, after=()):
    rows = queries.shape[0]
    kv_heads = kv_own.shape[1] // (2 * HEAD_WIDTH)
    blocks = rows // QROWS
    wide = GROUP * HEAD_WIDTH
    pairs = chunk_pairs(sum(min(b, TAIL_CHUNKS) + 1 for b in range(blocks)), kv_heads)
    return call(
        attend_own_kernel,
        (queries, kv_own, kv_own, bounds,),
        grid=(kv_heads,),
        in_specs=[
            pl.BlockSpec((rows, wide), lambda j: (0, j)),
            pl.BlockSpec((rows, HEAD_WIDTH), lambda j: (0, j)),
            pl.BlockSpec((rows, HEAD_WIDTH), lambda j: (0, kv_heads + j)),
            pl.BlockSpec((blocks, 8, QROWS), lambda j: (0, 0, 0)),
        ],
        out_specs=[
            pl.BlockSpec((wide, rows), lambda j: (j, 0)),
            pl.BlockSpec((None, 8, rows), lambda j: (j, 0, 0)),
        ],
        out_shape=[shape_of((kv_heads * wide, rows), f32), shape_of((kv_heads, 8, rows), f32)],
        mib=32,
        estimate=cost(4 * pairs * HEAD_WIDTH, 4 << 20, pairs),
        name="attend_own",
        after=after,
    )


def attend_tail_kernel(
    shift, parts, part_ref, q_ref, k_ref, v_ref, bounds_ref, own_ref, own_total_ref, w_ref,
    attn_ref, total_ref, proj_ref, out_ref, acc_ref
):
    block = (part_ref[0] + shift) % parts
    out_ref[...] = own_ref[...]
    total_ref[...] = own_total_ref[...]
    for chunk in range(TAIL_CHUNKS):

        @pl.when(block + chunk < TAIL_CHUNKS)
        def add(chunk=chunk):
            there = pl.ds(pl.multiple_of((block + chunk) * QROWS, QROWS), QROWS)
            keys = k_ref[there, :]
            values = v_ref[there, :]
            mask = chunk_mask(bounds_ref[0:1, :], bounds_ref[1:2, :], chunk)
            for g in range(GROUP):
                scores = nt_dot(keys, q_ref[:, head_span(g)])
                weights = jnp.where(mask, jnp.exp2(scores * (score_scale * log2_e)), 0.0)
                total_ref[g : g + 1, :] += jnp.sum(weights, axis=0, keepdims=True)
                out_ref[head_span(g), :] += tn_dot(values, weights.astype(bf16))

    for g in range(GROUP):
        share = 1.0 / total_ref[g : g + 1, :]
        attn_ref[:, head_span(g)] = (out_ref[head_span(g), :] * share).T.astype(bf16)
    term = nt_dot(attn_ref[...], w_ref[...])
    last = pl.num_programs(0) - 1

    @pl.when(pl.program_id(0) == 0)
    def start():
        acc_ref[...] = term

    @pl.when(pl.program_id(0) > 0)
    def add_up():
        acc_ref[...] += term

    @pl.when(pl.program_id(0) == last)
    def finish():
        proj_ref[...] = acc_ref[...].astype(bf16)


def attend_tail(shift, part, parts, queries, kv_tail, bounds, outs, totals, attn_w, attn_cols, after=()):
    q_cols = queries.shape[1]
    width = attn_w.shape[0]
    kv_heads = kv_tail.shape[1] // (2 * HEAD_WIDTH)
    wide = GROUP * HEAD_WIDTH
    at = lambda p: (p[0] + shift) % parts
    pairs = chunk_pairs(TAIL_CHUNKS // 2, kv_heads)
    return call(
        functools.partial(attend_tail_kernel, shift, parts),
        (part, queries, kv_tail, kv_tail, bounds, outs, totals, attn_w,),
        prefetch=1,
        grid=(kv_heads,),
        in_specs=[
            pl.BlockSpec((QROWS, wide), lambda j, p: (at(p), j)),
            pl.BlockSpec((WINDOW_TOKENS, HEAD_WIDTH), lambda j, p: (0, j)),
            pl.BlockSpec((WINDOW_TOKENS, HEAD_WIDTH), lambda j, p: (0, kv_heads + j)),
            pl.BlockSpec((None, 8, QROWS), lambda j, p: (at(p), 0, 0)),
            pl.BlockSpec((wide, QROWS), lambda j, p: (j, at(p))),
            pl.BlockSpec((None, 8, QROWS), lambda j, p: (j, 0, at(p))),
            pl.BlockSpec((width, wide), lambda j, p: (0, attn_cols // wide + j)),
        ],
        out_specs=[
            pl.BlockSpec((QROWS, wide), lambda j, p: (0, j)),
            pl.BlockSpec((None, 8, QROWS), lambda j, p: (j, 0, 0)),
            pl.BlockSpec((QROWS, width), lambda j, p: (0, 0)),
        ],
        scratch=[pltpu.VMEM((wide, QROWS), f32), pltpu.VMEM((QROWS, width), f32)],
        out_shape=[
            shape_of((QROWS, q_cols), bf16),
            shape_of((kv_heads, 8, QROWS), f32),
            shape_of((QROWS, width), bf16),
        ],
        mib=32,
        estimate=cost(
            4 * pairs * HEAD_WIDTH + 2 * QROWS * width * q_cols, 4 << 20, pairs
        ),
        name="attend_tail",
        after=after,
    )


def chunk_backward(keys, values, queries, d_outs, mask, shares, deltas, turned):
    d_key = None
    d_value = None
    for g in range(GROUP):
        scores = nt_dot(keys, queries[g])
        probs = jnp.where(mask, jnp.exp2(scores * (score_scale * log2_e)) * shares[g], 0.0)
        d_probs = nt_dot(values, d_outs[g])
        d_scores = (probs * (d_probs - deltas[g]) * score_scale).astype(bf16)
        d_value_now = nn_dot(probs.astype(bf16), d_outs[g])
        d_key_now = nn_dot(d_scores, queries[g])
        d_value = d_value_now if g == 0 else d_value + d_value_now
        d_key = d_key_now if g == 0 else d_key + d_key_now
        turned[g] = turned[g] + tn_dot(keys, d_scores)
    return d_key, d_value


def attend_back_tail_kernel(
    q_ref, k_ref, v_ref, bounds_ref, total_ref, attn_ref, d_proj_ref, w_ref,
    d_out_ref, turned_ref, delta_ref, d_kv_ref, dk_ref, dv_ref
):
    d_out_ref[...] = nn_dot(d_proj_ref[...], w_ref[...]).astype(bf16)
    for block in range(q_ref.shape[0] // QROWS):
        here = slice(block * QROWS, (block + 1) * QROWS)
        shares = [1.0 / total_ref[g : g + 1, here] for g in range(GROUP)]
        queries = [q_ref[here, head_span(g)] for g in range(GROUP)]
        d_outs = [d_out_ref[here, head_span(g)] for g in range(GROUP)]
        deltas = []
        for g in range(GROUP):
            product = d_outs[g].astype(f32) * attn_ref[here, head_span(g)].astype(f32)
            deltas.append(jnp.sum(product.T, axis=0, keepdims=True))
            delta_ref[g : g + 1, here] = deltas[g]
        turned = [jnp.zeros((HEAD_WIDTH, QROWS), f32) for g in range(GROUP)]
        for chunk in range(0, max(TAIL_CHUNKS - block, 0)):
            there = slice((block + chunk) * QROWS, (block + chunk + 1) * QROWS)
            mask = chunk_mask(bounds_ref[block, 0:1, :], bounds_ref[block, 1:2, :], chunk)
            d_key, d_value = chunk_backward(
                k_ref[there, :], v_ref[there, :], queries, d_outs, mask, shares, deltas, turned
            )
            if block == 0:
                dk_ref[there, :] = d_key
                dv_ref[there, :] = d_value
            else:
                dk_ref[there, :] += d_key
                dv_ref[there, :] += d_value
        for g in range(GROUP):
            turned_ref[head_span(g), here] = turned[g]
    d_kv_ref[0] = dk_ref[...].astype(bf16)
    d_kv_ref[1] = dv_ref[...].astype(bf16)


def attend_back_own_kernel(
    q_ref, k_ref, v_ref, bounds_ref, total_ref, d_out_ref, turned_ref, delta_ref, dq_ref, d_kv_ref
):
    for block in range(q_ref.shape[0] // QROWS):
        here = slice(block * QROWS, (block + 1) * QROWS)
        shares = [1.0 / total_ref[g : g + 1, here] for g in range(GROUP)]
        queries = [q_ref[here, head_span(g)] for g in range(GROUP)]
        d_outs = [d_out_ref[here, head_span(g)] for g in range(GROUP)]
        deltas = [delta_ref[g : g + 1, here] for g in range(GROUP)]
        turned = [turned_ref[head_span(g), here] for g in range(GROUP)]
        for chunk in range(max(TAIL_CHUNKS - block, 0), TAIL_CHUNKS + 1):
            row = (block + chunk - TAIL_CHUNKS) * QROWS
            there = slice(row, row + QROWS)
            mask = chunk_mask(bounds_ref[block, 0:1, :], bounds_ref[block, 1:2, :], chunk)
            d_key, d_value = chunk_backward(
                k_ref[there, :], v_ref[there, :], queries, d_outs, mask, shares, deltas, turned
            )
            if chunk == TAIL_CHUNKS:
                d_kv_ref[0, there, :] = d_key
                d_kv_ref[1, there, :] = d_value
            else:
                d_kv_ref[0, there, :] += d_key
                d_kv_ref[1, there, :] += d_value
        for g in range(GROUP):
            dq_ref[here, head_span(g)] = turned[g].T.astype(bf16)


def attend_back_tail(
    queries, kv_tail, bounds, totals, attn, d_proj, attn_w, attn_cols, after=()
):
    rows, q_cols = queries.shape
    width = attn_w.shape[0]
    kv_heads = kv_tail.shape[1] // (2 * HEAD_WIDTH)
    blocks = rows // QROWS
    wide = GROUP * HEAD_WIDTH
    pairs = chunk_pairs(sum(max(TAIL_CHUNKS - b, 0) for b in range(blocks)), kv_heads)
    head_spec = pl.BlockSpec((rows, wide), lambda j: (0, j))
    row_spec = pl.BlockSpec((None, 8, rows), lambda j: (j, 0, 0))
    return call(
        attend_back_tail_kernel,
        (queries, kv_tail, kv_tail, bounds, totals, attn, d_proj, attn_w),
        grid=(kv_heads,),
        in_specs=[
            head_spec,
            pl.BlockSpec((WINDOW_TOKENS, HEAD_WIDTH), lambda j: (0, j)),
            pl.BlockSpec((WINDOW_TOKENS, HEAD_WIDTH), lambda j: (0, kv_heads + j)),
            pl.BlockSpec((blocks, 8, QROWS), lambda j: (0, 0, 0)),
            row_spec,
            head_spec,
            pl.BlockSpec((rows, width), lambda j: (0, 0)),
            pl.BlockSpec((width, wide), lambda j: (0, attn_cols // wide + j)),
        ],
        out_specs=[
            head_spec,
            pl.BlockSpec((wide, rows), lambda j: (j, 0)),
            row_spec,
            pl.BlockSpec((2, WINDOW_TOKENS, HEAD_WIDTH), lambda j: (0, 0, j)),
        ],
        scratch=[pltpu.VMEM((WINDOW_TOKENS, HEAD_WIDTH), f32)] * 2,
        out_shape=[
            shape_of((rows, q_cols), bf16),
            shape_of((kv_heads * wide, rows), f32),
            shape_of((kv_heads, 8, rows), f32),
            shape_of((2, WINDOW_TOKENS, kv_heads * HEAD_WIDTH), bf16),
        ],
        mib=40,
        estimate=cost(10 * pairs * HEAD_WIDTH + 2 * rows * width * q_cols, 8 << 20, pairs),
        name="attend_back_tail",
        after=after,
    )


def attend_back_own(queries, kv_own, bounds, totals, d_outs, turned, deltas, after=()):
    rows, q_cols = queries.shape
    kv_heads = kv_own.shape[1] // (2 * HEAD_WIDTH)
    blocks = rows // QROWS
    wide = GROUP * HEAD_WIDTH
    pairs = chunk_pairs(sum(min(b, TAIL_CHUNKS) + 1 for b in range(blocks)), kv_heads)
    head_spec = pl.BlockSpec((rows, wide), lambda j: (0, j))
    row_spec = pl.BlockSpec((None, 8, rows), lambda j: (j, 0, 0))
    return call(
        attend_back_own_kernel,
        (queries, kv_own, kv_own, bounds, totals, d_outs, turned, deltas),
        grid=(kv_heads,),
        in_specs=[
            head_spec,
            pl.BlockSpec((rows, HEAD_WIDTH), lambda j: (0, j)),
            pl.BlockSpec((rows, HEAD_WIDTH), lambda j: (0, kv_heads + j)),
            pl.BlockSpec((blocks, 8, QROWS), lambda j: (0, 0, 0)),
            row_spec,
            head_spec,
            pl.BlockSpec((wide, rows), lambda j: (j, 0)),
            row_spec,
        ],
        out_specs=[
            head_spec,
            pl.BlockSpec((2, rows, HEAD_WIDTH), lambda j: (0, 0, j)),
        ],
        out_shape=[
            shape_of((rows, q_cols), bf16),
            shape_of((2, rows, kv_heads * HEAD_WIDTH), f32),
        ],
        mib=40,
        estimate=cost(10 * pairs * HEAD_WIDTH, 8 << 20, pairs, scale=1),
        name="attend_back_own",
        after=after,
    )


def mid_norm_kernel(x_ref, gain_ref, *refs):
    middle = x_ref[...].astype(f32)
    for ref in refs[:-2]:
        middle = middle + ref[...].astype(f32)
    refs[-2][...] = middle
    refs[-1][...] = (middle * norm_stats(middle) * gain_ref[...]).astype(bf16)


def mid_norm(hidden, gain, terms, after=()):
    rows, cols = hidden.shape
    spec = pl.BlockSpec((rows // 4, cols), lambda i: (i, 0))
    return call(
        mid_norm_kernel,
        (hidden, gain, *terms),
        grid=(4,),
        in_specs=[spec, pl.BlockSpec((1, cols), lambda i: (0, 0))] + [spec] * len(terms),
        out_specs=[spec, spec],
        out_shape=[shape_of((rows, cols), f32), shape_of((rows, cols), bf16)],
        estimate=cost(20 * rows * cols, 20 * rows * cols),
        name="mid_norm",
        after=after,
    )


def mid_back_kernel(own_ref, got_ref, middle_ref, grad_ref, gain_ref, out_ref, low_ref, sum_ref):
    @pl.when(pl.program_id(0) == 0)
    def clear():
        sum_ref[...] = jnp.zeros_like(sum_ref)

    d_normed = own_ref[...] + got_ref[...].astype(f32)
    middle = middle_ref[...]
    stats = norm_stats(middle)
    sum_ref[0:1, :] += jnp.sum(d_normed * (middle * stats), axis=0, keepdims=True)
    d_middle = grad_ref[...].astype(f32) + norm_back(d_normed, middle, stats, gain_ref[...])
    out_ref[...] = d_middle
    low_ref[...] = d_middle.astype(bf16)


def mid_back(own, got, middle, out_grad, gain, after=()):
    rows, cols = own.shape
    spec = pl.BlockSpec((rows // 4, cols), lambda i: (i, 0))
    return call(
        mid_back_kernel,
        (own, got, middle, out_grad, gain),
        grid=(4,),
        in_specs=[spec] * 4 + [pl.BlockSpec((1, cols), lambda i: (0, 0))],
        out_specs=[spec, spec, pl.BlockSpec((8, cols), lambda i: (0, 0))],
        out_shape=[
            shape_of((rows, cols), f32),
            shape_of((rows, cols), bf16),
            shape_of((8, cols), f32),
        ],
        estimate=cost(30 * rows * cols, 20 * rows * cols),
        name="mid_back",
        after=after,
    )


def mlp_kernel(
    x_own_ref, x_got_ref, g_own_ref, g_got_ref, wg_ref, wu_ref, wd_ref,
    mixed_ref, d_gate_ref, d_up_ref, d_mid_ref, d_mid_give_ref, out_ref, out_give_ref,
    x_ref, g_ref, d_mid_acc, out_acc
):
    step = pl.program_id(0)
    tokens = x_own_ref.shape[0]

    @pl.when(step == 0)
    def start():
        x_ref[:tokens, :] = x_own_ref[...]
        x_ref[tokens:, :] = x_got_ref[...]
        g_ref[:tokens, :] = g_own_ref[...]
        g_ref[tokens:, :] = g_got_ref[...]
        d_mid_acc[...] = jnp.zeros_like(d_mid_acc)
        out_acc[...] = jnp.zeros_like(out_acc)

    gate = nn_dot(x_ref[...], wg_ref[...])
    up = nn_dot(x_ref[...], wu_ref[...])
    d_mixed = nn_dot(g_ref[...], wd_ref[...])
    sig = 1.0 / (1.0 + jnp.exp(-gate))
    gated = gate * sig
    mixed = (gated * up).astype(bf16)
    d_gate = (d_mixed * up * sig * (1.0 + gate * (1.0 - sig))).astype(bf16)
    d_up = (d_mixed * gated).astype(bf16)
    mixed_ref[...] = mixed
    d_gate_ref[...] = d_gate
    d_up_ref[...] = d_up
    d_mid_acc[...] += nt_dot(d_gate, wg_ref[...]) + nt_dot(d_up, wu_ref[...])
    out_acc[...] += nt_dot(mixed, wd_ref[...])

    @pl.when(step == pl.num_programs(0) - 1)
    def finish():
        d_mid_ref[...] = d_mid_acc[:tokens, :]
        d_mid_give_ref[...] = d_mid_acc[tokens:, :].astype(bf16)
        out_ref[...] = out_acc[:tokens, :]
        out_give_ref[...] = out_acc[tokens:, :].astype(bf16)


def mlp(x_own, x_got, g_own, g_got, mlp_w, after=()):
    tokens, width = x_own.shape
    units = mlp_w.shape[1] // 3
    tile = 512
    steps = units // tile
    fixed = lambda j: (0, 0)
    rows_spec = pl.BlockSpec((tokens, width), fixed)
    tile_spec = pl.BlockSpec((2 * tokens, tile), lambda j: (0, j))
    tile_shape = shape_of((2 * tokens, units), bf16)
    return call(
        mlp_kernel,
        (x_own, x_got, g_own, g_got, mlp_w, mlp_w, mlp_w,),
        grid=(steps,),
        in_specs=[rows_spec] * 4
        + [
            pl.BlockSpec((width, tile), lambda j: (0, j)),
            pl.BlockSpec((width, tile), lambda j: (0, steps + j)),
            pl.BlockSpec((width, tile), lambda j: (0, 2 * steps + j)),
        ],
        out_specs=[tile_spec] * 3 + [rows_spec] * 4,
        out_shape=[tile_shape] * 3
        + [
            shape_of((tokens, width), f32),
            shape_of((tokens, width), bf16),
            shape_of((tokens, width), f32),
            shape_of((tokens, width), bf16),
        ],
        scratch=[
            pltpu.VMEM((2 * tokens, width), bf16),
            pltpu.VMEM((2 * tokens, width), bf16),
            pltpu.VMEM((2 * tokens, width), f32),
            pltpu.VMEM((2 * tokens, width), f32),
        ],
        mib=48,
        estimate=cost(12 * 2 * tokens * width * units, 16 << 20),
        name="mlp",
        after=after,
    )


def mlp_grad_kernel(own_ref, got_ref, d_ref, out_ref, turned_ref):
    tokens = own_ref.shape[0]

    @pl.when(pl.program_id(0) == 0)
    def start():
        turned_ref[:, :tokens] = own_ref[...].T
        turned_ref[:, tokens:] = got_ref[...].T

    out_ref[...] = nn_dot(turned_ref[...], d_ref[...]).astype(bf16)


def mlp_grad(own, got, d_units, after=()):
    tokens, width = own.shape
    units = d_units.shape[1]
    tile = 512
    fixed = lambda j: (0, 0)
    return call(
        mlp_grad_kernel,
        (own, got, d_units,),
        grid=(units // tile,),
        in_specs=[
            pl.BlockSpec((tokens, width), fixed),
            pl.BlockSpec((tokens, width), fixed),
            pl.BlockSpec((2 * tokens, tile), lambda j: (0, j)),
        ],
        out_specs=pl.BlockSpec((width, tile), lambda j: (0, j)),
        out_shape=shape_of((width, units), bf16),
        scratch=[pltpu.VMEM((width, 2 * tokens), bf16)],
        mib=32,
        estimate=cost(4 * tokens * width * units, 8 << 20),
        name="mlp_grad",
        after=after,
    )


def mlp_grad_pair_kernel(
    steps, own_a_ref, got_a_ref, d_a_ref, own_b_ref, got_b_ref, d_b_ref, out_ref, turned_ref
):
    step = pl.program_id(0)
    tokens = own_a_ref.shape[0]

    @pl.when(step == 0)
    def first():
        turned_ref[:, :tokens] = own_a_ref[...].T
        turned_ref[:, tokens:] = got_a_ref[...].T

    @pl.when(step == steps)
    def second():
        turned_ref[:, :tokens] = own_b_ref[...].T
        turned_ref[:, tokens:] = got_b_ref[...].T

    @pl.when(step < steps)
    def left():
        out_ref[...] = nn_dot(turned_ref[...], d_a_ref[...]).astype(bf16)

    @pl.when(step >= steps)
    def right():
        out_ref[...] = nn_dot(turned_ref[...], d_b_ref[...]).astype(bf16)


def mlp_grad_pair(own_a, got_a, d_a, own_b, got_b, d_b, after=()):
    tokens, width = own_a.shape
    units = d_a.shape[1]
    tile = 512
    steps = units // tile
    rows = pl.BlockSpec((tokens, width), lambda j: (0, 0))
    return call(
        functools.partial(mlp_grad_pair_kernel, steps),
        (own_a, got_a, d_a, own_b, got_b, d_b),
        grid=(2 * steps,),
        in_specs=[
            rows,
            rows,
            pl.BlockSpec((2 * tokens, tile), lambda j: (0, jnp.minimum(j, steps - 1))),
            rows,
            rows,
            pl.BlockSpec((2 * tokens, tile), lambda j: (0, jnp.maximum(j - steps, 0))),
        ],
        out_specs=pl.BlockSpec((width, tile), lambda j: (0, j)),
        scratch=[pltpu.VMEM((width, 2 * tokens), bf16)],
        out_shape=shape_of((width, 2 * units), bf16),
        mib=48,
        estimate=cost(8 * tokens * width * units, 16 << 20),
        name="mlp_grad_pair",
        after=after,
    )


def body(
    hidden_in,
    doc_lengths,
    pad_lengths,
    w_query,
    key_matrix,
    value_matrix,
    w_output,
    w_gate,
    w_up,
    w_down,
    attn_gain,
    mlp_gain,
    query_gain,
    key_gain,
    out_grad,
):
    core = lax.axis_index("c")
    chip = lax.axis_index("q")
    chips = lax.axis_size("q")
    group = chip * 2 + core
    part = lax.axis_index("seq")
    groups = chips * 2
    parts = lax.axis_size("seq")
    tokens, width = hidden_in.shape
    group_rows = tokens * parts
    slice_rows = width // groups
    units = FEEDFWD_UNITS // 2
    q_cols = QUERY_HEADS * HEAD_WIDTH // parts
    kv_cols = KEY_VALUE_HEADS * HEAD_WIDTH // parts
    attn_cols = q_cols + 2 * kv_cols
    pack_cols = attn_cols + q_cols
    core_at = core.astype(jnp.int32).reshape(1)
    part_at = part.astype(jnp.int32).reshape(1)

    def swapped(value):
        return lax.ppermute(value, "c", core_swap)

    def sent(value, shift):
        return lax.ppermute(value, "seq", [(i, (i + shift) % parts) for i in range(parts)])

    def from_all(value):
        return [value] + [sent(value, shift) for shift in range(1, parts)]

    hidden_blocks = from_all(hidden_in)

    packed = pack_attn(
        part_at, parts, w_query, key_matrix, value_matrix, w_output,
        (attn_gain, mlp_gain, query_gain, key_gain),
    )
    attn_w = lax.all_gather(packed, dp_axes, axis=0, tiled=True)

    mlp_pack, mlp_give = pack_mlp(core_at, w_gate, w_up, w_down, after=(packed,))
    mlp_pack = lax.dynamic_update_slice_in_dim(
        mlp_pack, swapped(mlp_give), (1 - core) * slice_rows, 0
    )
    mlp_w = lax.all_gather(mlp_pack, "q", axis=0, tiled=True)
    grad_spread = jnp.where(
        (jnp.arange(2) == core)[:, None, None], jnp.zeros((), bf16), out_grad[None]
    )
    grad_got = lax.psum_scatter(grad_spread, "c", scatter_dimension=0, tiled=True)
    grad_got = grad_got.reshape(tokens, width)

    gains = read_gains(attn_w, pack_cols)
    head_piece = query_gain.shape[0]
    ga = gains[0:1]
    gm = gains[1:2]
    gqk = gains[2:4].reshape(2, groups, slice_rows)[:, :, :head_piece].reshape(2, HEAD_WIDTH)

    doc_ends = jnp.cumsum(doc_lengths)
    doc_starts = doc_ends - doc_lengths
    pad_starts = doc_ends - pad_lengths
    first = group * group_rows
    token = first + jnp.arange(group_rows, dtype=jnp.int32)
    inside = (token[:, None] >= doc_starts[None, :]) & (token[:, None] < doc_ends[None, :])
    start = jnp.sum(jnp.where(inside, doc_starts[None, :], 0), axis=1)
    pad_start = jnp.sum(jnp.where(inside, pad_starts[None, :], 0), axis=1)
    inv_freq = rope_base ** (-jnp.arange(HEAD_WIDTH // 2, dtype=f32) * 2.0 / HEAD_WIDTH)
    angles = (token - start).astype(f32)[:, None] * inv_freq[None, :]
    cosine = jnp.cos(angles)
    sine = jnp.sin(angles)
    cosine = jnp.concatenate([cosine, cosine], axis=1)
    sine = jnp.concatenate([-sine, sine], axis=1)
    offset = (token // QROWS) * QROWS - WINDOW_TOKENS
    low = jnp.maximum(start, token - (WINDOW_TOKENS - 1)) - offset
    high = jnp.minimum(token, pad_start - 1) - offset
    bounds = jnp.pad(
        jnp.stack([low.reshape(parts, QROWS), high.reshape(parts, QROWS)], axis=1),
        ((0, 0), (0, 6), (0, 0)),
    )

    normed_all, queries, kv_own, qk_proj = project(
        part_at, hidden_blocks, attn_w, ga, gqk, cosine, sine, q_cols, kv_cols
    )
    kv_tail = lax.ppermute(
        kv_own[group_rows - WINDOW_TOKENS :], dp_axes, [(i, i + 1) for i in range(groups - 1)]
    )
    own_outs, own_totals = attend_own(queries, kv_own, bounds)
    terms = []
    attn = [None] * parts
    totals = [None] * parts
    order = [shift for shift in range(1, parts)] + [0]
    for shift in order:
        attn[shift], totals[shift], term = attend_tail(
            shift, part_at, parts, queries, kv_tail, bounds, own_outs, own_totals, attn_w, attn_cols
        )
        terms.append(sent(term, shift) if shift else term)
    attn_all = jnp.zeros((group_rows, q_cols), bf16)
    totals_all = jnp.zeros((kv_cols // HEAD_WIDTH, 8, group_rows), f32)
    for shift in range(parts):
        row = (part + shift) % parts * tokens
        attn_all = lax.dynamic_update_slice_in_dim(attn_all, attn[shift], row, 0)
        totals_all = lax.dynamic_update_slice_in_dim(totals_all, totals[shift], row, 2)
    middle, normed_mid = mid_norm(hidden_in, gm, terms)

    mid_got = swapped(normed_mid)
    mixed, d_gate, d_up, d_mid, d_mid_give, out_part, out_give = mlp(
        normed_mid, mid_got, out_grad, grad_got, mlp_w
    )
    d_middle, d_proj, mlp_gain_rows = mid_back(
        d_mid, swapped(d_mid_give), middle, out_grad, gm
    )
    term_pair = mlp_grad_pair(
        out_grad, grad_got, mixed, normed_mid, mid_got, d_gate, after=(d_proj,)
    )
    d_proj_all = lax.all_gather(d_proj, "seq", axis=0, tiled=True)
    output_act = (middle + out_part + swapped(out_give).astype(f32)).astype(bf16)

    def chip_sums(grad):
        return lax.psum_scatter(grad, "q", scatter_dimension=0, tiled=True)

    own_pair = chip_sums(term_pair)
    term_up = mlp_grad(normed_mid, mid_got, d_up, after=(d_proj,))
    own_up = chip_sums(term_up)
    line = list(range(parts))

    def unpacked(sums, column, turned, after=()):
        give = lax.dynamic_slice(
            sums, ((1 - core) * slice_rows, column * units), (slice_rows, units)
        )
        return unpack_half(core_at, sums, swapped(give), column, turned, after=after)

    d_attn, turned, deltas, d_tail = attend_back_tail(
        queries, kv_tail, bounds, totals_all, attn_all, d_proj_all, attn_w, attn_cols,
        after=(term_up,),
    )
    d_tail = lax.ppermute(d_tail, dp_axes, [(i + 1, i) for i in range(groups - 1)])
    d_queries, d_kv = attend_back_own(
        queries, kv_own, bounds, totals_all, d_attn, turned, deltas
    )
    own_pair = touch(own_pair, after=(d_attn,))
    sum_pair = lax.psum(own_pair, "seq")
    w_out_grad = out_grad_sums([d_proj_all], [attn_all], after=(d_queries,))
    d_in, attn_term = project_back(
        part_at, groups, [hidden_blocks[(parts - k) % parts] for k in range(parts)],
        d_queries, d_kv, d_tail, qk_proj, attn_w, gqk, cosine, sine, normed_all, w_out_grad,
        mlp_gain_rows,
    )
    d_in = lax.psum_scatter(d_in, "seq", scatter_dimension=0, tiled=True)

    attn_grad = lax.psum_scatter(attn_term, dp_axes, scatter_dimension=0, tiled=True)
    give = lax.dynamic_slice_in_dim(own_up, (1 - core) * slice_rows, slice_rows, 0)
    own_up = join_halves(core_at, own_up, swapped(give), after=(sum_pair,))
    sum_up = lax.psum(own_up, "seq", axis_index_groups=[line[::-1]])
    grad_down = unpacked(sum_pair, 0, True)
    grad_gate = unpacked(sum_pair, 1, False, after=(grad_down,))
    attn_grad = touch(attn_grad, after=(grad_gate, sum_up))
    attn_grads = lax.all_gather(attn_grad, "seq", axis=0)
    in_grad = finish_in(d_in, d_middle, hidden_in, ga)
    grad_up = widened(sum_up, after=(in_grad,))
    gain_sums = jnp.sum(attn_grads[:, :, pack_cols : pack_cols + 4].astype(f32), axis=0)
    grad_query, grad_key, grad_value, grad_output = unpack_attn(
        attn_grads, q_cols, kv_cols, after=(grad_up,)
    )
    return (
        output_act,
        in_grad,
        grad_query,
        grad_key,
        grad_value,
        grad_output,
        grad_gate,
        grad_up,
        grad_down,
        gain_sums[:, 0],
        gain_sums[:, 1],
        gain_sums[:head_piece, 2],
        gain_sums[:head_piece, 3],
    )


def solution(mesh):
    groups, parts = mesh.devices.shape
    mesh = Mesh(mesh.devices.reshape(groups // 2, 2, parts), ("q", "c", "seq"))
    tokens = P(("q", "c", "seq"), None)
    rows = P(dp_axes, None)
    cols = P(None, dp_axes)
    flat = P(dp_axes)
    in_specs = (
        tokens, P(), P(), rows, rows, rows, cols, rows, rows, cols, flat, flat, flat, flat, tokens,
    )
    out_specs = (
        tokens, tokens, rows, rows, rows, cols, rows, rows, cols, flat, flat, flat, flat,
    )
    return jax.shard_map(body, mesh=mesh, in_specs=in_specs, out_specs=out_specs, check_vma=False)
```

```python
import functools

import jax
import jax.numpy as jnp
from jax import lax
from jax.experimental import pallas as pl
from jax.experimental.pallas import tpu as pltpu
from jax.sharding import Mesh, PartitionSpec as P

QUERY_HEADS = 16
KEY_VALUE_HEADS = 8
HEAD_WIDTH = 128
FEEDFWD_UNITS = 3072
WINDOW_TOKENS = 1024
QROWS = 256
GROUP = QUERY_HEADS // KEY_VALUE_HEADS
TAIL_CHUNKS = WINDOW_TOKENS // QROWS

norm_eps = 1e-06
rope_base = 1000000.0
score_scale = HEAD_WIDTH**-0.5
log2_e = 1.4426950408889634
bf16 = jnp.bfloat16
f32 = jnp.float32
dp_axes = ("q", "c")
core_swap = [(0, 1), (1, 0)]


def nt_dot(left, right):
    return lax.dot_general(left, right, (((1,), (1,)), ((), ())), preferred_element_type=f32)


def tn_dot(left, right):
    return lax.dot_general(left, right, (((0,), (0,)), ((), ())), preferred_element_type=f32)


def nn_dot(left, right):
    return jnp.dot(left, right, preferred_element_type=f32)


def shape_of(dims, kind):
    return jax.ShapeDtypeStruct(dims, kind)


def call(
    kernel, args, *, grid, in_specs, out_specs, out_shape, name, estimate, prefetch=0, scratch=(),
    mib=32, after=()
):
    count = prefetch + len(in_specs)

    def body_of(*refs):
        kernel(*refs[:count], *refs[count + len(after) :])

    return pl.pallas_call(
        body_of,
        grid_spec=pltpu.PrefetchScalarGridSpec(
            num_scalar_prefetch=prefetch,
            grid=grid,
            in_specs=list(in_specs) + [pl.BlockSpec(memory_space=pl.ANY)] * len(after),
            out_specs=out_specs,
            scratch_shapes=list(scratch),
        ),
        out_shape=out_shape,
        compiler_params=pltpu.CompilerParams(vmem_limit_bytes=mib << 20),
        cost_estimate=estimate,
        name=name,
    )(*args, *after)


def cost(flops, moved, exps=0, scale=100):
    flops, moved, exps = flops * scale, moved * scale, exps * scale
    return pl.CostEstimate(flops=int(flops), bytes_accessed=int(moved), transcendentals=int(exps))


def norm_stats(rows):
    return lax.rsqrt(jnp.mean(rows * rows, axis=-1, keepdims=True) + norm_eps)


def norm_back(d_normed, rows, stats, gains):
    scaled = d_normed * gains
    unit = rows * stats
    return stats * (scaled - unit * jnp.mean(scaled * unit, axis=-1, keepdims=True))


def pack_attn_kernel(
    part_ref, wq_ref, wk_ref, wv_ref, wo_ref, ga_ref, gm_ref, gq_ref, gk_ref, out_ref, gains_ref
):
    gains_ref[...] = jnp.zeros_like(gains_ref)
    for row, gain_ref in enumerate((ga_ref, gm_ref, gq_ref, gk_ref)):
        gains_ref[row : row + 1, : gain_ref.shape[1]] = gain_ref[...]
    column = 0
    for piece in (
        wq_ref[...].astype(bf16),
        wk_ref[...].astype(bf16),
        wv_ref[...].astype(bf16),
        wo_ref[...].T.astype(bf16),
    ):
        out_ref[:, column : column + piece.shape[1]] = piece
        column += piece.shape[1]
    gains = gains_ref[...].T
    rest = jnp.zeros((gains.shape[0], HEAD_WIDTH - gains.shape[1]), f32)
    out_ref[:, column:] = jnp.concatenate([gains, rest], axis=1).astype(bf16)


def pack_attn(part, parts, w_query, key_matrix, value_matrix, w_output, gains, after=()):
    gains = [gain[None] for gain in gains]
    rows = w_query.shape[0]
    q_cols = w_query.shape[1] // parts
    kv_cols = key_matrix.shape[1] // parts
    total = 2 * q_cols + 2 * kv_cols + HEAD_WIDTH
    return call(
        pack_attn_kernel,
        (part, w_query, key_matrix, value_matrix, w_output, *gains),
        prefetch=1,
        grid=(1,),
        in_specs=[
            pl.BlockSpec((rows, q_cols), lambda i, p: (0, p[0])),
            pl.BlockSpec((rows, kv_cols), lambda i, p: (0, p[0])),
            pl.BlockSpec((rows, kv_cols), lambda i, p: (0, p[0])),
            pl.BlockSpec((q_cols, rows), lambda i, p: (p[0], 0)),
        ]
        + [pl.BlockSpec(gain.shape, lambda i, p: (0, 0)) for gain in gains],
        scratch=[pltpu.VMEM((8, rows), f32)],
        mib=60,
        out_specs=pl.BlockSpec((rows, total), lambda i, p: (0, 0)),
        out_shape=shape_of((rows, total), bf16),
        estimate=cost(0, rows * total * 6),
        name="pack_attn",
        after=after,
    )


def touch_kernel(in_ref, out_ref):
    out_ref[...] = in_ref[...]


def touch(value, after):
    rows, cols = value.shape
    spec = pl.BlockSpec((rows // 4, cols), lambda i: (i, 0))
    return call(
        touch_kernel,
        (value,),
        grid=(4,),
        in_specs=[spec],
        out_specs=spec,
        out_shape=shape_of((rows, cols), value.dtype),
        estimate=cost(0, 4 * rows * cols),
        name="touch",
        after=after,
    )


def finish_in_kernel(d_normed_ref, d_middle_ref, x_ref, gain_ref, out_ref):
    rows = x_ref[...].astype(f32)
    back = norm_back(d_normed_ref[...].astype(f32), rows, norm_stats(rows), gain_ref[...])
    out_ref[...] = (d_middle_ref[...] + back).astype(bf16)


def finish_in(d_normed, d_middle, hidden, gain, after=()):
    rows, cols = hidden.shape
    spec = pl.BlockSpec((rows // 4, cols), lambda i: (i, 0))
    return call(
        finish_in_kernel,
        (d_normed, d_middle, hidden, gain),
        grid=(4,),
        in_specs=[spec] * 3 + [pl.BlockSpec((1, cols), lambda i: (0, 0))],
        out_specs=spec,
        out_shape=shape_of((rows, cols), bf16),
        estimate=cost(20 * rows * cols, 12 * rows * cols, scale=1),
        name="finish_in",
        after=after,
    )


def read_gains_kernel(in_ref, out_ref):
    out_ref[...] = in_ref[...].astype(f32).T[:8, :]


def read_gains(attn_w, column, after=()):
    width = attn_w.shape[0]
    return call(
        read_gains_kernel,
        (attn_w,),
        grid=(1,),
        in_specs=[pl.BlockSpec((width, HEAD_WIDTH), lambda i: (0, column // HEAD_WIDTH))],
        out_specs=pl.BlockSpec((8, width), lambda i: (0, 0)),
        out_shape=shape_of((8, width), f32),
        estimate=cost(0, width * HEAD_WIDTH * 4),
        name="read_gains",
        after=after,
    )


def pack_mlp_kernel(core_ref, wg_ref, wu_ref, wd_ref, own_ref, give_ref):
    units = wg_ref.shape[1]

    def fill(out_ref):
        out_ref[:, :units] = wg_ref[...].astype(bf16)
        out_ref[:, units : 2 * units] = wu_ref[...].astype(bf16)
        out_ref[:, 2 * units :] = wd_ref[...].T.astype(bf16)

    @pl.when(pl.program_id(0) == 0)
    def first():
        fill(give_ref)

    @pl.when(pl.program_id(0) == 1)
    def second():
        fill(own_ref)


def pack_mlp(core, w_gate, w_up, w_down, after=()):
    rows = w_gate.shape[0]
    units = w_gate.shape[1] // 2
    half = lambda i, c: (c[0] + 1 - i) % 2
    return call(
        pack_mlp_kernel,
        (core, w_gate, w_up, w_down,),
        prefetch=1,
        grid=(2,),
        in_specs=[
            pl.BlockSpec((rows, units), lambda i, c: (0, half(i, c))),
            pl.BlockSpec((rows, units), lambda i, c: (0, half(i, c))),
            pl.BlockSpec((units, rows), lambda i, c: (half(i, c), 0)),
        ],
        out_specs=[
            pl.BlockSpec((rows, 3 * units), lambda i, c: (c[0], 0)),
            pl.BlockSpec((rows, 3 * units), lambda i, c: (0, 0)),
        ],
        out_shape=[shape_of((2 * rows, 3 * units), bf16), shape_of((rows, 3 * units), bf16)],
        estimate=cost(0, rows * units * 36),
        name="pack_mlp",
        after=after,
    )


def unpack_half_kernel(turned, core_ref, own_ref, got_ref, out_ref):
    def fill(in_ref):
        rows = in_ref[...].astype(f32)
        out_ref[...] = rows.T if turned else rows

    @pl.when(pl.program_id(0) == 0)
    def first():
        fill(own_ref)

    @pl.when(pl.program_id(0) == 1)
    def second():
        fill(got_ref)


def unpack_half(core, sums, got, column, turned, after=()):
    rows, units = got.shape
    half = lambda i, c: (c[0] + i) % 2
    if turned:
        out_spec = pl.BlockSpec((units, rows), lambda i, c: (half(i, c), 0))
        out_shape = shape_of((2 * units, rows), f32)
    else:
        out_spec = pl.BlockSpec((rows, units), lambda i, c: (0, half(i, c)))
        out_shape = shape_of((rows, 2 * units), f32)
    return call(
        functools.partial(unpack_half_kernel, turned),
        (core, sums, got,),
        prefetch=1,
        grid=(2,),
        in_specs=[
            pl.BlockSpec((rows, units), lambda i, c: (c[0], column)),
            pl.BlockSpec((rows, units), lambda i, c: (0, 0)),
        ],
        out_specs=out_spec,
        out_shape=out_shape,
        estimate=cost(0, rows * units * 12, scale=1),
        name="unpack_half",
        after=after,
    )


def join_halves_kernel(core_ref, own_ref, got_ref, out_ref):
    @pl.when(pl.program_id(0) == 0)
    def first():
        out_ref[...] = own_ref[...]

    @pl.when(pl.program_id(0) == 1)
    def second():
        out_ref[...] = got_ref[...]


def join_halves(core, sums, got, after=()):
    rows, units = got.shape
    return call(
        join_halves_kernel,
        (core, sums, got),
        prefetch=1,
        grid=(2,),
        in_specs=[
            pl.BlockSpec((rows, units), lambda i, c: (c[0], 0)),
            pl.BlockSpec((rows, units), lambda i, c: (0, 0)),
        ],
        out_specs=pl.BlockSpec((rows, units), lambda i, c: (0, (c[0] + i) % 2)),
        out_shape=shape_of((rows, 2 * units), bf16),
        estimate=cost(0, rows * units * 8, scale=1),
        name="join_halves",
        after=after,
    )


def widened_kernel(in_ref, out_ref):
    out_ref[...] = in_ref[...].astype(f32)


def widened(value, after=()):
    rows, cols = value.shape
    spec = pl.BlockSpec((rows, cols // 2), lambda i: (0, i))
    return call(
        widened_kernel,
        (value,),
        grid=(2,),
        in_specs=[spec],
        out_specs=spec,
        out_shape=shape_of((rows, cols), f32),
        estimate=cost(0, rows * cols * 6, scale=1),
        name="widened",
        after=after,
    )


def unpack_attn_kernel(in_ref, wq_ref, wk_ref, wv_ref, wo_ref):
    column = 0
    for out_ref in (wq_ref, wk_ref, wv_ref):
        count = out_ref.shape[1]
        out_ref[...] = in_ref[:, column : column + count].astype(f32)
        column += count
    wo_ref[...] = in_ref[:, column : column + wo_ref.shape[0]].astype(f32).T


def unpack_attn(gathered, q_cols, kv_cols, after=()):
    parts, rows, total = gathered.shape
    return call(
        unpack_attn_kernel,
        (gathered,),
        grid=(parts,),
        in_specs=[pl.BlockSpec((None, rows, total), lambda i: (i, 0, 0))],
        out_specs=[
            pl.BlockSpec((rows, q_cols), lambda i: (0, i)),
            pl.BlockSpec((rows, kv_cols), lambda i: (0, i)),
            pl.BlockSpec((rows, kv_cols), lambda i: (0, i)),
            pl.BlockSpec((q_cols, rows), lambda i: (i, 0)),
        ],
        out_shape=[
            shape_of((rows, parts * q_cols), f32),
            shape_of((rows, parts * kv_cols), f32),
            shape_of((rows, parts * kv_cols), f32),
            shape_of((parts * q_cols, rows), f32),
        ],
        estimate=cost(0, parts * rows * total * 6, scale=1),
        name="unpack_attn",
        after=after,
    )


def pick(refs, scratch):
    for k, ref in enumerate(refs):

        @pl.when(pl.program_id(0) == k)
        def take(ref=ref):
            scratch[...] = ref[...]


def turn(rows):
    half = HEAD_WIDTH // 2
    return jnp.concatenate([rows[:, half:], rows[:, :half]], axis=1)


def project_kernel(parts, q_cols, kv_cols, part_ref, *refs):
    blocks = refs[:parts]
    w_ref, ga_ref, gqk_ref, cos_ref, sin_ref, normed_ref, q_ref, kv_ref, proj_ref, x_ref = refs[parts:]
    pick(blocks, x_ref)
    rows = x_ref[...].astype(f32)
    normed = (rows * norm_stats(rows) * ga_ref[...]).astype(bf16)
    normed_ref[...] = normed
    cosine = cos_ref[...]
    sine = sin_ref[...]
    qk_cols = q_cols + kv_cols
    proj = nn_dot(normed, w_ref[...])
    proj_ref[...] = proj[:, :qk_cols]
    kv_ref[:, kv_cols:] = proj[:, qk_cols:].astype(bf16)
    for column in range(0, qk_cols, HEAD_WIDTH):
        head = proj[:, column : column + HEAD_WIDTH]
        gain = gqk_ref[0:1, :] if column < q_cols else gqk_ref[1:2, :]
        head = head * norm_stats(head) * gain
        head = (head * cosine + turn(head) * sine).astype(bf16)
        if column < q_cols:
            q_ref[:, column : column + HEAD_WIDTH] = head
        else:
            kv_ref[:, column - q_cols : column - q_cols + HEAD_WIDTH] = head


def project(part, blocks, attn_w, ga, gqk, cosine, sine, q_cols, kv_cols, after=()):
    parts = len(blocks)
    tokens, width = blocks[0].shape
    attn_cols = q_cols + 2 * kv_cols
    place = lambda k, p: ((p[0] + parts - k) % parts, 0)
    fixed = lambda k, p: (0, 0)
    rows = parts * tokens
    return call(
        functools.partial(project_kernel, parts, q_cols, kv_cols),
        (part, *blocks, attn_w, ga, gqk, cosine, sine,),
        prefetch=1,
        grid=(parts,),
        in_specs=[pl.BlockSpec((tokens, width), fixed)] * parts
        + [
            pl.BlockSpec((width, attn_cols), fixed),
            pl.BlockSpec((1, width), fixed),
            pl.BlockSpec((2, HEAD_WIDTH), fixed),
            pl.BlockSpec((tokens, HEAD_WIDTH), place),
            pl.BlockSpec((tokens, HEAD_WIDTH), place),
        ],
        out_specs=[
            pl.BlockSpec((tokens, width), place),
            pl.BlockSpec((tokens, q_cols), place),
            pl.BlockSpec((tokens, 2 * kv_cols), place),
            pl.BlockSpec((tokens, q_cols + kv_cols), place),
        ],
        scratch=[pltpu.VMEM((tokens, width), bf16)],
        out_shape=[
            shape_of((rows, width), bf16),
            shape_of((rows, q_cols), bf16),
            shape_of((rows, 2 * kv_cols), bf16),
            shape_of((rows, q_cols + kv_cols), f32),
        ],
        mib=32,
        estimate=cost(2 * rows * width * attn_cols, 12 << 20),
        name="project",
        after=after,
    )


def project_back_kernel(
    parts, groups, tail_from, q_cols, kv_cols, part_ref, *refs
):
    blocks = refs[:parts]
    (dq_ref, d_kv_ref, tail_ref, proj_ref, w_ref, gqk_ref, cos_ref, sin_ref, normed_ref,
     w_out_ref, mlp_gain_ref, out_ref, term_ref,
     x_ref, dqkv_ref, acc_ref, gain_ref, head_gain_ref) = refs[parts:]
    step = pl.program_id(0)
    block = (part_ref[0] + step) % parts
    pick(blocks, x_ref)

    @pl.when(step == 0)
    def clear():
        gain_ref[...] = jnp.zeros_like(gain_ref)
        head_gain_ref[...] = jnp.zeros_like(head_gain_ref)
        acc_ref[...] = jnp.zeros_like(acc_ref)

    cosine = cos_ref[...]
    sine = sin_ref[...]
    has_tail = jnp.where(block >= tail_from, 1.0, 0.0)
    dk = (d_kv_ref[0] + tail_ref[0].astype(f32) * has_tail).astype(bf16)
    dqkv_ref[:, q_cols + kv_cols :] = (
        d_kv_ref[1] + tail_ref[1].astype(f32) * has_tail
    ).astype(bf16)
    head_gains = [jnp.zeros((1, HEAD_WIDTH), f32) for _ in range(2)]
    for column in range(0, q_cols + kv_cols, HEAD_WIDTH):
        index = 0 if column < q_cols else 1
        if index == 0:
            d_head = dq_ref[:, column : column + HEAD_WIDTH].astype(f32)
        else:
            d_head = dk[:, column - q_cols : column - q_cols + HEAD_WIDTH].astype(f32)
        d_head = d_head * cosine + turn(d_head * sine)
        head = proj_ref[:, column : column + HEAD_WIDTH]
        stats = norm_stats(head)
        unit = head * stats
        head_gains[index] = head_gains[index] + jnp.sum(d_head * unit, axis=0, keepdims=True)
        scaled = d_head * gqk_ref[index : index + 1, :]
        d_proj = stats * (scaled - unit * jnp.mean(scaled * unit, axis=-1, keepdims=True))
        dqkv_ref[:, column : column + HEAD_WIDTH] = d_proj.astype(bf16)
    head_gain_ref[0:1, :] += head_gains[0]
    head_gain_ref[1:2, :] += head_gains[1]
    d_in = nt_dot(dqkv_ref[...], w_ref[...])
    rows = x_ref[...].astype(f32)
    gain_ref[0:1, :] += jnp.sum(d_in * (rows * norm_stats(rows)), axis=0, keepdims=True)
    out_ref[...] = d_in.astype(bf16)
    acc_ref[...] += tn_dot(normed_ref[...], dqkv_ref[...])

    @pl.when(step == parts - 1)
    def finish():
        attn_cols = acc_ref.shape[1]
        term_ref[:, :attn_cols] = acc_ref[...].astype(bf16)
        term_ref[:, attn_cols : attn_cols + q_cols] = w_out_ref[...]
        gain_ref[1:2, :] = mlp_gain_ref[0:1, :]
        piece = HEAD_WIDTH // groups
        slice_rows = gain_ref.shape[1] // groups
        for index in range(2):
            for group in range(groups):
                gain_ref[2 + index : 3 + index, group * slice_rows : group * slice_rows + piece] = (
                    head_gain_ref[index : index + 1, group * piece : (group + 1) * piece]
                )
        gains = gain_ref[...].T
        rest = jnp.zeros((gains.shape[0], HEAD_WIDTH - gains.shape[1]), f32)
        term_ref[:, attn_cols + q_cols :] = jnp.concatenate([gains, rest], axis=1).astype(bf16)


def project_back(
    part, groups, hidden, dq, d_kv, tail, proj, attn_w, gqk, cosine, sine, normed,
    w_out_grad, mlp_gain_rows, after=()
):
    parts = len(hidden)
    tokens, width = hidden[0].shape
    rows, q_cols = dq.shape
    kv_cols = d_kv.shape[2]
    attn_cols = q_cols + 2 * kv_cols
    tail_from = (rows - WINDOW_TOKENS) // tokens
    place = lambda k, p: ((p[0] + k) % parts, 0)
    kv_place = lambda k, p: (0, (p[0] + k) % parts, 0)
    tail_place = lambda k, p: (0, jnp.maximum((p[0] + k) % parts - tail_from, 0), 0)
    fixed = lambda k, p: (0, 0)
    total = attn_cols + q_cols + HEAD_WIDTH
    return call(
        functools.partial(project_back_kernel, parts, groups, tail_from, q_cols, kv_cols),
        (part, *hidden, dq, d_kv, tail, proj, attn_w, gqk, cosine, sine, normed, w_out_grad, mlp_gain_rows),
        prefetch=1,
        grid=(parts,),
        in_specs=[pl.BlockSpec((tokens, width), fixed)] * parts
        + [
            pl.BlockSpec((tokens, q_cols), place),
            pl.BlockSpec((2, tokens, kv_cols), kv_place),
            pl.BlockSpec((2, tokens, kv_cols), tail_place),
            pl.BlockSpec((tokens, q_cols + kv_cols), place),
            pl.BlockSpec((width, attn_cols), fixed),
            pl.BlockSpec((2, HEAD_WIDTH), fixed),
            pl.BlockSpec((tokens, HEAD_WIDTH), place),
            pl.BlockSpec((tokens, HEAD_WIDTH), place),
            pl.BlockSpec((tokens, width), place),
            pl.BlockSpec((width, q_cols), fixed),
            pl.BlockSpec((8, width), fixed),
        ],
        out_specs=[
            pl.BlockSpec((tokens, width), place),
            pl.BlockSpec((width, total), fixed),
        ],
        scratch=[
            pltpu.VMEM((tokens, width), bf16),
            pltpu.VMEM((tokens, attn_cols), bf16),
            pltpu.VMEM((width, attn_cols), f32),
            pltpu.VMEM((8, width), f32),
            pltpu.VMEM((8, HEAD_WIDTH), f32),
        ],
        mib=48,
        out_shape=[
            shape_of((rows, width), bf16),
            shape_of((width, total), bf16),
        ],
        estimate=cost(4 * rows * width * attn_cols, 16 << 20, scale=1),
        name="project_back",
        after=after,
    )


def out_grad_kernel(parts, *refs):
    d_projs = refs[:parts]
    attns = refs[parts : 2 * parts]
    out_ref = refs[2 * parts]
    total = None
    for d_proj, attn in zip(d_projs, attns):
        term = tn_dot(d_proj[...], attn[...])
        total = term if total is None else total + term
    out_ref[...] = total.astype(bf16)


def out_grad_sums(d_projs, attns, after=()):
    parts = len(attns)
    tokens, q_cols = attns[0].shape
    width = d_projs[0].shape[1]
    cols = width // 4
    return call(
        functools.partial(out_grad_kernel, parts),
        (*d_projs, *attns,),
        grid=(4,),
        in_specs=[pl.BlockSpec((tokens, cols), lambda i: (0, i))] * parts
        + [pl.BlockSpec((tokens, q_cols), lambda i: (0, 0))] * parts,
        out_specs=pl.BlockSpec((cols, q_cols), lambda i: (i, 0)),
        out_shape=shape_of((width, q_cols), bf16),
        mib=32,
        estimate=cost(2 * parts * tokens * width * q_cols, 4 << 20, scale=1),
        name="out_grad",
        after=after,
    )


def chunk_mask(low, high, chunk):
    key = lax.broadcasted_iota(jnp.int32, (QROWS, QROWS), 0) + chunk * QROWS
    mask = (key >= low) & (key <= high)
    if chunk == TAIL_CHUNKS:
        own = lax.broadcasted_iota(jnp.int32, (QROWS, QROWS), 1) + WINDOW_TOKENS
        mask = mask | (key == own)
    return mask


def head_span(g):
    return slice(g * HEAD_WIDTH, (g + 1) * HEAD_WIDTH)


def attend_own_kernel(q_ref, k_ref, v_ref, bounds_ref, out_ref, total_ref):
    for block in range(q_ref.shape[0] // QROWS):
        here = slice(block * QROWS, (block + 1) * QROWS)
        sums = [jnp.zeros((1, QROWS), f32) for g in range(GROUP)]
        outs = [jnp.zeros((HEAD_WIDTH, QROWS), f32) for g in range(GROUP)]
        for chunk in range(max(TAIL_CHUNKS - block, 0), TAIL_CHUNKS + 1):
            row = (block + chunk - TAIL_CHUNKS) * QROWS
            there = slice(row, row + QROWS)
            mask = chunk_mask(bounds_ref[block, 0:1, :], bounds_ref[block, 1:2, :], chunk)
            for g in range(GROUP):
                scores = nt_dot(k_ref[there, :], q_ref[here, head_span(g)])
                weights = jnp.where(mask, jnp.exp2(scores * (score_scale * log2_e)), 0.0)
                sums[g] = sums[g] + jnp.sum(weights, axis=0, keepdims=True)
                outs[g] = outs[g] + tn_dot(v_ref[there, :], weights.astype(bf16))
        for g in range(GROUP):
            out_ref[head_span(g), here] = outs[g]
            total_ref[g : g + 1, here] = sums[g]


def chunk_pairs(chunks, kv_heads):
    return chunks * kv_heads * GROUP * QROWS * QROWS


def attend_own(queries, kv_own, bounds, after=()):
    rows = queries.shape[0]
    kv_heads = kv_own.shape[1] // (2 * HEAD_WIDTH)
    blocks = rows // QROWS
    wide = GROUP * HEAD_WIDTH
    pairs = chunk_pairs(sum(min(b, TAIL_CHUNKS) + 1 for b in range(blocks)), kv_heads)
    return call(
        attend_own_kernel,
        (queries, kv_own, kv_own, bounds,),
        grid=(kv_heads,),
        in_specs=[
            pl.BlockSpec((rows, wide), lambda j: (0, j)),
            pl.BlockSpec((rows, HEAD_WIDTH), lambda j: (0, j)),
            pl.BlockSpec((rows, HEAD_WIDTH), lambda j: (0, kv_heads + j)),
            pl.BlockSpec((blocks, 8, QROWS), lambda j: (0, 0, 0)),
        ],
        out_specs=[
            pl.BlockSpec((wide, rows), lambda j: (j, 0)),
            pl.BlockSpec((None, 8, rows), lambda j: (j, 0, 0)),
        ],
        out_shape=[shape_of((kv_heads * wide, rows), f32), shape_of((kv_heads, 8, rows), f32)],
        mib=32,
        estimate=cost(4 * pairs * HEAD_WIDTH, 4 << 20, pairs),
        name="attend_own",
        after=after,
    )


def attend_tail_kernel(
    shift, parts, part_ref, q_ref, k_ref, v_ref, bounds_ref, own_ref, own_total_ref, w_ref,
    attn_ref, total_ref, proj_ref, out_ref, acc_ref
):
    block = (part_ref[0] + shift) % parts
    out_ref[...] = own_ref[...]
    total_ref[...] = own_total_ref[...]
    for chunk in range(TAIL_CHUNKS):

        @pl.when(block + chunk < TAIL_CHUNKS)
        def add(chunk=chunk):
            there = pl.ds(pl.multiple_of((block + chunk) * QROWS, QROWS), QROWS)
            keys = k_ref[there, :]
            values = v_ref[there, :]
            mask = chunk_mask(bounds_ref[0:1, :], bounds_ref[1:2, :], chunk)
            for g in range(GROUP):
                scores = nt_dot(keys, q_ref[:, head_span(g)])
                weights = jnp.where(mask, jnp.exp2(scores * (score_scale * log2_e)), 0.0)
                total_ref[g : g + 1, :] += jnp.sum(weights, axis=0, keepdims=True)
                out_ref[head_span(g), :] += tn_dot(values, weights.astype(bf16))

    for g in range(GROUP):
        share = 1.0 / total_ref[g : g + 1, :]
        attn_ref[:, head_span(g)] = (out_ref[head_span(g), :] * share).T.astype(bf16)
    term = nt_dot(attn_ref[...], w_ref[...])
    last = pl.num_programs(0) - 1

    @pl.when(pl.program_id(0) == 0)
    def start():
        acc_ref[...] = term

    @pl.when(pl.program_id(0) > 0)
    def add_up():
        acc_ref[...] += term

    @pl.when(pl.program_id(0) == last)
    def finish():
        proj_ref[...] = acc_ref[...].astype(bf16)


def attend_tail(shift, part, parts, queries, kv_tail, bounds, outs, totals, attn_w, attn_cols, after=()):
    q_cols = queries.shape[1]
    width = attn_w.shape[0]
    kv_heads = kv_tail.shape[1] // (2 * HEAD_WIDTH)
    wide = GROUP * HEAD_WIDTH
    at = lambda p: (p[0] + shift) % parts
    pairs = chunk_pairs(TAIL_CHUNKS // 2, kv_heads)
    return call(
        functools.partial(attend_tail_kernel, shift, parts),
        (part, queries, kv_tail, kv_tail, bounds, outs, totals, attn_w,),
        prefetch=1,
        grid=(kv_heads,),
        in_specs=[
            pl.BlockSpec((QROWS, wide), lambda j, p: (at(p), j)),
            pl.BlockSpec((WINDOW_TOKENS, HEAD_WIDTH), lambda j, p: (0, j)),
            pl.BlockSpec((WINDOW_TOKENS, HEAD_WIDTH), lambda j, p: (0, kv_heads + j)),
            pl.BlockSpec((None, 8, QROWS), lambda j, p: (at(p), 0, 0)),
            pl.BlockSpec((wide, QROWS), lambda j, p: (j, at(p))),
            pl.BlockSpec((None, 8, QROWS), lambda j, p: (j, 0, at(p))),
            pl.BlockSpec((width, wide), lambda j, p: (0, attn_cols // wide + j)),
        ],
        out_specs=[
            pl.BlockSpec((QROWS, wide), lambda j, p: (0, j)),
            pl.BlockSpec((None, 8, QROWS), lambda j, p: (j, 0, 0)),
            pl.BlockSpec((QROWS, width), lambda j, p: (0, 0)),
        ],
        scratch=[pltpu.VMEM((wide, QROWS), f32), pltpu.VMEM((QROWS, width), f32)],
        out_shape=[
            shape_of((QROWS, q_cols), bf16),
            shape_of((kv_heads, 8, QROWS), f32),
            shape_of((QROWS, width), bf16),
        ],
        mib=32,
        estimate=cost(
            4 * pairs * HEAD_WIDTH + 2 * QROWS * width * q_cols, 4 << 20, pairs
        ),
        name="attend_tail",
        after=after,
    )


def chunk_backward(keys, values, queries, d_outs, mask, shares, deltas, turned):
    d_key = None
    d_value = None
    for g in range(GROUP):
        scores = nt_dot(keys, queries[g])
        probs = jnp.where(mask, jnp.exp2(scores * (score_scale * log2_e)) * shares[g], 0.0)
        d_probs = nt_dot(values, d_outs[g])
        d_scores = (probs * (d_probs - deltas[g]) * score_scale).astype(bf16)
        d_value_now = nn_dot(probs.astype(bf16), d_outs[g])
        d_key_now = nn_dot(d_scores, queries[g])
        d_value = d_value_now if g == 0 else d_value + d_value_now
        d_key = d_key_now if g == 0 else d_key + d_key_now
        turned[g] = turned[g] + tn_dot(keys, d_scores)
    return d_key, d_value


def attend_back_tail_kernel(
    q_ref, k_ref, v_ref, bounds_ref, total_ref, attn_ref, d_proj_ref, w_ref,
    d_out_ref, turned_ref, delta_ref, d_kv_ref, dk_ref, dv_ref
):
    d_out_ref[...] = nn_dot(d_proj_ref[...], w_ref[...]).astype(bf16)
    for block in range(q_ref.shape[0] // QROWS):
        here = slice(block * QROWS, (block + 1) * QROWS)
        shares = [1.0 / total_ref[g : g + 1, here] for g in range(GROUP)]
        queries = [q_ref[here, head_span(g)] for g in range(GROUP)]
        d_outs = [d_out_ref[here, head_span(g)] for g in range(GROUP)]
        deltas = []
        for g in range(GROUP):
            product = d_outs[g].astype(f32) * attn_ref[here, head_span(g)].astype(f32)
            deltas.append(jnp.sum(product.T, axis=0, keepdims=True))
            delta_ref[g : g + 1, here] = deltas[g]
        turned = [jnp.zeros((HEAD_WIDTH, QROWS), f32) for g in range(GROUP)]
        for chunk in range(0, max(TAIL_CHUNKS - block, 0)):
            there = slice((block + chunk) * QROWS, (block + chunk + 1) * QROWS)
            mask = chunk_mask(bounds_ref[block, 0:1, :], bounds_ref[block, 1:2, :], chunk)
            d_key, d_value = chunk_backward(
                k_ref[there, :], v_ref[there, :], queries, d_outs, mask, shares, deltas, turned
            )
            if block == 0:
                dk_ref[there, :] = d_key
                dv_ref[there, :] = d_value
            else:
                dk_ref[there, :] += d_key
                dv_ref[there, :] += d_value
        for g in range(GROUP):
            turned_ref[head_span(g), here] = turned[g]
    d_kv_ref[0] = dk_ref[...].astype(bf16)
    d_kv_ref[1] = dv_ref[...].astype(bf16)


def attend_back_own_kernel(
    q_ref, k_ref, v_ref, bounds_ref, total_ref, d_out_ref, turned_ref, delta_ref, dq_ref, d_kv_ref
):
    for block in range(q_ref.shape[0] // QROWS):
        here = slice(block * QROWS, (block + 1) * QROWS)
        shares = [1.0 / total_ref[g : g + 1, here] for g in range(GROUP)]
        queries = [q_ref[here, head_span(g)] for g in range(GROUP)]
        d_outs = [d_out_ref[here, head_span(g)] for g in range(GROUP)]
        deltas = [delta_ref[g : g + 1, here] for g in range(GROUP)]
        turned = [turned_ref[head_span(g), here] for g in range(GROUP)]
        for chunk in range(max(TAIL_CHUNKS - block, 0), TAIL_CHUNKS + 1):
            row = (block + chunk - TAIL_CHUNKS) * QROWS
            there = slice(row, row + QROWS)
            mask = chunk_mask(bounds_ref[block, 0:1, :], bounds_ref[block, 1:2, :], chunk)
            d_key, d_value = chunk_backward(
                k_ref[there, :], v_ref[there, :], queries, d_outs, mask, shares, deltas, turned
            )
            if chunk == TAIL_CHUNKS:
                d_kv_ref[0, there, :] = d_key
                d_kv_ref[1, there, :] = d_value
            else:
                d_kv_ref[0, there, :] += d_key
                d_kv_ref[1, there, :] += d_value
        for g in range(GROUP):
            dq_ref[here, head_span(g)] = turned[g].T.astype(bf16)


def attend_back_tail(
    queries, kv_tail, bounds, totals, attn, d_proj, attn_w, attn_cols, after=()
):
    rows, q_cols = queries.shape
    width = attn_w.shape[0]
    kv_heads = kv_tail.shape[1] // (2 * HEAD_WIDTH)
    blocks = rows // QROWS
    wide = GROUP * HEAD_WIDTH
    pairs = chunk_pairs(sum(max(TAIL_CHUNKS - b, 0) for b in range(blocks)), kv_heads)
    head_spec = pl.BlockSpec((rows, wide), lambda j: (0, j))
    row_spec = pl.BlockSpec((None, 8, rows), lambda j: (j, 0, 0))
    return call(
        attend_back_tail_kernel,
        (queries, kv_tail, kv_tail, bounds, totals, attn, d_proj, attn_w),
        grid=(kv_heads,),
        in_specs=[
            head_spec,
            pl.BlockSpec((WINDOW_TOKENS, HEAD_WIDTH), lambda j: (0, j)),
            pl.BlockSpec((WINDOW_TOKENS, HEAD_WIDTH), lambda j: (0, kv_heads + j)),
            pl.BlockSpec((blocks, 8, QROWS), lambda j: (0, 0, 0)),
            row_spec,
            head_spec,
            pl.BlockSpec((rows, width), lambda j: (0, 0)),
            pl.BlockSpec((width, wide), lambda j: (0, attn_cols // wide + j)),
        ],
        out_specs=[
            head_spec,
            pl.BlockSpec((wide, rows), lambda j: (j, 0)),
            row_spec,
            pl.BlockSpec((2, WINDOW_TOKENS, HEAD_WIDTH), lambda j: (0, 0, j)),
        ],
        scratch=[pltpu.VMEM((WINDOW_TOKENS, HEAD_WIDTH), f32)] * 2,
        out_shape=[
            shape_of((rows, q_cols), bf16),
            shape_of((kv_heads * wide, rows), f32),
            shape_of((kv_heads, 8, rows), f32),
            shape_of((2, WINDOW_TOKENS, kv_heads * HEAD_WIDTH), bf16),
        ],
        mib=40,
        estimate=cost(10 * pairs * HEAD_WIDTH + 2 * rows * width * q_cols, 8 << 20, pairs),
        name="attend_back_tail",
        after=after,
    )


def attend_back_own(queries, kv_own, bounds, totals, d_outs, turned, deltas, after=()):
    rows, q_cols = queries.shape
    kv_heads = kv_own.shape[1] // (2 * HEAD_WIDTH)
    blocks = rows // QROWS
    wide = GROUP * HEAD_WIDTH
    pairs = chunk_pairs(sum(min(b, TAIL_CHUNKS) + 1 for b in range(blocks)), kv_heads)
    head_spec = pl.BlockSpec((rows, wide), lambda j: (0, j))
    row_spec = pl.BlockSpec((None, 8, rows), lambda j: (j, 0, 0))
    return call(
        attend_back_own_kernel,
        (queries, kv_own, kv_own, bounds, totals, d_outs, turned, deltas),
        grid=(kv_heads,),
        in_specs=[
            head_spec,
            pl.BlockSpec((rows, HEAD_WIDTH), lambda j: (0, j)),
            pl.BlockSpec((rows, HEAD_WIDTH), lambda j: (0, kv_heads + j)),
            pl.BlockSpec((blocks, 8, QROWS), lambda j: (0, 0, 0)),
            row_spec,
            head_spec,
            pl.BlockSpec((wide, rows), lambda j: (j, 0)),
            row_spec,
        ],
        out_specs=[
            head_spec,
            pl.BlockSpec((2, rows, HEAD_WIDTH), lambda j: (0, 0, j)),
        ],
        out_shape=[
            shape_of((rows, q_cols), bf16),
            shape_of((2, rows, kv_heads * HEAD_WIDTH), f32),
        ],
        mib=40,
        estimate=cost(10 * pairs * HEAD_WIDTH, 8 << 20, pairs, scale=1),
        name="attend_back_own",
        after=after,
    )


def mid_norm_kernel(x_ref, gain_ref, *refs):
    middle = x_ref[...].astype(f32)
    for ref in refs[:-2]:
        middle = middle + ref[...].astype(f32)
    refs[-2][...] = middle
    refs[-1][...] = (middle * norm_stats(middle) * gain_ref[...]).astype(bf16)


def mid_norm(hidden, gain, terms, after=()):
    rows, cols = hidden.shape
    spec = pl.BlockSpec((rows // 4, cols), lambda i: (i, 0))
    return call(
        mid_norm_kernel,
        (hidden, gain, *terms),
        grid=(4,),
        in_specs=[spec, pl.BlockSpec((1, cols), lambda i: (0, 0))] + [spec] * len(terms),
        out_specs=[spec, spec],
        out_shape=[shape_of((rows, cols), f32), shape_of((rows, cols), bf16)],
        estimate=cost(20 * rows * cols, 20 * rows * cols),
        name="mid_norm",
        after=after,
    )


def mid_back_kernel(own_ref, got_ref, middle_ref, grad_ref, gain_ref, out_ref, low_ref, sum_ref):
    @pl.when(pl.program_id(0) == 0)
    def clear():
        sum_ref[...] = jnp.zeros_like(sum_ref)

    d_normed = own_ref[...] + got_ref[...].astype(f32)
    middle = middle_ref[...]
    stats = norm_stats(middle)
    sum_ref[0:1, :] += jnp.sum(d_normed * (middle * stats), axis=0, keepdims=True)
    d_middle = grad_ref[...].astype(f32) + norm_back(d_normed, middle, stats, gain_ref[...])
    out_ref[...] = d_middle
    low_ref[...] = d_middle.astype(bf16)


def mid_back(own, got, middle, out_grad, gain, after=()):
    rows, cols = own.shape
    spec = pl.BlockSpec((rows // 4, cols), lambda i: (i, 0))
    return call(
        mid_back_kernel,
        (own, got, middle, out_grad, gain),
        grid=(4,),
        in_specs=[spec] * 4 + [pl.BlockSpec((1, cols), lambda i: (0, 0))],
        out_specs=[spec, spec, pl.BlockSpec((8, cols), lambda i: (0, 0))],
        out_shape=[
            shape_of((rows, cols), f32),
            shape_of((rows, cols), bf16),
            shape_of((8, cols), f32),
        ],
        estimate=cost(30 * rows * cols, 20 * rows * cols),
        name="mid_back",
        after=after,
    )


def mlp_kernel(
    x_own_ref, x_got_ref, g_own_ref, g_got_ref, wg_ref, wu_ref, wd_ref,
    mixed_ref, d_gate_ref, d_up_ref, d_mid_ref, d_mid_give_ref, out_ref, out_give_ref,
    x_ref, g_ref, d_mid_acc, out_acc
):
    step = pl.program_id(0)
    tokens = x_own_ref.shape[0]

    @pl.when(step == 0)
    def start():
        x_ref[:tokens, :] = x_own_ref[...]
        x_ref[tokens:, :] = x_got_ref[...]
        g_ref[:tokens, :] = g_own_ref[...]
        g_ref[tokens:, :] = g_got_ref[...]
        d_mid_acc[...] = jnp.zeros_like(d_mid_acc)
        out_acc[...] = jnp.zeros_like(out_acc)

    gate = nn_dot(x_ref[...], wg_ref[...])
    up = nn_dot(x_ref[...], wu_ref[...])
    d_mixed = nn_dot(g_ref[...], wd_ref[...])
    sig = 1.0 / (1.0 + jnp.exp(-gate))
    gated = gate * sig
    mixed = (gated * up).astype(bf16)
    d_gate = (d_mixed * up * sig * (1.0 + gate * (1.0 - sig))).astype(bf16)
    d_up = (d_mixed * gated).astype(bf16)
    mixed_ref[...] = mixed
    d_gate_ref[...] = d_gate
    d_up_ref[...] = d_up
    d_mid_acc[...] += nt_dot(d_gate, wg_ref[...]) + nt_dot(d_up, wu_ref[...])
    out_acc[...] += nt_dot(mixed, wd_ref[...])

    @pl.when(step == pl.num_programs(0) - 1)
    def finish():
        d_mid_ref[...] = d_mid_acc[:tokens, :]
        d_mid_give_ref[...] = d_mid_acc[tokens:, :].astype(bf16)
        out_ref[...] = out_acc[:tokens, :]
        out_give_ref[...] = out_acc[tokens:, :].astype(bf16)


def mlp(x_own, x_got, g_own, g_got, mlp_w, after=()):
    tokens, width = x_own.shape
    units = mlp_w.shape[1] // 3
    tile = 512
    steps = units // tile
    fixed = lambda j: (0, 0)
    rows_spec = pl.BlockSpec((tokens, width), fixed)
    tile_spec = pl.BlockSpec((2 * tokens, tile), lambda j: (0, j))
    tile_shape = shape_of((2 * tokens, units), bf16)
    return call(
        mlp_kernel,
        (x_own, x_got, g_own, g_got, mlp_w, mlp_w, mlp_w,),
        grid=(steps,),
        in_specs=[rows_spec] * 4
        + [
            pl.BlockSpec((width, tile), lambda j: (0, j)),
            pl.BlockSpec((width, tile), lambda j: (0, steps + j)),
            pl.BlockSpec((width, tile), lambda j: (0, 2 * steps + j)),
        ],
        out_specs=[tile_spec] * 3 + [rows_spec] * 4,
        out_shape=[tile_shape] * 3
        + [
            shape_of((tokens, width), f32),
            shape_of((tokens, width), bf16),
            shape_of((tokens, width), f32),
            shape_of((tokens, width), bf16),
        ],
        scratch=[
            pltpu.VMEM((2 * tokens, width), bf16),
            pltpu.VMEM((2 * tokens, width), bf16),
            pltpu.VMEM((2 * tokens, width), f32),
            pltpu.VMEM((2 * tokens, width), f32),
        ],
        mib=48,
        estimate=cost(12 * 2 * tokens * width * units, 16 << 20),
        name="mlp",
        after=after,
    )


def mlp_grad_kernel(own_ref, got_ref, d_ref, out_ref, turned_ref):
    tokens = own_ref.shape[0]

    @pl.when(pl.program_id(0) == 0)
    def start():
        turned_ref[:, :tokens] = own_ref[...].T
        turned_ref[:, tokens:] = got_ref[...].T

    out_ref[...] = nn_dot(turned_ref[...], d_ref[...]).astype(bf16)


def mlp_grad(own, got, d_units, after=()):
    tokens, width = own.shape
    units = d_units.shape[1]
    tile = 512
    fixed = lambda j: (0, 0)
    return call(
        mlp_grad_kernel,
        (own, got, d_units,),
        grid=(units // tile,),
        in_specs=[
            pl.BlockSpec((tokens, width), fixed),
            pl.BlockSpec((tokens, width), fixed),
            pl.BlockSpec((2 * tokens, tile), lambda j: (0, j)),
        ],
        out_specs=pl.BlockSpec((width, tile), lambda j: (0, j)),
        out_shape=shape_of((width, units), bf16),
        scratch=[pltpu.VMEM((width, 2 * tokens), bf16)],
        mib=32,
        estimate=cost(4 * tokens * width * units, 8 << 20),
        name="mlp_grad",
        after=after,
    )


def mlp_grad_pair_kernel(
    steps, own_a_ref, got_a_ref, d_a_ref, own_b_ref, got_b_ref, d_b_ref, out_ref, turned_ref
):
    step = pl.program_id(0)
    tokens = own_a_ref.shape[0]

    @pl.when(step == 0)
    def first():
        turned_ref[:, :tokens] = own_a_ref[...].T
        turned_ref[:, tokens:] = got_a_ref[...].T

    @pl.when(step == steps)
    def second():
        turned_ref[:, :tokens] = own_b_ref[...].T
        turned_ref[:, tokens:] = got_b_ref[...].T

    @pl.when(step < steps)
    def left():
        out_ref[...] = nn_dot(turned_ref[...], d_a_ref[...]).astype(bf16)

    @pl.when(step >= steps)
    def right():
        out_ref[...] = nn_dot(turned_ref[...], d_b_ref[...]).astype(bf16)


def mlp_grad_pair(own_a, got_a, d_a, own_b, got_b, d_b, after=()):
    tokens, width = own_a.shape
    units = d_a.shape[1]
    tile = 512
    steps = units // tile
    rows = pl.BlockSpec((tokens, width), lambda j: (0, 0))
    return call(
        functools.partial(mlp_grad_pair_kernel, steps),
        (own_a, got_a, d_a, own_b, got_b, d_b),
        grid=(2 * steps,),
        in_specs=[
            rows,
            rows,
            pl.BlockSpec((2 * tokens, tile), lambda j: (0, jnp.minimum(j, steps - 1))),
            rows,
            rows,
            pl.BlockSpec((2 * tokens, tile), lambda j: (0, jnp.maximum(j - steps, 0))),
        ],
        out_specs=pl.BlockSpec((width, tile), lambda j: (0, j)),
        scratch=[pltpu.VMEM((width, 2 * tokens), bf16)],
        out_shape=shape_of((width, 2 * units), bf16),
        mib=48,
        estimate=cost(8 * tokens * width * units, 16 << 20),
        name="mlp_grad_pair",
        after=after,
    )


def body(
    hidden_in,
    doc_lengths,
    pad_lengths,
    w_query,
    key_matrix,
    value_matrix,
    w_output,
    w_gate,
    w_up,
    w_down,
    attn_gain,
    mlp_gain,
    query_gain,
    key_gain,
    out_grad,
):
    core = lax.axis_index("c")
    chip = lax.axis_index("q")
    chips = lax.axis_size("q")
    group = chip * 2 + core
    part = lax.axis_index("seq")
    groups = chips * 2
    parts = lax.axis_size("seq")
    tokens, width = hidden_in.shape
    group_rows = tokens * parts
    slice_rows = width // groups
    units = FEEDFWD_UNITS // 2
    q_cols = QUERY_HEADS * HEAD_WIDTH // parts
    kv_cols = KEY_VALUE_HEADS * HEAD_WIDTH // parts
    attn_cols = q_cols + 2 * kv_cols
    pack_cols = attn_cols + q_cols
    core_at = core.astype(jnp.int32).reshape(1)
    part_at = part.astype(jnp.int32).reshape(1)

    def swapped(value):
        return lax.ppermute(value, "c", core_swap)

    def sent(value, shift):
        return lax.ppermute(value, "seq", [(i, (i + shift) % parts) for i in range(parts)])

    def from_all(value):
        return [value] + [sent(value, shift) for shift in range(1, parts)]

    hidden_blocks = from_all(hidden_in)

    packed = pack_attn(
        part_at, parts, w_query, key_matrix, value_matrix, w_output,
        (attn_gain, mlp_gain, query_gain, key_gain),
    )
    attn_w = lax.all_gather(packed, dp_axes, axis=0, tiled=True)

    mlp_pack, mlp_give = pack_mlp(core_at, w_gate, w_up, w_down, after=(packed,))
    mlp_pack = lax.dynamic_update_slice_in_dim(
        mlp_pack, swapped(mlp_give), (1 - core) * slice_rows, 0
    )
    mlp_w = lax.all_gather(mlp_pack, "q", axis=0, tiled=True)
    grad_spread = jnp.where(
        (jnp.arange(2) == core)[:, None, None], jnp.zeros((), bf16), out_grad[None]
    )
    grad_got = lax.psum_scatter(grad_spread, "c", scatter_dimension=0, tiled=True)
    grad_got = grad_got.reshape(tokens, width)

    gains = read_gains(attn_w, pack_cols)
    head_piece = query_gain.shape[0]
    ga = gains[0:1]
    gm = gains[1:2]
    gqk = gains[2:4].reshape(2, groups, slice_rows)[:, :, :head_piece].reshape(2, HEAD_WIDTH)

    doc_ends = jnp.cumsum(doc_lengths)
    doc_starts = doc_ends - doc_lengths
    pad_starts = doc_ends - pad_lengths
    first = group * group_rows
    token = first + jnp.arange(group_rows, dtype=jnp.int32)
    inside = (token[:, None] >= doc_starts[None, :]) & (token[:, None] < doc_ends[None, :])
    start = jnp.sum(jnp.where(inside, doc_starts[None, :], 0), axis=1)
    pad_start = jnp.sum(jnp.where(inside, pad_starts[None, :], 0), axis=1)
    inv_freq = rope_base ** (-jnp.arange(HEAD_WIDTH // 2, dtype=f32) * 2.0 / HEAD_WIDTH)
    angles = (token - start).astype(f32)[:, None] * inv_freq[None, :]
    cosine = jnp.cos(angles)
    sine = jnp.sin(angles)
    cosine = jnp.concatenate([cosine, cosine], axis=1)
    sine = jnp.concatenate([-sine, sine], axis=1)
    offset = (token // QROWS) * QROWS - WINDOW_TOKENS
    low = jnp.maximum(start, token - (WINDOW_TOKENS - 1)) - offset
    high = jnp.minimum(token, pad_start - 1) - offset
    bounds = jnp.pad(
        jnp.stack([low.reshape(parts, QROWS), high.reshape(parts, QROWS)], axis=1),
        ((0, 0), (0, 6), (0, 0)),
    )

    normed_all, queries, kv_own, qk_proj = project(
        part_at, hidden_blocks, attn_w, ga, gqk, cosine, sine, q_cols, kv_cols
    )
    kv_tail = lax.ppermute(
        kv_own[group_rows - WINDOW_TOKENS :], dp_axes, [(i, i + 1) for i in range(groups - 1)]
    )
    own_outs, own_totals = attend_own(queries, kv_own, bounds)
    terms = []
    attn = [None] * parts
    totals = [None] * parts
    order = [shift for shift in range(1, parts)] + [0]
    for shift in order:
        attn[shift], totals[shift], term = attend_tail(
            shift, part_at, parts, queries, kv_tail, bounds, own_outs, own_totals, attn_w, attn_cols
        )
        terms.append(sent(term, shift) if shift else term)
    attn_all = jnp.zeros((group_rows, q_cols), bf16)
    totals_all = jnp.zeros((kv_cols // HEAD_WIDTH, 8, group_rows), f32)
    for shift in range(parts):
        row = (part + shift) % parts * tokens
        attn_all = lax.dynamic_update_slice_in_dim(attn_all, attn[shift], row, 0)
        totals_all = lax.dynamic_update_slice_in_dim(totals_all, totals[shift], row, 2)
    middle, normed_mid = mid_norm(hidden_in, gm, terms)

    mid_got = swapped(normed_mid)
    mixed, d_gate, d_up, d_mid, d_mid_give, out_part, out_give = mlp(
        normed_mid, mid_got, out_grad, grad_got, mlp_w
    )
    d_middle, d_proj, mlp_gain_rows = mid_back(
        d_mid, swapped(d_mid_give), middle, out_grad, gm
    )
    term_pair = mlp_grad_pair(
        out_grad, grad_got, mixed, normed_mid, mid_got, d_gate, after=(d_proj,)
    )
    d_proj_all = lax.all_gather(d_proj, "seq", axis=0, tiled=True)
    output_act = (middle + out_part + swapped(out_give).astype(f32)).astype(bf16)

    def chip_sums(grad):
        return lax.psum_scatter(grad, "q", scatter_dimension=0, tiled=True)

    own_pair = chip_sums(term_pair)
    term_up = mlp_grad(normed_mid, mid_got, d_up, after=(d_proj,))
    own_up = chip_sums(term_up)
    line = list(range(parts))

    def unpacked(sums, column, turned, after=()):
        give = lax.dynamic_slice(
            sums, ((1 - core) * slice_rows, column * units), (slice_rows, units)
        )
        return unpack_half(core_at, sums, swapped(give), column, turned, after=after)

    d_attn, turned, deltas, d_tail = attend_back_tail(
        queries, kv_tail, bounds, totals_all, attn_all, d_proj_all, attn_w, attn_cols,
        after=(term_up,),
    )
    d_tail = lax.ppermute(d_tail, dp_axes, [(i + 1, i) for i in range(groups - 1)])
    d_queries, d_kv = attend_back_own(
        queries, kv_own, bounds, totals_all, d_attn, turned, deltas
    )
    sum_pair = lax.psum(own_pair, "seq")
    w_out_grad = out_grad_sums([d_proj_all], [attn_all], after=(d_queries,))
    d_in, attn_term = project_back(
        part_at, groups, [hidden_blocks[(parts - k) % parts] for k in range(parts)],
        d_queries, d_kv, d_tail, qk_proj, attn_w, gqk, cosine, sine, normed_all, w_out_grad,
        mlp_gain_rows,
    )
    d_in = lax.psum_scatter(d_in, "seq", scatter_dimension=0, tiled=True)

    attn_grad = lax.psum_scatter(attn_term, dp_axes, scatter_dimension=0, tiled=True)
    give = lax.dynamic_slice_in_dim(own_up, (1 - core) * slice_rows, slice_rows, 0)
    own_up = join_halves(core_at, own_up, swapped(give), after=(sum_pair,))
    sum_up = lax.psum(own_up, "seq", axis_index_groups=[line[::-1]])
    grad_down = unpacked(sum_pair, 0, True)
    grad_gate = unpacked(sum_pair, 1, False, after=(grad_down,))
    attn_grad = touch(attn_grad, after=(grad_gate, sum_up))
    attn_grads = lax.all_gather(attn_grad, "seq", axis=0)
    in_grad = finish_in(d_in, d_middle, hidden_in, ga)
    grad_up = widened(sum_up, after=(in_grad,))
    gain_sums = jnp.sum(attn_grads[:, :, pack_cols : pack_cols + 4].astype(f32), axis=0)
    grad_query, grad_key, grad_value, grad_output = unpack_attn(
        attn_grads, q_cols, kv_cols, after=(grad_up,)
    )
    return (
        output_act,
        in_grad,
        grad_query,
        grad_key,
        grad_value,
        grad_output,
        grad_gate,
        grad_up,
        grad_down,
        gain_sums[:, 0],
        gain_sums[:, 1],
        gain_sums[:head_piece, 2],
        gain_sums[:head_piece, 3],
    )


def solution(mesh):
    groups, parts = mesh.devices.shape
    mesh = Mesh(mesh.devices.reshape(groups // 2, 2, parts), ("q", "c", "seq"))
    tokens = P(("q", "c", "seq"), None)
    rows = P(dp_axes, None)
    cols = P(None, dp_axes)
    flat = P(dp_axes)
    in_specs = (
        tokens, P(), P(), rows, rows, rows, cols, rows, rows, cols, flat, flat, flat, flat, tokens,
    )
    out_specs = (
        tokens, tokens, rows, rows, rows, cols, rows, rows, cols, flat, flat, flat, flat,
    )
    return jax.shard_map(body, mesh=mesh, in_specs=in_specs, out_specs=out_specs, check_vma=False)
```

```python
import functools

import jax
import jax.numpy as jnp
from jax import lax
from jax.experimental import pallas as pl
from jax.experimental.pallas import tpu as pltpu
from jax.sharding import Mesh, PartitionSpec as P

QUERY_HEADS = 16
KEY_VALUE_HEADS = 8
HEAD_WIDTH = 128
FEEDFWD_UNITS = 3072
WINDOW_TOKENS = 1024
QROWS = 256
GROUP = QUERY_HEADS // KEY_VALUE_HEADS
TAIL_CHUNKS = WINDOW_TOKENS // QROWS

norm_eps = 1e-06
rope_base = 1000000.0
score_scale = HEAD_WIDTH**-0.5
log2_e = 1.4426950408889634
bf16 = jnp.bfloat16
f32 = jnp.float32
dp_axes = ("q", "c")
core_swap = [(0, 1), (1, 0)]


def nt_dot(left, right):
    return lax.dot_general(left, right, (((1,), (1,)), ((), ())), preferred_element_type=f32)


def tn_dot(left, right):
    return lax.dot_general(left, right, (((0,), (0,)), ((), ())), preferred_element_type=f32)


def nn_dot(left, right):
    return jnp.dot(left, right, preferred_element_type=f32)


def shape_of(dims, kind):
    return jax.ShapeDtypeStruct(dims, kind)


def call(
    kernel, args, *, grid, in_specs, out_specs, out_shape, name, estimate, prefetch=0, scratch=(),
    mib=32, after=()
):
    count = prefetch + len(in_specs)

    def body_of(*refs):
        kernel(*refs[:count], *refs[count + len(after) :])

    return pl.pallas_call(
        body_of,
        grid_spec=pltpu.PrefetchScalarGridSpec(
            num_scalar_prefetch=prefetch,
            grid=grid,
            in_specs=list(in_specs) + [pl.BlockSpec(memory_space=pl.ANY)] * len(after),
            out_specs=out_specs,
            scratch_shapes=list(scratch),
        ),
        out_shape=out_shape,
        compiler_params=pltpu.CompilerParams(vmem_limit_bytes=mib << 20),
        cost_estimate=estimate,
        name=name,
    )(*args, *after)


def cost(flops, moved, exps=0, scale=100):
    flops, moved, exps = flops * scale, moved * scale, exps * scale
    return pl.CostEstimate(flops=int(flops), bytes_accessed=int(moved), transcendentals=int(exps))


def norm_stats(rows):
    return lax.rsqrt(jnp.mean(rows * rows, axis=-1, keepdims=True) + norm_eps)


def norm_back(d_normed, rows, stats, gains):
    scaled = d_normed * gains
    unit = rows * stats
    return stats * (scaled - unit * jnp.mean(scaled * unit, axis=-1, keepdims=True))


def pack_attn_kernel(
    part_ref, wq_ref, wk_ref, wv_ref, wo_ref, ga_ref, gm_ref, gq_ref, gk_ref, out_ref, gains_ref
):
    gains_ref[...] = jnp.zeros_like(gains_ref)
    for row, gain_ref in enumerate((ga_ref, gm_ref, gq_ref, gk_ref)):
        gains_ref[row : row + 1, : gain_ref.shape[1]] = gain_ref[...]
    column = 0
    for piece in (
        wq_ref[...].astype(bf16),
        wk_ref[...].astype(bf16),
        wv_ref[...].astype(bf16),
        wo_ref[...].T.astype(bf16),
    ):
        out_ref[:, column : column + piece.shape[1]] = piece
        column += piece.shape[1]
    gains = gains_ref[...].T
    rest = jnp.zeros((gains.shape[0], HEAD_WIDTH - gains.shape[1]), f32)
    out_ref[:, column:] = jnp.concatenate([gains, rest], axis=1).astype(bf16)


def pack_attn(part, parts, w_query, key_matrix, value_matrix, w_output, gains, after=()):
    gains = [gain[None] for gain in gains]
    rows = w_query.shape[0]
    q_cols = w_query.shape[1] // parts
    kv_cols = key_matrix.shape[1] // parts
    total = 2 * q_cols + 2 * kv_cols + HEAD_WIDTH
    return call(
        pack_attn_kernel,
        (part, w_query, key_matrix, value_matrix, w_output, *gains),
        prefetch=1,
        grid=(1,),
        in_specs=[
            pl.BlockSpec((rows, q_cols), lambda i, p: (0, p[0])),
            pl.BlockSpec((rows, kv_cols), lambda i, p: (0, p[0])),
            pl.BlockSpec((rows, kv_cols), lambda i, p: (0, p[0])),
            pl.BlockSpec((q_cols, rows), lambda i, p: (p[0], 0)),
        ]
        + [pl.BlockSpec(gain.shape, lambda i, p: (0, 0)) for gain in gains],
        scratch=[pltpu.VMEM((8, rows), f32)],
        mib=60,
        out_specs=pl.BlockSpec((rows, total), lambda i, p: (0, 0)),
        out_shape=shape_of((rows, total), bf16),
        estimate=cost(0, rows * total * 6),
        name="pack_attn",
        after=after,
    )


def touch_kernel(in_ref, out_ref):
    out_ref[...] = in_ref[...]


def touch(value, after):
    rows, cols = value.shape
    spec = pl.BlockSpec((rows // 4, cols), lambda i: (i, 0))
    return call(
        touch_kernel,
        (value,),
        grid=(4,),
        in_specs=[spec],
        out_specs=spec,
        out_shape=shape_of((rows, cols), value.dtype),
        estimate=cost(0, 4 * rows * cols),
        name="touch",
        after=after,
    )


def finish_in_kernel(d_normed_ref, d_middle_ref, x_ref, gain_ref, out_ref):
    rows = x_ref[...].astype(f32)
    back = norm_back(d_normed_ref[...].astype(f32), rows, norm_stats(rows), gain_ref[...])
    out_ref[...] = (d_middle_ref[...] + back).astype(bf16)


def finish_in(d_normed, d_middle, hidden, gain, after=()):
    rows, cols = hidden.shape
    spec = pl.BlockSpec((rows // 4, cols), lambda i: (i, 0))
    return call(
        finish_in_kernel,
        (d_normed, d_middle, hidden, gain),
        grid=(4,),
        in_specs=[spec] * 3 + [pl.BlockSpec((1, cols), lambda i: (0, 0))],
        out_specs=spec,
        out_shape=shape_of((rows, cols), bf16),
        estimate=cost(20 * rows * cols, 12 * rows * cols, scale=1),
        name="finish_in",
        after=after,
    )


def read_gains_kernel(in_ref, out_ref):
    out_ref[...] = in_ref[...].astype(f32).T[:8, :]


def read_gains(attn_w, column, after=()):
    width = attn_w.shape[0]
    return call(
        read_gains_kernel,
        (attn_w,),
        grid=(1,),
        in_specs=[pl.BlockSpec((width, HEAD_WIDTH), lambda i: (0, column // HEAD_WIDTH))],
        out_specs=pl.BlockSpec((8, width), lambda i: (0, 0)),
        out_shape=shape_of((8, width), f32),
        estimate=cost(0, width * HEAD_WIDTH * 4),
        name="read_gains",
        after=after,
    )


def pack_mlp_kernel(core_ref, wg_ref, wu_ref, wd_ref, own_ref, give_ref):
    units = wg_ref.shape[1]

    def fill(out_ref):
        out_ref[:, :units] = wg_ref[...].astype(bf16)
        out_ref[:, units : 2 * units] = wu_ref[...].astype(bf16)
        out_ref[:, 2 * units :] = wd_ref[...].T.astype(bf16)

    @pl.when(pl.program_id(0) == 0)
    def first():
        fill(give_ref)

    @pl.when(pl.program_id(0) == 1)
    def second():
        fill(own_ref)


def pack_mlp(core, w_gate, w_up, w_down, after=()):
    rows = w_gate.shape[0]
    units = w_gate.shape[1] // 2
    half = lambda i, c: (c[0] + 1 - i) % 2
    return call(
        pack_mlp_kernel,
        (core, w_gate, w_up, w_down,),
        prefetch=1,
        grid=(2,),
        in_specs=[
            pl.BlockSpec((rows, units), lambda i, c: (0, half(i, c))),
            pl.BlockSpec((rows, units), lambda i, c: (0, half(i, c))),
            pl.BlockSpec((units, rows), lambda i, c: (half(i, c), 0)),
        ],
        out_specs=[
            pl.BlockSpec((rows, 3 * units), lambda i, c: (c[0], 0)),
            pl.BlockSpec((rows, 3 * units), lambda i, c: (0, 0)),
        ],
        out_shape=[shape_of((2 * rows, 3 * units), bf16), shape_of((rows, 3 * units), bf16)],
        estimate=cost(0, rows * units * 36),
        name="pack_mlp",
        after=after,
    )


def unpack_half_kernel(turned, core_ref, own_ref, got_ref, out_ref):
    def fill(in_ref):
        rows = in_ref[...].astype(f32)
        out_ref[...] = rows.T if turned else rows

    @pl.when(pl.program_id(0) == 0)
    def first():
        fill(own_ref)

    @pl.when(pl.program_id(0) == 1)
    def second():
        fill(got_ref)


def unpack_half(core, sums, got, column, turned, after=()):
    rows, units = got.shape
    half = lambda i, c: (c[0] + i) % 2
    if turned:
        out_spec = pl.BlockSpec((units, rows), lambda i, c: (half(i, c), 0))
        out_shape = shape_of((2 * units, rows), f32)
    else:
        out_spec = pl.BlockSpec((rows, units), lambda i, c: (0, half(i, c)))
        out_shape = shape_of((rows, 2 * units), f32)
    return call(
        functools.partial(unpack_half_kernel, turned),
        (core, sums, got,),
        prefetch=1,
        grid=(2,),
        in_specs=[
            pl.BlockSpec((rows, units), lambda i, c: (c[0], column)),
            pl.BlockSpec((rows, units), lambda i, c: (0, 0)),
        ],
        out_specs=out_spec,
        out_shape=out_shape,
        estimate=cost(0, rows * units * 12, scale=1),
        name="unpack_half",
        after=after,
    )


def join_halves_kernel(core_ref, own_ref, got_ref, out_ref):
    @pl.when(pl.program_id(0) == 0)
    def first():
        out_ref[...] = own_ref[...]

    @pl.when(pl.program_id(0) == 1)
    def second():
        out_ref[...] = got_ref[...]


def join_halves(core, sums, got, after=()):
    rows, units = got.shape
    return call(
        join_halves_kernel,
        (core, sums, got),
        prefetch=1,
        grid=(2,),
        in_specs=[
            pl.BlockSpec((rows, units), lambda i, c: (c[0], 0)),
            pl.BlockSpec((rows, units), lambda i, c: (0, 0)),
        ],
        out_specs=pl.BlockSpec((rows, units), lambda i, c: (0, (c[0] + i) % 2)),
        out_shape=shape_of((rows, 2 * units), bf16),
        estimate=cost(0, rows * units * 8, scale=1),
        name="join_halves",
        after=after,
    )


def widened_kernel(in_ref, out_ref):
    out_ref[...] = in_ref[...].astype(f32)


def widened(value, after=()):
    rows, cols = value.shape
    spec = pl.BlockSpec((rows, cols // 2), lambda i: (0, i))
    return call(
        widened_kernel,
        (value,),
        grid=(2,),
        in_specs=[spec],
        out_specs=spec,
        out_shape=shape_of((rows, cols), f32),
        estimate=cost(0, rows * cols * 6, scale=1),
        name="widened",
        after=after,
    )


def unpack_attn_kernel(in_ref, wq_ref, wk_ref, wv_ref, wo_ref):
    column = 0
    for out_ref in (wq_ref, wk_ref, wv_ref):
        count = out_ref.shape[1]
        out_ref[...] = in_ref[:, column : column + count].astype(f32)
        column += count
    wo_ref[...] = in_ref[:, column : column + wo_ref.shape[0]].astype(f32).T


def unpack_attn(gathered, q_cols, kv_cols, after=()):
    parts, rows, total = gathered.shape
    return call(
        unpack_attn_kernel,
        (gathered,),
        grid=(parts,),
        in_specs=[pl.BlockSpec((None, rows, total), lambda i: (i, 0, 0))],
        out_specs=[
            pl.BlockSpec((rows, q_cols), lambda i: (0, i)),
            pl.BlockSpec((rows, kv_cols), lambda i: (0, i)),
            pl.BlockSpec((rows, kv_cols), lambda i: (0, i)),
            pl.BlockSpec((q_cols, rows), lambda i: (i, 0)),
        ],
        out_shape=[
            shape_of((rows, parts * q_cols), f32),
            shape_of((rows, parts * kv_cols), f32),
            shape_of((rows, parts * kv_cols), f32),
            shape_of((parts * q_cols, rows), f32),
        ],
        estimate=cost(0, parts * rows * total * 6, scale=1),
        mib=60,
        name="unpack_attn",
        after=after,
    )


def pick(refs, scratch):
    for k, ref in enumerate(refs):

        @pl.when(pl.program_id(0) == k)
        def take(ref=ref):
            scratch[...] = ref[...]


def turn(rows):
    half = HEAD_WIDTH // 2
    return jnp.concatenate([rows[:, half:], rows[:, :half]], axis=1)


def project_kernel(parts, q_cols, kv_cols, part_ref, *refs):
    blocks = refs[:parts]
    w_ref, ga_ref, gqk_ref, cos_ref, sin_ref, normed_ref, q_ref, kv_ref, proj_ref, x_ref = refs[parts:]
    pick(blocks, x_ref)
    rows = x_ref[...].astype(f32)
    normed = (rows * norm_stats(rows) * ga_ref[...]).astype(bf16)
    normed_ref[...] = normed
    cosine = cos_ref[...]
    sine = sin_ref[...]
    qk_cols = q_cols + kv_cols
    proj = nn_dot(normed, w_ref[...])
    proj_ref[...] = proj[:, :qk_cols]
    kv_ref[:, kv_cols:] = proj[:, qk_cols:].astype(bf16)
    for column in range(0, qk_cols, HEAD_WIDTH):
        head = proj[:, column : column + HEAD_WIDTH]
        gain = gqk_ref[0:1, :] if column < q_cols else gqk_ref[1:2, :]
        head = head * norm_stats(head) * gain
        head = (head * cosine + turn(head) * sine).astype(bf16)
        if column < q_cols:
            q_ref[:, column : column + HEAD_WIDTH] = head
        else:
            kv_ref[:, column - q_cols : column - q_cols + HEAD_WIDTH] = head


def project(part, blocks, attn_w, ga, gqk, cosine, sine, q_cols, kv_cols, after=()):
    parts = len(blocks)
    tokens, width = blocks[0].shape
    attn_cols = q_cols + 2 * kv_cols
    place = lambda k, p: ((p[0] + parts - k) % parts, 0)
    fixed = lambda k, p: (0, 0)
    rows = parts * tokens
    return call(
        functools.partial(project_kernel, parts, q_cols, kv_cols),
        (part, *blocks, attn_w, ga, gqk, cosine, sine,),
        prefetch=1,
        grid=(parts,),
        in_specs=[pl.BlockSpec((tokens, width), fixed)] * parts
        + [
            pl.BlockSpec((width, attn_cols), fixed),
            pl.BlockSpec((1, width), fixed),
            pl.BlockSpec((2, HEAD_WIDTH), fixed),
            pl.BlockSpec((tokens, HEAD_WIDTH), place),
            pl.BlockSpec((tokens, HEAD_WIDTH), place),
        ],
        out_specs=[
            pl.BlockSpec((tokens, width), place),
            pl.BlockSpec((tokens, q_cols), place),
            pl.BlockSpec((tokens, 2 * kv_cols), place),
            pl.BlockSpec((tokens, q_cols + kv_cols), place),
        ],
        scratch=[pltpu.VMEM((tokens, width), bf16)],
        out_shape=[
            shape_of((rows, width), bf16),
            shape_of((rows, q_cols), bf16),
            shape_of((rows, 2 * kv_cols), bf16),
            shape_of((rows, q_cols + kv_cols), f32),
        ],
        mib=32,
        estimate=cost(2 * rows * width * attn_cols, 12 << 20),
        name="project",
        after=after,
    )


def project_back_kernel(
    parts, groups, tail_from, q_cols, kv_cols, part_ref, *refs
):
    blocks = refs[:parts]
    (dq_ref, d_kv_ref, tail_ref, proj_ref, w_ref, gqk_ref, cos_ref, sin_ref, normed_ref,
     w_out_ref, mlp_gain_ref, out_ref, term_ref,
     x_ref, dqkv_ref, acc_ref, gain_ref, head_gain_ref) = refs[parts:]
    step = pl.program_id(0)
    block = (part_ref[0] + step) % parts
    pick(blocks, x_ref)

    @pl.when(step == 0)
    def clear():
        gain_ref[...] = jnp.zeros_like(gain_ref)
        head_gain_ref[...] = jnp.zeros_like(head_gain_ref)
        acc_ref[...] = jnp.zeros_like(acc_ref)

    cosine = cos_ref[...]
    sine = sin_ref[...]
    has_tail = jnp.where(block >= tail_from, 1.0, 0.0)
    dk = (d_kv_ref[0] + tail_ref[0].astype(f32) * has_tail).astype(bf16)
    dqkv_ref[:, q_cols + kv_cols :] = (
        d_kv_ref[1] + tail_ref[1].astype(f32) * has_tail
    ).astype(bf16)
    head_gains = [jnp.zeros((1, HEAD_WIDTH), f32) for _ in range(2)]
    for column in range(0, q_cols + kv_cols, HEAD_WIDTH):
        index = 0 if column < q_cols else 1
        if index == 0:
            d_head = dq_ref[:, column : column + HEAD_WIDTH].astype(f32)
        else:
            d_head = dk[:, column - q_cols : column - q_cols + HEAD_WIDTH].astype(f32)
        d_head = d_head * cosine + turn(d_head * sine)
        head = proj_ref[:, column : column + HEAD_WIDTH]
        stats = norm_stats(head)
        unit = head * stats
        head_gains[index] = head_gains[index] + jnp.sum(d_head * unit, axis=0, keepdims=True)
        scaled = d_head * gqk_ref[index : index + 1, :]
        d_proj = stats * (scaled - unit * jnp.mean(scaled * unit, axis=-1, keepdims=True))
        dqkv_ref[:, column : column + HEAD_WIDTH] = d_proj.astype(bf16)
    head_gain_ref[0:1, :] += head_gains[0]
    head_gain_ref[1:2, :] += head_gains[1]
    d_in = nt_dot(dqkv_ref[...], w_ref[...])
    rows = x_ref[...].astype(f32)
    gain_ref[0:1, :] += jnp.sum(d_in * (rows * norm_stats(rows)), axis=0, keepdims=True)
    out_ref[...] = d_in.astype(bf16)
    acc_ref[...] += tn_dot(normed_ref[...], dqkv_ref[...])

    @pl.when(step == parts - 1)
    def finish():
        attn_cols = acc_ref.shape[1]
        term_ref[:, :attn_cols] = acc_ref[...].astype(bf16)
        term_ref[:, attn_cols : attn_cols + q_cols] = w_out_ref[...]
        gain_ref[1:2, :] = mlp_gain_ref[0:1, :]
        piece = HEAD_WIDTH // groups
        slice_rows = gain_ref.shape[1] // groups
        for index in range(2):
            for group in range(groups):
                gain_ref[2 + index : 3 + index, group * slice_rows : group * slice_rows + piece] = (
                    head_gain_ref[index : index + 1, group * piece : (group + 1) * piece]
                )
        gains = gain_ref[...].T
        rest = jnp.zeros((gains.shape[0], HEAD_WIDTH - gains.shape[1]), f32)
        term_ref[:, attn_cols + q_cols :] = jnp.concatenate([gains, rest], axis=1).astype(bf16)


def project_back(
    part, groups, hidden, dq, d_kv, tail, proj, attn_w, gqk, cosine, sine, normed,
    w_out_grad, mlp_gain_rows, after=()
):
    parts = len(hidden)
    tokens, width = hidden[0].shape
    rows, q_cols = dq.shape
    kv_cols = d_kv.shape[2]
    attn_cols = q_cols + 2 * kv_cols
    tail_from = (rows - WINDOW_TOKENS) // tokens
    place = lambda k, p: ((p[0] + k) % parts, 0)
    kv_place = lambda k, p: (0, (p[0] + k) % parts, 0)
    tail_place = lambda k, p: (0, jnp.maximum((p[0] + k) % parts - tail_from, 0), 0)
    fixed = lambda k, p: (0, 0)
    total = attn_cols + q_cols + HEAD_WIDTH
    return call(
        functools.partial(project_back_kernel, parts, groups, tail_from, q_cols, kv_cols),
        (part, *hidden, dq, d_kv, tail, proj, attn_w, gqk, cosine, sine, normed, w_out_grad, mlp_gain_rows),
        prefetch=1,
        grid=(parts,),
        in_specs=[pl.BlockSpec((tokens, width), fixed)] * parts
        + [
            pl.BlockSpec((tokens, q_cols), place),
            pl.BlockSpec((2, tokens, kv_cols), kv_place),
            pl.BlockSpec((2, tokens, kv_cols), tail_place),
            pl.BlockSpec((tokens, q_cols + kv_cols), place),
            pl.BlockSpec((width, attn_cols), fixed),
            pl.BlockSpec((2, HEAD_WIDTH), fixed),
            pl.BlockSpec((tokens, HEAD_WIDTH), place),
            pl.BlockSpec((tokens, HEAD_WIDTH), place),
            pl.BlockSpec((tokens, width), place),
            pl.BlockSpec((width, q_cols), fixed),
            pl.BlockSpec((8, width), fixed),
        ],
        out_specs=[
            pl.BlockSpec((tokens, width), place),
            pl.BlockSpec((width, total), fixed),
        ],
        scratch=[
            pltpu.VMEM((tokens, width), bf16),
            pltpu.VMEM((tokens, attn_cols), bf16),
            pltpu.VMEM((width, attn_cols), f32),
            pltpu.VMEM((8, width), f32),
            pltpu.VMEM((8, HEAD_WIDTH), f32),
        ],
        mib=48,
        out_shape=[
            shape_of((rows, width), bf16),
            shape_of((width, total), bf16),
        ],
        estimate=cost(4 * rows * width * attn_cols, 16 << 20, scale=1),
        name="project_back",
        after=after,
    )


def out_grad_kernel(parts, *refs):
    d_projs = refs[:parts]
    attns = refs[parts : 2 * parts]
    out_ref = refs[2 * parts]
    total = None
    for d_proj, attn in zip(d_projs, attns):
        term = tn_dot(d_proj[...], attn[...])
        total = term if total is None else total + term
    out_ref[...] = total.astype(bf16)


def out_grad_sums(d_projs, attns, after=()):
    parts = len(attns)
    tokens, q_cols = attns[0].shape
    width = d_projs[0].shape[1]
    cols = width // 4
    return call(
        functools.partial(out_grad_kernel, parts),
        (*d_projs, *attns,),
        grid=(4,),
        in_specs=[pl.BlockSpec((tokens, cols), lambda i: (0, i))] * parts
        + [pl.BlockSpec((tokens, q_cols), lambda i: (0, 0))] * parts,
        out_specs=pl.BlockSpec((cols, q_cols), lambda i: (i, 0)),
        out_shape=shape_of((width, q_cols), bf16),
        mib=32,
        estimate=cost(2 * parts * tokens * width * q_cols, 4 << 20, scale=1),
        name="out_grad",
        after=after,
    )


def chunk_mask(low, high, chunk):
    key = lax.broadcasted_iota(jnp.int32, (QROWS, QROWS), 0) + chunk * QROWS
    mask = (key >= low) & (key <= high)
    if chunk == TAIL_CHUNKS:
        own = lax.broadcasted_iota(jnp.int32, (QROWS, QROWS), 1) + WINDOW_TOKENS
        mask = mask | (key == own)
    return mask


def head_span(g):
    return slice(g * HEAD_WIDTH, (g + 1) * HEAD_WIDTH)


def attend_own_kernel(q_ref, k_ref, v_ref, bounds_ref, out_ref, total_ref):
    for block in range(q_ref.shape[0] // QROWS):
        here = slice(block * QROWS, (block + 1) * QROWS)
        sums = [jnp.zeros((1, QROWS), f32) for g in range(GROUP)]
        outs = [jnp.zeros((HEAD_WIDTH, QROWS), f32) for g in range(GROUP)]
        for chunk in range(max(TAIL_CHUNKS - block, 0), TAIL_CHUNKS + 1):
            row = (block + chunk - TAIL_CHUNKS) * QROWS
            there = slice(row, row + QROWS)
            mask = chunk_mask(bounds_ref[block, 0:1, :], bounds_ref[block, 1:2, :], chunk)
            for g in range(GROUP):
                scores = nt_dot(k_ref[there, :], q_ref[here, head_span(g)])
                weights = jnp.where(mask, jnp.exp2(scores * (score_scale * log2_e)), 0.0)
                sums[g] = sums[g] + jnp.sum(weights, axis=0, keepdims=True)
                outs[g] = outs[g] + tn_dot(v_ref[there, :], weights.astype(bf16))
        for g in range(GROUP):
            out_ref[head_span(g), here] = outs[g]
            total_ref[g : g + 1, here] = sums[g]


def chunk_pairs(chunks, kv_heads):
    return chunks * kv_heads * GROUP * QROWS * QROWS


def attend_own(queries, kv_own, bounds, after=()):
    rows = queries.shape[0]
    kv_heads = kv_own.shape[1] // (2 * HEAD_WIDTH)
    blocks = rows // QROWS
    wide = GROUP * HEAD_WIDTH
    pairs = chunk_pairs(sum(min(b, TAIL_CHUNKS) + 1 for b in range(blocks)), kv_heads)
    return call(
        attend_own_kernel,
        (queries, kv_own, kv_own, bounds,),
        grid=(kv_heads,),
        in_specs=[
            pl.BlockSpec((rows, wide), lambda j: (0, j)),
            pl.BlockSpec((rows, HEAD_WIDTH), lambda j: (0, j)),
            pl.BlockSpec((rows, HEAD_WIDTH), lambda j: (0, kv_heads + j)),
            pl.BlockSpec((blocks, 8, QROWS), lambda j: (0, 0, 0)),
        ],
        out_specs=[
            pl.BlockSpec((wide, rows), lambda j: (j, 0)),
            pl.BlockSpec((None, 8, rows), lambda j: (j, 0, 0)),
        ],
        out_shape=[shape_of((kv_heads * wide, rows), f32), shape_of((kv_heads, 8, rows), f32)],
        mib=32,
        estimate=cost(4 * pairs * HEAD_WIDTH, 4 << 20, pairs),
        name="attend_own",
        after=after,
    )


def attend_tail_kernel(
    shift, parts, part_ref, q_ref, k_ref, v_ref, bounds_ref, own_ref, own_total_ref, w_ref,
    attn_ref, total_ref, proj_ref, out_ref, acc_ref
):
    block = (part_ref[0] + shift) % parts
    out_ref[...] = own_ref[...]
    total_ref[...] = own_total_ref[...]
    for chunk in range(TAIL_CHUNKS):

        @pl.when(block + chunk < TAIL_CHUNKS)
        def add(chunk=chunk):
            there = pl.ds(pl.multiple_of((block + chunk) * QROWS, QROWS), QROWS)
            keys = k_ref[there, :]
            values = v_ref[there, :]
            mask = chunk_mask(bounds_ref[0:1, :], bounds_ref[1:2, :], chunk)
            for g in range(GROUP):
                scores = nt_dot(keys, q_ref[:, head_span(g)])
                weights = jnp.where(mask, jnp.exp2(scores * (score_scale * log2_e)), 0.0)
                total_ref[g : g + 1, :] += jnp.sum(weights, axis=0, keepdims=True)
                out_ref[head_span(g), :] += tn_dot(values, weights.astype(bf16))

    for g in range(GROUP):
        share = 1.0 / total_ref[g : g + 1, :]
        attn_ref[:, head_span(g)] = (out_ref[head_span(g), :] * share).T.astype(bf16)
    term = nt_dot(attn_ref[...], w_ref[...])
    last = pl.num_programs(0) - 1

    @pl.when(pl.program_id(0) == 0)
    def start():
        acc_ref[...] = term

    @pl.when(pl.program_id(0) > 0)
    def add_up():
        acc_ref[...] += term

    @pl.when(pl.program_id(0) == last)
    def finish():
        proj_ref[...] = acc_ref[...].astype(bf16)


def attend_tail(shift, part, parts, queries, kv_tail, bounds, outs, totals, attn_w, attn_cols, after=()):
    q_cols = queries.shape[1]
    width = attn_w.shape[0]
    kv_heads = kv_tail.shape[1] // (2 * HEAD_WIDTH)
    wide = GROUP * HEAD_WIDTH
    at = lambda p: (p[0] + shift) % parts
    pairs = chunk_pairs(TAIL_CHUNKS // 2, kv_heads)
    return call(
        functools.partial(attend_tail_kernel, shift, parts),
        (part, queries, kv_tail, kv_tail, bounds, outs, totals, attn_w,),
        prefetch=1,
        grid=(kv_heads,),
        in_specs=[
            pl.BlockSpec((QROWS, wide), lambda j, p: (at(p), j)),
            pl.BlockSpec((WINDOW_TOKENS, HEAD_WIDTH), lambda j, p: (0, j)),
            pl.BlockSpec((WINDOW_TOKENS, HEAD_WIDTH), lambda j, p: (0, kv_heads + j)),
            pl.BlockSpec((None, 8, QROWS), lambda j, p: (at(p), 0, 0)),
            pl.BlockSpec((wide, QROWS), lambda j, p: (j, at(p))),
            pl.BlockSpec((None, 8, QROWS), lambda j, p: (j, 0, at(p))),
            pl.BlockSpec((width, wide), lambda j, p: (0, attn_cols // wide + j)),
        ],
        out_specs=[
            pl.BlockSpec((QROWS, wide), lambda j, p: (0, j)),
            pl.BlockSpec((None, 8, QROWS), lambda j, p: (j, 0, 0)),
            pl.BlockSpec((QROWS, width), lambda j, p: (0, 0)),
        ],
        scratch=[pltpu.VMEM((wide, QROWS), f32), pltpu.VMEM((QROWS, width), f32)],
        out_shape=[
            shape_of((QROWS, q_cols), bf16),
            shape_of((kv_heads, 8, QROWS), f32),
            shape_of((QROWS, width), bf16),
        ],
        mib=32,
        estimate=cost(
            4 * pairs * HEAD_WIDTH + 2 * QROWS * width * q_cols, 4 << 20, pairs
        ),
        name="attend_tail",
        after=after,
    )


def chunk_backward(keys, values, queries, d_outs, mask, shares, deltas, turned):
    d_key = None
    d_value = None
    for g in range(GROUP):
        scores = nt_dot(keys, queries[g])
        probs = jnp.where(mask, jnp.exp2(scores * (score_scale * log2_e)) * shares[g], 0.0)
        d_probs = nt_dot(values, d_outs[g])
        d_scores = (probs * (d_probs - deltas[g]) * score_scale).astype(bf16)
        d_value_now = nn_dot(probs.astype(bf16), d_outs[g])
        d_key_now = nn_dot(d_scores, queries[g])
        d_value = d_value_now if g == 0 else d_value + d_value_now
        d_key = d_key_now if g == 0 else d_key + d_key_now
        turned[g] = turned[g] + tn_dot(keys, d_scores)
    return d_key, d_value


def attend_back_tail_kernel(
    q_ref, k_ref, v_ref, bounds_ref, total_ref, attn_ref, d_proj_ref, w_ref,
    d_out_ref, turned_ref, delta_ref, d_kv_ref, dk_ref, dv_ref
):
    d_out_ref[...] = nn_dot(d_proj_ref[...], w_ref[...]).astype(bf16)
    for block in range(q_ref.shape[0] // QROWS):
        here = slice(block * QROWS, (block + 1) * QROWS)
        shares = [1.0 / total_ref[g : g + 1, here] for g in range(GROUP)]
        queries = [q_ref[here, head_span(g)] for g in range(GROUP)]
        d_outs = [d_out_ref[here, head_span(g)] for g in range(GROUP)]
        deltas = []
        for g in range(GROUP):
            product = d_outs[g].astype(f32) * attn_ref[here, head_span(g)].astype(f32)
            deltas.append(jnp.sum(product.T, axis=0, keepdims=True))
            delta_ref[g : g + 1, here] = deltas[g]
        turned = [jnp.zeros((HEAD_WIDTH, QROWS), f32) for g in range(GROUP)]
        for chunk in range(0, max(TAIL_CHUNKS - block, 0)):
            there = slice((block + chunk) * QROWS, (block + chunk + 1) * QROWS)
            mask = chunk_mask(bounds_ref[block, 0:1, :], bounds_ref[block, 1:2, :], chunk)
            d_key, d_value = chunk_backward(
                k_ref[there, :], v_ref[there, :], queries, d_outs, mask, shares, deltas, turned
            )
            if block == 0:
                dk_ref[there, :] = d_key
                dv_ref[there, :] = d_value
            else:
                dk_ref[there, :] += d_key
                dv_ref[there, :] += d_value
        for g in range(GROUP):
            turned_ref[head_span(g), here] = turned[g]
    d_kv_ref[0] = dk_ref[...].astype(bf16)
    d_kv_ref[1] = dv_ref[...].astype(bf16)


def attend_back_own_kernel(
    q_ref, k_ref, v_ref, bounds_ref, total_ref, d_out_ref, turned_ref, delta_ref, dq_ref, d_kv_ref
):
    for block in range(q_ref.shape[0] // QROWS):
        here = slice(block * QROWS, (block + 1) * QROWS)
        shares = [1.0 / total_ref[g : g + 1, here] for g in range(GROUP)]
        queries = [q_ref[here, head_span(g)] for g in range(GROUP)]
        d_outs = [d_out_ref[here, head_span(g)] for g in range(GROUP)]
        deltas = [delta_ref[g : g + 1, here] for g in range(GROUP)]
        turned = [turned_ref[head_span(g), here] for g in range(GROUP)]
        for chunk in range(max(TAIL_CHUNKS - block, 0), TAIL_CHUNKS + 1):
            row = (block + chunk - TAIL_CHUNKS) * QROWS
            there = slice(row, row + QROWS)
            mask = chunk_mask(bounds_ref[block, 0:1, :], bounds_ref[block, 1:2, :], chunk)
            d_key, d_value = chunk_backward(
                k_ref[there, :], v_ref[there, :], queries, d_outs, mask, shares, deltas, turned
            )
            if chunk == TAIL_CHUNKS:
                d_kv_ref[0, there, :] = d_key
                d_kv_ref[1, there, :] = d_value
            else:
                d_kv_ref[0, there, :] += d_key
                d_kv_ref[1, there, :] += d_value
        for g in range(GROUP):
            dq_ref[here, head_span(g)] = turned[g].T.astype(bf16)


def attend_back_tail(
    queries, kv_tail, bounds, totals, attn, d_proj, attn_w, attn_cols, after=()
):
    rows, q_cols = queries.shape
    width = attn_w.shape[0]
    kv_heads = kv_tail.shape[1] // (2 * HEAD_WIDTH)
    blocks = rows // QROWS
    wide = GROUP * HEAD_WIDTH
    pairs = chunk_pairs(sum(max(TAIL_CHUNKS - b, 0) for b in range(blocks)), kv_heads)
    head_spec = pl.BlockSpec((rows, wide), lambda j: (0, j))
    row_spec = pl.BlockSpec((None, 8, rows), lambda j: (j, 0, 0))
    return call(
        attend_back_tail_kernel,
        (queries, kv_tail, kv_tail, bounds, totals, attn, d_proj, attn_w),
        grid=(kv_heads,),
        in_specs=[
            head_spec,
            pl.BlockSpec((WINDOW_TOKENS, HEAD_WIDTH), lambda j: (0, j)),
            pl.BlockSpec((WINDOW_TOKENS, HEAD_WIDTH), lambda j: (0, kv_heads + j)),
            pl.BlockSpec((blocks, 8, QROWS), lambda j: (0, 0, 0)),
            row_spec,
            head_spec,
            pl.BlockSpec((rows, width), lambda j: (0, 0)),
            pl.BlockSpec((width, wide), lambda j: (0, attn_cols // wide + j)),
        ],
        out_specs=[
            head_spec,
            pl.BlockSpec((wide, rows), lambda j: (j, 0)),
            row_spec,
            pl.BlockSpec((2, WINDOW_TOKENS, HEAD_WIDTH), lambda j: (0, 0, j)),
        ],
        scratch=[pltpu.VMEM((WINDOW_TOKENS, HEAD_WIDTH), f32)] * 2,
        out_shape=[
            shape_of((rows, q_cols), bf16),
            shape_of((kv_heads * wide, rows), f32),
            shape_of((kv_heads, 8, rows), f32),
            shape_of((2, WINDOW_TOKENS, kv_heads * HEAD_WIDTH), bf16),
        ],
        mib=40,
        estimate=cost(10 * pairs * HEAD_WIDTH + 2 * rows * width * q_cols, 8 << 20, pairs),
        name="attend_back_tail",
        after=after,
    )


def attend_back_own(queries, kv_own, bounds, totals, d_outs, turned, deltas, after=()):
    rows, q_cols = queries.shape
    kv_heads = kv_own.shape[1] // (2 * HEAD_WIDTH)
    blocks = rows // QROWS
    wide = GROUP * HEAD_WIDTH
    pairs = chunk_pairs(sum(min(b, TAIL_CHUNKS) + 1 for b in range(blocks)), kv_heads)
    head_spec = pl.BlockSpec((rows, wide), lambda j: (0, j))
    row_spec = pl.BlockSpec((None, 8, rows), lambda j: (j, 0, 0))
    return call(
        attend_back_own_kernel,
        (queries, kv_own, kv_own, bounds, totals, d_outs, turned, deltas),
        grid=(kv_heads,),
        in_specs=[
            head_spec,
            pl.BlockSpec((rows, HEAD_WIDTH), lambda j: (0, j)),
            pl.BlockSpec((rows, HEAD_WIDTH), lambda j: (0, kv_heads + j)),
            pl.BlockSpec((blocks, 8, QROWS), lambda j: (0, 0, 0)),
            row_spec,
            head_spec,
            pl.BlockSpec((wide, rows), lambda j: (j, 0)),
            row_spec,
        ],
        out_specs=[
            head_spec,
            pl.BlockSpec((2, rows, HEAD_WIDTH), lambda j: (0, 0, j)),
        ],
        out_shape=[
            shape_of((rows, q_cols), bf16),
            shape_of((2, rows, kv_heads * HEAD_WIDTH), f32),
        ],
        mib=40,
        estimate=cost(10 * pairs * HEAD_WIDTH, 8 << 20, pairs, scale=1),
        name="attend_back_own",
        after=after,
    )


def mid_norm_kernel(x_ref, gain_ref, *refs):
    middle = x_ref[...].astype(f32)
    for ref in refs[:-2]:
        middle = middle + ref[...].astype(f32)
    refs[-2][...] = middle
    refs[-1][...] = (middle * norm_stats(middle) * gain_ref[...]).astype(bf16)


def mid_norm(hidden, gain, terms, after=()):
    rows, cols = hidden.shape
    spec = pl.BlockSpec((rows // 4, cols), lambda i: (i, 0))
    return call(
        mid_norm_kernel,
        (hidden, gain, *terms),
        grid=(4,),
        in_specs=[spec, pl.BlockSpec((1, cols), lambda i: (0, 0))] + [spec] * len(terms),
        out_specs=[spec, spec],
        out_shape=[shape_of((rows, cols), f32), shape_of((rows, cols), bf16)],
        estimate=cost(20 * rows * cols, 20 * rows * cols),
        name="mid_norm",
        after=after,
    )


def mid_back_kernel(own_ref, got_ref, middle_ref, grad_ref, gain_ref, out_ref, low_ref, sum_ref):
    @pl.when(pl.program_id(0) == 0)
    def clear():
        sum_ref[...] = jnp.zeros_like(sum_ref)

    d_normed = own_ref[...] + got_ref[...].astype(f32)
    middle = middle_ref[...]
    stats = norm_stats(middle)
    sum_ref[0:1, :] += jnp.sum(d_normed * (middle * stats), axis=0, keepdims=True)
    d_middle = grad_ref[...].astype(f32) + norm_back(d_normed, middle, stats, gain_ref[...])
    out_ref[...] = d_middle
    low_ref[...] = d_middle.astype(bf16)


def mid_back(own, got, middle, out_grad, gain, after=()):
    rows, cols = own.shape
    spec = pl.BlockSpec((rows // 4, cols), lambda i: (i, 0))
    return call(
        mid_back_kernel,
        (own, got, middle, out_grad, gain),
        grid=(4,),
        in_specs=[spec] * 4 + [pl.BlockSpec((1, cols), lambda i: (0, 0))],
        out_specs=[spec, spec, pl.BlockSpec((8, cols), lambda i: (0, 0))],
        out_shape=[
            shape_of((rows, cols), f32),
            shape_of((rows, cols), bf16),
            shape_of((8, cols), f32),
        ],
        estimate=cost(30 * rows * cols, 20 * rows * cols),
        name="mid_back",
        after=after,
    )


def mlp_kernel(
    x_own_ref, x_got_ref, g_own_ref, g_got_ref, wg_ref, wu_ref, wd_ref,
    mixed_ref, d_gate_ref, d_up_ref, d_mid_ref, d_mid_give_ref, out_ref, out_give_ref,
    x_ref, g_ref, d_mid_acc, out_acc
):
    step = pl.program_id(0)
    tokens = x_own_ref.shape[0]

    @pl.when(step == 0)
    def start():
        x_ref[:tokens, :] = x_own_ref[...]
        x_ref[tokens:, :] = x_got_ref[...]
        g_ref[:tokens, :] = g_own_ref[...]
        g_ref[tokens:, :] = g_got_ref[...]
        d_mid_acc[...] = jnp.zeros_like(d_mid_acc)
        out_acc[...] = jnp.zeros_like(out_acc)

    gate = nn_dot(x_ref[...], wg_ref[...])
    up = nn_dot(x_ref[...], wu_ref[...])
    d_mixed = nn_dot(g_ref[...], wd_ref[...])
    sig = 1.0 / (1.0 + jnp.exp(-gate))
    gated = gate * sig
    mixed = (gated * up).astype(bf16)
    d_gate = (d_mixed * up * sig * (1.0 + gate * (1.0 - sig))).astype(bf16)
    d_up = (d_mixed * gated).astype(bf16)
    mixed_ref[...] = mixed
    d_gate_ref[...] = d_gate
    d_up_ref[...] = d_up
    d_mid_acc[...] += nt_dot(d_gate, wg_ref[...]) + nt_dot(d_up, wu_ref[...])
    out_acc[...] += nt_dot(mixed, wd_ref[...])

    @pl.when(step == pl.num_programs(0) - 1)
    def finish():
        d_mid_ref[...] = d_mid_acc[:tokens, :]
        d_mid_give_ref[...] = d_mid_acc[tokens:, :].astype(bf16)
        out_ref[...] = out_acc[:tokens, :]
        out_give_ref[...] = out_acc[tokens:, :].astype(bf16)


def mlp(x_own, x_got, g_own, g_got, mlp_w, after=()):
    tokens, width = x_own.shape
    units = mlp_w.shape[1] // 3
    tile = 512
    steps = units // tile
    fixed = lambda j: (0, 0)
    rows_spec = pl.BlockSpec((tokens, width), fixed)
    tile_spec = pl.BlockSpec((2 * tokens, tile), lambda j: (0, j))
    tile_shape = shape_of((2 * tokens, units), bf16)
    return call(
        mlp_kernel,
        (x_own, x_got, g_own, g_got, mlp_w, mlp_w, mlp_w,),
        grid=(steps,),
        in_specs=[rows_spec] * 4
        + [
            pl.BlockSpec((width, tile), lambda j: (0, j)),
            pl.BlockSpec((width, tile), lambda j: (0, steps + j)),
            pl.BlockSpec((width, tile), lambda j: (0, 2 * steps + j)),
        ],
        out_specs=[tile_spec] * 3 + [rows_spec] * 4,
        out_shape=[tile_shape] * 3
        + [
            shape_of((tokens, width), f32),
            shape_of((tokens, width), bf16),
            shape_of((tokens, width), f32),
            shape_of((tokens, width), bf16),
        ],
        scratch=[
            pltpu.VMEM((2 * tokens, width), bf16),
            pltpu.VMEM((2 * tokens, width), bf16),
            pltpu.VMEM((2 * tokens, width), f32),
            pltpu.VMEM((2 * tokens, width), f32),
        ],
        mib=48,
        estimate=cost(12 * 2 * tokens * width * units, 16 << 20),
        name="mlp",
        after=after,
    )


def mlp_grad_kernel(own_ref, got_ref, d_ref, out_ref, turned_ref):
    tokens = own_ref.shape[0]

    @pl.when(pl.program_id(0) == 0)
    def start():
        turned_ref[:, :tokens] = own_ref[...].T
        turned_ref[:, tokens:] = got_ref[...].T

    out_ref[...] = nn_dot(turned_ref[...], d_ref[...]).astype(bf16)


def mlp_grad(own, got, d_units, after=()):
    tokens, width = own.shape
    units = d_units.shape[1]
    tile = 512
    fixed = lambda j: (0, 0)
    return call(
        mlp_grad_kernel,
        (own, got, d_units,),
        grid=(units // tile,),
        in_specs=[
            pl.BlockSpec((tokens, width), fixed),
            pl.BlockSpec((tokens, width), fixed),
            pl.BlockSpec((2 * tokens, tile), lambda j: (0, j)),
        ],
        out_specs=pl.BlockSpec((width, tile), lambda j: (0, j)),
        out_shape=shape_of((width, units), bf16),
        scratch=[pltpu.VMEM((width, 2 * tokens), bf16)],
        mib=32,
        estimate=cost(4 * tokens * width * units, 8 << 20),
        name="mlp_grad",
        after=after,
    )


def mlp_grad_pair_kernel(
    steps, own_a_ref, got_a_ref, d_a_ref, own_b_ref, got_b_ref, d_b_ref, out_ref, turned_ref
):
    step = pl.program_id(0)
    tokens = own_a_ref.shape[0]

    @pl.when(step == 0)
    def first():
        turned_ref[:, :tokens] = own_a_ref[...].T
        turned_ref[:, tokens:] = got_a_ref[...].T

    @pl.when(step == steps)
    def second():
        turned_ref[:, :tokens] = own_b_ref[...].T
        turned_ref[:, tokens:] = got_b_ref[...].T

    @pl.when(step < steps)
    def left():
        out_ref[...] = nn_dot(turned_ref[...], d_a_ref[...]).astype(bf16)

    @pl.when(step >= steps)
    def right():
        out_ref[...] = nn_dot(turned_ref[...], d_b_ref[...]).astype(bf16)


def mlp_grad_pair(own_a, got_a, d_a, own_b, got_b, d_b, after=()):
    tokens, width = own_a.shape
    units = d_a.shape[1]
    tile = 512
    steps = units // tile
    rows = pl.BlockSpec((tokens, width), lambda j: (0, 0))
    return call(
        functools.partial(mlp_grad_pair_kernel, steps),
        (own_a, got_a, d_a, own_b, got_b, d_b),
        grid=(2 * steps,),
        in_specs=[
            rows,
            rows,
            pl.BlockSpec((2 * tokens, tile), lambda j: (0, jnp.minimum(j, steps - 1))),
            rows,
            rows,
            pl.BlockSpec((2 * tokens, tile), lambda j: (0, jnp.maximum(j - steps, 0))),
        ],
        out_specs=pl.BlockSpec((width, tile), lambda j: (0, j)),
        scratch=[pltpu.VMEM((width, 2 * tokens), bf16)],
        out_shape=shape_of((width, 2 * units), bf16),
        mib=48,
        estimate=cost(8 * tokens * width * units, 16 << 20),
        name="mlp_grad_pair",
        after=after,
    )


def body(
    hidden_in,
    doc_lengths,
    pad_lengths,
    w_query,
    key_matrix,
    value_matrix,
    w_output,
    w_gate,
    w_up,
    w_down,
    attn_gain,
    mlp_gain,
    query_gain,
    key_gain,
    out_grad,
):
    core = lax.axis_index("c")
    chip = lax.axis_index("q")
    chips = lax.axis_size("q")
    group = chip * 2 + core
    part = lax.axis_index("seq")
    groups = chips * 2
    parts = lax.axis_size("seq")
    tokens, width = hidden_in.shape
    group_rows = tokens * parts
    slice_rows = width // groups
    units = FEEDFWD_UNITS // 2
    q_cols = QUERY_HEADS * HEAD_WIDTH // parts
    kv_cols = KEY_VALUE_HEADS * HEAD_WIDTH // parts
    attn_cols = q_cols + 2 * kv_cols
    pack_cols = attn_cols + q_cols
    core_at = core.astype(jnp.int32).reshape(1)
    part_at = part.astype(jnp.int32).reshape(1)

    def swapped(value):
        return lax.ppermute(value, "c", core_swap)

    def sent(value, shift):
        return lax.ppermute(value, "seq", [(i, (i + shift) % parts) for i in range(parts)])

    def from_all(value):
        return [value] + [sent(value, shift) for shift in range(1, parts)]

    hidden_blocks = from_all(hidden_in)

    packed = pack_attn(
        part_at, parts, w_query, key_matrix, value_matrix, w_output,
        (attn_gain, mlp_gain, query_gain, key_gain),
    )
    attn_w = lax.all_gather(packed, dp_axes, axis=0, tiled=True)

    mlp_pack, mlp_give = pack_mlp(core_at, w_gate, w_up, w_down, after=(packed,))
    mlp_pack = lax.dynamic_update_slice_in_dim(
        mlp_pack, swapped(mlp_give), (1 - core) * slice_rows, 0
    )
    mlp_w = lax.all_gather(mlp_pack, "q", axis=0, tiled=True)
    grad_spread = jnp.where(
        (jnp.arange(2) == core)[:, None, None], jnp.zeros((), bf16), out_grad[None]
    )
    grad_got = lax.psum_scatter(grad_spread, "c", scatter_dimension=0, tiled=True)
    grad_got = grad_got.reshape(tokens, width)

    gains = read_gains(attn_w, pack_cols)
    head_piece = query_gain.shape[0]
    ga = gains[0:1]
    gm = gains[1:2]
    gqk = gains[2:4].reshape(2, groups, slice_rows)[:, :, :head_piece].reshape(2, HEAD_WIDTH)

    doc_ends = jnp.cumsum(doc_lengths)
    doc_starts = doc_ends - doc_lengths
    pad_starts = doc_ends - pad_lengths
    first = group * group_rows
    token = first + jnp.arange(group_rows, dtype=jnp.int32)
    inside = (token[:, None] >= doc_starts[None, :]) & (token[:, None] < doc_ends[None, :])
    start = jnp.sum(jnp.where(inside, doc_starts[None, :], 0), axis=1)
    pad_start = jnp.sum(jnp.where(inside, pad_starts[None, :], 0), axis=1)
    inv_freq = rope_base ** (-jnp.arange(HEAD_WIDTH // 2, dtype=f32) * 2.0 / HEAD_WIDTH)
    angles = (token - start).astype(f32)[:, None] * inv_freq[None, :]
    cosine = jnp.cos(angles)
    sine = jnp.sin(angles)
    cosine = jnp.concatenate([cosine, cosine], axis=1)
    sine = jnp.concatenate([-sine, sine], axis=1)
    offset = (token // QROWS) * QROWS - WINDOW_TOKENS
    low = jnp.maximum(start, token - (WINDOW_TOKENS - 1)) - offset
    high = jnp.minimum(token, pad_start - 1) - offset
    bounds = jnp.pad(
        jnp.stack([low.reshape(parts, QROWS), high.reshape(parts, QROWS)], axis=1),
        ((0, 0), (0, 6), (0, 0)),
    )

    normed_all, queries, kv_own, qk_proj = project(
        part_at, hidden_blocks, attn_w, ga, gqk, cosine, sine, q_cols, kv_cols
    )
    kv_tail = lax.ppermute(
        kv_own[group_rows - WINDOW_TOKENS :], dp_axes, [(i, i + 1) for i in range(groups - 1)]
    )
    own_outs, own_totals = attend_own(queries, kv_own, bounds)
    terms = []
    attn = [None] * parts
    totals = [None] * parts
    order = [shift for shift in range(1, parts)] + [0]
    for shift in order:
        attn[shift], totals[shift], term = attend_tail(
            shift, part_at, parts, queries, kv_tail, bounds, own_outs, own_totals, attn_w, attn_cols
        )
        terms.append(sent(term, shift) if shift else term)
    attn_all = jnp.zeros((group_rows, q_cols), bf16)
    totals_all = jnp.zeros((kv_cols // HEAD_WIDTH, 8, group_rows), f32)
    for shift in range(parts):
        row = (part + shift) % parts * tokens
        attn_all = lax.dynamic_update_slice_in_dim(attn_all, attn[shift], row, 0)
        totals_all = lax.dynamic_update_slice_in_dim(totals_all, totals[shift], row, 2)
    middle, normed_mid = mid_norm(hidden_in, gm, terms)

    mid_got = swapped(normed_mid)
    mixed, d_gate, d_up, d_mid, d_mid_give, out_part, out_give = mlp(
        normed_mid, mid_got, out_grad, grad_got, mlp_w
    )
    d_middle, d_proj, mlp_gain_rows = mid_back(
        d_mid, swapped(d_mid_give), middle, out_grad, gm
    )
    term_pair = mlp_grad_pair(
        out_grad, grad_got, mixed, normed_mid, mid_got, d_gate, after=(d_proj,)
    )
    d_proj_all = lax.all_gather(d_proj, "seq", axis=0, tiled=True)
    output_act = (middle + out_part + swapped(out_give).astype(f32)).astype(bf16)

    def chip_sums(grad):
        return lax.psum_scatter(grad, "q", scatter_dimension=0, tiled=True)

    own_pair = chip_sums(term_pair)
    term_up = mlp_grad(normed_mid, mid_got, d_up, after=(d_proj,))
    own_up = chip_sums(term_up)
    line = list(range(parts))

    def unpacked(sums, column, turned, after=()):
        give = lax.dynamic_slice(
            sums, ((1 - core) * slice_rows, column * units), (slice_rows, units)
        )
        return unpack_half(core_at, sums, swapped(give), column, turned, after=after)

    d_attn, turned, deltas, d_tail = attend_back_tail(
        queries, kv_tail, bounds, totals_all, attn_all, d_proj_all, attn_w, attn_cols,
        after=(term_up,),
    )
    d_tail = lax.ppermute(d_tail, dp_axes, [(i + 1, i) for i in range(groups - 1)])
    d_queries, d_kv = attend_back_own(
        queries, kv_own, bounds, totals_all, d_attn, turned, deltas
    )
    sum_pair = lax.psum(own_pair, "seq")
    w_out_grad = out_grad_sums([d_proj_all], [attn_all], after=(d_queries,))
    d_in, attn_term = project_back(
        part_at, groups, [hidden_blocks[(parts - k) % parts] for k in range(parts)],
        d_queries, d_kv, d_tail, qk_proj, attn_w, gqk, cosine, sine, normed_all, w_out_grad,
        mlp_gain_rows,
    )
    d_in = lax.psum_scatter(d_in, "seq", scatter_dimension=0, tiled=True)

    attn_grad = lax.psum_scatter(attn_term, dp_axes, scatter_dimension=0, tiled=True)
    give = lax.dynamic_slice_in_dim(own_up, (1 - core) * slice_rows, slice_rows, 0)
    own_up = join_halves(core_at, own_up, swapped(give), after=(sum_pair,))
    sum_up = lax.psum(own_up, "seq", axis_index_groups=[line[::-1]])
    grad_down = unpacked(sum_pair, 0, True)
    grad_gate = unpacked(sum_pair, 1, False, after=(grad_down,))
    attn_grad = touch(attn_grad, after=(grad_gate, sum_up))
    attn_grads = lax.all_gather(attn_grad, "seq", axis=0)
    in_grad = finish_in(d_in, d_middle, hidden_in, ga)
    grad_up = widened(sum_up, after=(in_grad,))
    gain_sums = jnp.sum(attn_grads[:, :, pack_cols : pack_cols + 4].astype(f32), axis=0)
    grad_query, grad_key, grad_value, grad_output = unpack_attn(
        attn_grads, q_cols, kv_cols, after=(grad_up,)
    )
    return (
        output_act,
        in_grad,
        grad_query,
        grad_key,
        grad_value,
        grad_output,
        grad_gate,
        grad_up,
        grad_down,
        gain_sums[:, 0],
        gain_sums[:, 1],
        gain_sums[:head_piece, 2],
        gain_sums[:head_piece, 3],
    )


def solution(mesh):
    groups, parts = mesh.devices.shape
    mesh = Mesh(mesh.devices.reshape(groups // 2, 2, parts), ("q", "c", "seq"))
    tokens = P(("q", "c", "seq"), None)
    rows = P(dp_axes, None)
    cols = P(None, dp_axes)
    flat = P(dp_axes)
    in_specs = (
        tokens, P(), P(), rows, rows, rows, cols, rows, rows, cols, flat, flat, flat, flat, tokens,
    )
    out_specs = (
        tokens, tokens, rows, rows, rows, cols, rows, rows, cols, flat, flat, flat, flat,
    )
    return jax.shard_map(body, mesh=mesh, in_specs=in_specs, out_specs=out_specs, check_vma=False)
```
